32 devices in a mesh: dp: 8 (over z, y), mp: 4 (over x, core).
Axes of the slice: x: 2, y: 2, z: 4, core: 2. Of those that a mesh axis runs over, the one named last changes fastest.
Arguments:
- tokens: bfloat16 [16384, 1024], P(('dp', 'mp')), may hold values from -6 to 6
- cotangent: bfloat16 [16384, 1024], P(('dp', 'mp')), may hold values from -6 to 6
- item_lengths: int32 [40], P('dp'), may hold values from 0 to 1024, as said below
- gsd_ratio: float32 [40], P('dp'), may hold values from 0.25 to 1
- ln1_gain: bfloat16 [1024], replicated, may hold values from 0.5 to 1.5
- ln1_bias: bfloat16 [1024], replicated, may hold values from -1.1953125 to 1.1953125
- w_qkv: bfloat16 [3, 1024, 1024], P(None, 'mp'), may hold values from -0.1875 to 0.1875
- qv_bias: float32 [2, 1024], P(None, 'mp'), may hold values from -3 to 3
- w_out: bfloat16 [1024, 1024], P('mp'), may hold values from -1.5 to 1.5
- out_bias: float32 [1024], replicated, may hold values from -1.2 to 1.2
- ln2_gain: float32 [1024], replicated, may hold values from 0.5 to 1.5
- ln2_bias: float32 [1024], replicated, may hold values from -1.2 to 1.2
- w_up: bfloat16 [1024, 4096], P(None, 'mp'), may hold values from -0.1875 to 0.1875
- up_bias: float32 [4096], P('mp'), may hold values from -1.8 to 1.8
- w_down: bfloat16 [4096, 1024], P('mp'), may hold values from -0.09375 to 0.09375
- down_bias: float32 [1024], replicated, may hold values from -1.2 to 1.2
Outputs:
- output: bfloat16 [16384, 1024], P(('dp', 'mp'))
- input_grad: float32 [16384, 1024], P(('dp', 'mp'))
- grad_ln1_gain: float32 [1024], replicated
- grad_ln1_bias: float32 [1024], replicated
- grad_qkv: float32 [3, 1024, 1024], P(None, 'mp')
- grad_qv_bias: float32 [2, 1024], P(None, 'mp')
- grad_out_weight: float32 [1024, 1024], P('mp')
- grad_out_bias: float32 [1024], replicated
- grad_ln2_gain: float32 [1024], replicated
- grad_ln2_bias: float32 [1024], replicated
- grad_up: float32 [1024, 4096], P(None, 'mp')
- grad_up_bias: float32 [4096], P('mp')
- grad_down: float32 [4096, 1024], P('mp')
- grad_down_bias: float32 [1024], replicated
- stats: float32 [3], replicated
The draws below stay inside these ranges and needn't reach their ends.
Inputs may be any that keep to these rules, and one draw needn't show every extreme that they name: `item_lengths`: in each block of 5 entries the first is a scene of 512 to 1024 patches, exactly 1024 in some block of every draw; the others are chips of 64 to 256 patches, nonzero ones first, then zeros; the items of a block fit in its 2048 rows and the rows after them are padding.
All inputs are finite; a program needn't handle non-finite values.
Results may differ from the reference program's by a relative error of at most 0.02.
Values may be sent and summed in bfloat16 or wider, within the bound.
No kernel may reach another device: no remote copies, remote signals or barrier semaphores. Data moves between devices by JAX's collectives and lax.ppermute only.
A program may use at most 192 MiB of HBM per device.

```python
import math
import jax
import jax.numpy as jnp
from jax import lax

D = 1024
HEADS = 16
HD = 64
FF = 4096
TOK_DEV = 2048
ITEMS_DEV = 5
TOKENS = 16384
N_DP = 8


def draw_item_lengths(key, part):
    key = jax.random.fold_in(key, 11)
    key_scene, key_widest, key_chips, key_count = jax.random.split(key, 4)
    blocks = TOKENS // TOK_DEV
    half_rows = TOK_DEV // 2
    scenes = jax.random.randint(key_scene, (blocks,), TOK_DEV // 4, half_rows + 1)
    widest = jax.random.randint(key_widest, (), 0, blocks)
    scenes = jnp.where(jnp.arange(blocks) == widest, half_rows, scenes)
    chips = jax.random.randint(key_chips, (blocks, ITEMS_DEV - 1), TOK_DEV // 32, TOK_DEV // 8 + 1)
    chip_count = jax.random.randint(key_count, (blocks, 1), 0, ITEMS_DEV)
    chips = jnp.where(jnp.arange(ITEMS_DEV - 1)[None, :] < chip_count, chips, 0)
    return jnp.concatenate([scenes[:, None], chips], axis=1).reshape(-1).astype(jnp.int32)


def steps_of(rng, dims, cuts, low, top_value):
    level, own = 1.0, jax.random.fold_in(rng, 6)
    for dim, blocks in cuts:
        draws = jnp.exp(jax.random.uniform(jax.random.fold_in(own, dim), (blocks,), jnp.float32, low / len(cuts), top_value / len(cuts)))
        level = level * jnp.repeat(draws, dims[dim] // blocks).reshape([-1 if axis == dim else 1 for axis in range(len(dims))])
    return level


def bell_draw(own_key, dims, width, most, cuts=(), kind=jnp.bfloat16):
    level = steps_of(own_key, dims, cuts, -0.22, 0.18) if cuts else 1.0
    array = jax.random.normal(own_key, dims, jnp.float32) * width * level
    return jnp.minimum(jnp.maximum(array, -most), most).astype(kind)


def setup_inputs(seed: int = 0) -> dict:
    seeds = jax.random.split(jax.random.key(seed), 17)
    tokens = bell_draw(seeds[0], (TOKENS, D), 1.0, 6.0, ((0, 32),))
    cotangent = bell_draw(seeds[1], (TOKENS, D), 1.0, 6.0, ((0, 32),))
    item_lengths = draw_item_lengths(jax.random.fold_in(seeds[16], 71), 0)
    gsd_ratio = jnp.clip(jnp.exp(math.log(1.0) - 1.3862944 * jax.random.uniform(seeds[3], (TOKENS // TOK_DEV * ITEMS_DEV,), jnp.float32) ** steps_of(seeds[3], (TOKENS // TOK_DEV * ITEMS_DEV,), ((0, 8),), -0.2, 0.2)), 0.25, 1.0)
    ln1_gain = jnp.clip(1.0 + 0.1 * jax.random.normal(seeds[4], (D,), jnp.float32), 0.5, 1.5).astype(jnp.bfloat16)
    ln1_bias = bell_draw(seeds[5], (D,), 0.2, 1.1953125)
    w_qkv = bell_draw(seeds[6], (3, D, D), D ** -0.5, 0.1875, ((1, 4),))
    qv_bias = bell_draw(seeds[7], (2, D), 0.5, 3.0, ((1, 4),), jnp.float32)
    w_out = bell_draw(seeds[8], (D, D), (HD // 4) ** -0.5, 1.5, ((0, 4),))
    out_bias = bell_draw(seeds[9], (D,), 0.2, 1.2, (), jnp.float32)
    ln2_gain = jnp.clip(1.0 + 0.1 * jax.random.normal(seeds[10], (D,), jnp.float32), 0.5, 1.5)
    ln2_bias = bell_draw(seeds[11], (D,), 0.2, 1.2, (), jnp.float32)
    w_up = bell_draw(seeds[12], (D, FF), D ** -0.5, 0.1875, ((1, 4),))
    up_bias = bell_draw(seeds[13], (FF,), 0.3, 1.8, ((0, 4),), jnp.float32)
    w_down = bell_draw(seeds[14], (FF, D), FF ** -0.5, 0.09375, ((0, 4),))
    down_bias = bell_draw(seeds[15], (D,), 0.2, 1.2, (), jnp.float32)
    return {"tokens": tokens, "cotangent": cotangent, "item_lengths": item_lengths, "gsd_ratio": gsd_ratio, "ln1_gain": ln1_gain, "ln1_bias": ln1_bias, "w_qkv": w_qkv, "qv_bias": qv_bias, "w_out": w_out, "out_bias": out_bias, "ln2_gain": ln2_gain, "ln2_bias": ln2_bias, "w_up": w_up, "up_bias": up_bias, "w_down": w_down, "down_bias": down_bias}


EPS = 1e-06
MASKED = -1e+30

@jax.custom_vjp
def low(v):
    return lax.optimization_barrier(v.astype(jnp.bfloat16)).astype(jnp.float32)

@jax.custom_vjp
def low_back(v):
    return v

def low_keep(v):
    return (low(v), None)

def low_pass(kept, grad):
    return (grad,)

def back_keep(v):
    return (v, None)

def back_low(kept, grad):
    return (low(grad),)
low.defvjp(low_keep, low_pass)
low_back.defvjp(back_keep, back_low)

def layout(lengths, row_count):
    item_count = lengths.shape[0]
    item_ends = jnp.cumsum(lengths).astype(jnp.int32)
    item_starts = (item_ends - lengths).astype(jnp.int32)
    places = jnp.arange(row_count, dtype=jnp.int32)
    segment = lax.optimization_barrier(jnp.sum((places[:, None] >= item_ends[None, :]).astype(jnp.int32), axis=1)).astype(jnp.int32)
    picked = segment[:, None] == jnp.arange(item_count, dtype=jnp.int32)[None, :]
    offset = lax.optimization_barrier(jnp.sum(jnp.where(picked, item_starts[None, :], 0), axis=1)).astype(jnp.int32)
    position = jnp.where(segment < item_count, places - offset, 0).astype(jnp.int32)
    return (segment, position, picked)

def encoding(position, row_ratio, columns, full_width):
    half_width = full_width // 2
    freq_index = jnp.where(columns < half_width, columns, columns - half_width).astype(jnp.float32)
    frequency = jnp.exp(freq_index * (-math.log(10000.0) / half_width))
    angles = (position.astype(jnp.float32) * row_ratio)[:, None] * frequency[None, :]
    return jnp.where((columns < half_width)[None, :], jnp.sin(angles), jnp.cos(angles))

def product(left, right):
    return jnp.dot(left, right, precision=lax.Precision.HIGHEST)

def layer_norm(stream, gain, shift):
    row_mean = lax.optimization_barrier(jnp.mean(stream, axis=-1, keepdims=True))
    centred = stream - row_mean
    variance = lax.optimization_barrier(jnp.mean(centred * centred, axis=-1, keepdims=True))
    return centred * lax.rsqrt(variance + EPS) * gain + shift

def head_attention(query_head, key_head, value_head, seg_part):
    scores = low_back(product(query_head, key_head.T) * HD ** (-0.5))
    scores = jnp.where(seg_part[:, None] == seg_part[None, :], scores, MASKED)
    probs = jax.nn.softmax(scores, axis=-1)
    return product(low(probs), value_head)

def attention(query, key_all, value_all, segment):
    shape_four = (N_DP, TOK_DEV, HEADS, HD)

    def device_part(inputs):
        query_part, key_part, value_part, seg_part = inputs

        def head_part(head_inputs):
            return head_attention(head_inputs[0], head_inputs[1], head_inputs[2], seg_part)
        stacked = (jnp.moveaxis(query_part, 1, 0), jnp.moveaxis(key_part, 1, 0), jnp.moveaxis(value_part, 1, 0))
        result = lax.map(jax.checkpoint(head_part), stacked)
        return jnp.moveaxis(result, 0, 1).reshape(TOK_DEV, HEADS * HD)
    result = lax.map(jax.checkpoint(device_part), (query.reshape(shape_four), key_all.reshape(shape_four), value_all.reshape(shape_four), segment))
    return result.reshape(TOKENS, D)

def reference(tokens, cotangent, item_lengths, gsd_ratio, ln1_gain, ln1_bias, w_qkv, qv_bias, w_out, out_bias, ln2_gain, ln2_bias, w_up, up_bias, w_down, down_bias):
    lengths = item_lengths.reshape(N_DP, ITEMS_DEV)
    segment, position, picked = jax.vmap(lambda entry: layout(entry, TOK_DEV))(lengths)
    ratios = gsd_ratio.reshape(N_DP, 1, ITEMS_DEV)
    row_ratio = lax.optimization_barrier(jnp.sum(jnp.where(picked, ratios, 0.0), axis=2)).reshape(TOKENS)
    valid_rows = (segment < ITEMS_DEV).astype(jnp.float32).reshape(TOKENS, 1)
    encoded = encoding(position.reshape(TOKENS), row_ratio, jnp.arange(D, dtype=jnp.int32), D)

    def forward(stream_in, gain1, shift1, qkv_weight, qv_shift, out_weight, out_shift, gain2, shift2, up_weight, up_shift, down_weight, down_shift):
        stream0 = stream_in + encoded
        normed1 = low(layer_norm(stream0, gain1, shift1))
        query = low(low_back(product(normed1, qkv_weight[0].T) + qv_shift[0]))
        key_all = low(low_back(product(normed1, qkv_weight[1].T)))
        value_all = low(low_back(product(normed1, qkv_weight[2].T) + qv_shift[1]))
        attended = low(low_back(attention(query, key_all, value_all, segment)))
        attn_branch = low_back(product(attended, out_weight) + out_shift)
        stream1 = stream0 + attn_branch
        normed2 = low(layer_norm(stream1, gain2, shift2))
        up_value = low_back(product(normed2, up_weight) + up_shift)
        activation = low(jax.nn.gelu(up_value, approximate=False))
        mlp_branch = low_back(product(activation, down_weight) + down_shift)
        stream2 = stream1 + mlp_branch
        return (valid_rows * stream2, (attn_branch, mlp_branch))
    primals = (tokens.astype(jnp.float32), ln1_gain.astype(jnp.float32), ln1_bias.astype(jnp.float32), w_qkv.astype(jnp.float32), qv_bias.astype(jnp.float32), w_out.astype(jnp.float32), out_bias.astype(jnp.float32), ln2_gain.astype(jnp.float32), ln2_bias.astype(jnp.float32), w_up.astype(jnp.float32), up_bias.astype(jnp.float32), w_down.astype(jnp.float32), down_bias.astype(jnp.float32))
    output_value, backward, branches = jax.vjp(forward, *primals, has_aux=True)
    grads = backward(cotangent.astype(jnp.float32))
    attn_branch, mlp_branch = branches
    count = jnp.sum(valid_rows)
    squares = jnp.stack([jnp.sum(output_value * output_value), jnp.sum(valid_rows * attn_branch * attn_branch), jnp.sum(valid_rows * mlp_branch * mlp_branch)])
    stats = jnp.sqrt(squares / (count * D))
    return (output_value.astype(jnp.bfloat16), grads[0], grads[1], grads[2], grads[3], grads[4], grads[5], grads[6], grads[7], grads[8], grads[9], grads[10], grads[11], grads[12], stats)
```

```python
import functools
import math

import jax
import jax.numpy as jnp
from jax import lax
from jax.experimental import pallas as pl
from jax.experimental.pallas import tpu as pltpu
from jax.sharding import PartitionSpec as P

HD = 64
EPS = 1e-06
MASKED = -1e30
F32 = jnp.float32
BF16 = jnp.bfloat16
NT = (((1,), (1,)), ((), ()))
TN = (((0,), (0,)), ((), ()))
NN = (((1,), (0,)), ((), ()))
VMEM_LIMIT = 56 * 1024 * 1024


def mxu(left, right, dims):
    return lax.dot_general(left, right, dims, preferred_element_type=F32)


def whole(shape):
    return pl.BlockSpec(shape, lambda *_: (0,) * len(shape))


def scalars():
    return pl.BlockSpec(memory_space=pltpu.SMEM)


def call(body, grid, in_specs, out_specs, out_shape, flops, moved, scratch=(), transcendentals=0):
    return pl.pallas_call(
        body,
        grid=grid,
        in_specs=in_specs,
        out_specs=out_specs,
        out_shape=out_shape,
        scratch_shapes=list(scratch),
        compiler_params=pltpu.CompilerParams(
            dimension_semantics=("arbitrary",) * len(grid), vmem_limit_bytes=VMEM_LIMIT
        ),
        cost_estimate=pl.CostEstimate(
            flops=int(flops), bytes_accessed=int(moved), transcendentals=int(transcendentals)
        ),
    )


def like(shape, dtype):
    return jax.ShapeDtypeStruct(shape, dtype)


def item_ends(lengths_ref, item_count):
    ends, total = [], 0
    for item in range(item_count):
        total = total + lengths_ref[item]
        ends.append(total)
    return ends


def segment_of(rows, ends):
    segment = jnp.zeros(rows.shape, jnp.int32)
    for end in ends:
        segment = segment + jnp.where(rows >= end, 1, 0)
    return segment


def scalar_segment(row, ends):
    segment = jnp.int32(0)
    for end in ends:
        segment = segment + jnp.where(row >= end, 1, 0)
    return segment


def valid_column(lengths_ref, item_count, first_row, row_count):
    rows = first_row + lax.broadcasted_iota(jnp.int32, (row_count, 1), 0)
    return jnp.where(rows < item_ends(lengths_ref, item_count)[-1], 1.0, 0.0).astype(F32)


def normalize(stream):
    centred = stream - jnp.mean(stream, axis=1, keepdims=True)
    rstd = lax.rsqrt(jnp.mean(centred * centred, axis=1, keepdims=True) + EPS)
    return centred * rstd, rstd


def norm_back(gradient, scaled, gain, rstd):
    spread = gradient * gain
    first = jnp.mean(spread, axis=1, keepdims=True)
    second = jnp.mean(spread * scaled, axis=1, keepdims=True)
    return rstd * (spread - first - scaled * second)


def column_sum(array):
    return jnp.sum(array, axis=0, keepdims=True)


def sin_cos(angle):
    turns = jnp.floor(angle * (2.0 / math.pi) + 0.5)
    rest = angle - turns * 1.5703125
    rest = rest - turns * 4.837512969970703125e-4
    rest = rest - turns * 7.54978995489188216e-8
    square = rest * rest
    sine = rest + rest * square * (
        -1.6666654611e-1 + square * (8.3321608736e-3 + square * -1.9515295891e-4)
    )
    cosine = (
        1.0
        - 0.5 * square
        + square
        * square
        * (
            4.166664568298827e-2
            + square * (-1.388731625493765e-3 + square * 2.443315711809948e-5)
        )
    )
    quarter = turns.astype(jnp.int32)
    odd = (quarter & 1) == 1
    sine_flip = (quarter & 2) != 0
    cosine_flip = ((quarter + 1) & 2) != 0
    first = jnp.where(odd, cosine, sine)
    second = jnp.where(odd, sine, cosine)
    return jnp.where(sine_flip, -first, first), jnp.where(cosine_flip, -second, second)


def encode_body(item_count, lengths, ratios, place, tokens, freq, gain, bias, stream_out, normed_out):
    rows_here, width = tokens.shape
    row = (
        place[0] * (rows_here * pl.num_programs(0))
        + pl.program_id(0) * rows_here
        + lax.broadcasted_iota(jnp.int32, (rows_here, 1), 0)
    )
    position = jnp.zeros((rows_here, 1), jnp.int32)
    ratio = jnp.zeros((rows_here, 1), F32)
    start = 0
    for item in range(item_count):
        end = start + lengths[item]
        inside = (row >= start) & (row < end)
        position = jnp.where(inside, row - start, position)
        ratio = jnp.where(inside, ratios[item], ratio)
        start = end
    angle = (position.astype(F32) * ratio) * freq[...]
    sine, cosine = sin_cos(angle)
    stream = tokens[...].astype(F32) + jnp.concatenate([sine, cosine], axis=1)
    stream_out[...] = stream
    scaled, _ = normalize(stream)
    normed_out[...] = (scaled * gain[...] + bias[...]).astype(BF16)


def encode(lengths, ratios, place, tokens, gain, bias):
    rows, width = tokens.shape
    half = width // 2
    tile = min(128, rows)
    freq = jnp.exp(jnp.arange(half, dtype=jnp.int32).astype(F32) * (-math.log(10000.0) / half))[None]
    body = functools.partial(encode_body, lengths.shape[0])
    block = pl.BlockSpec((tile, width), lambda i: (i, 0))
    return call(
        body,
        (rows // tile,),
        [scalars(), scalars(), scalars(), block, whole((1, half)), whole((1, width)), whole((1, width))],
        [block, block],
        [like((rows, width), F32), like((rows, width), BF16)],
        60 * rows * width,
        8 * rows * width,
    )(lengths, ratios, place, tokens, freq, gain, bias)


def tile_range(tile, tile_rows, own_rows, place, ends):
    span = max(tile_rows, own_rows)
    group = tile * tile_rows // span
    within = tile * tile_rows - group * span
    piece = group * (span // own_rows)
    first = ((piece ^ place) * own_rows) // span * span + within
    return scalar_segment(first, ends), scalar_segment(first + tile_rows - 1, ends)


def share_item(range_a, range_b, item_count):
    low = jnp.maximum(range_a[0], range_b[0])
    high = jnp.minimum(range_a[1], range_b[1])
    return (low <= high) & (low < item_count)


def marks(tile, tile_rows, own_rows, place, ends):
    rows = tile * tile_rows + lax.broadcasted_iota(jnp.int32, (tile_rows, HD), 0)
    lane = lax.broadcasted_iota(jnp.int32, (tile_rows, HD), 1)
    segment = segment_of(rows ^ (place * own_rows), ends)
    same = segment == lane
    query_marks = jnp.where(same, 1.0, 0.0).astype(BF16)
    key_marks = jnp.where(same | (lane > len(ends)), 0.0, MASKED).astype(BF16)
    return query_marks, key_marks


def attend_body(
    item_count, heads, tile, piece_count, lengths, place_ref, *refs
):
    pieces = refs[:piece_count]
    out, lse_out = refs[piece_count : piece_count + 2]
    qa, ka, vt, acc, top = refs[piece_count + 2 :]
    own_rows = pieces[0].shape[0]
    rows = own_rows * piece_count
    tiles = rows // tile
    width = heads * HD
    place = place_ref[0]
    ends = item_ends(lengths, item_count)
    part = min(tile, own_rows)
    for t in range(tiles):
        query_marks, key_marks = marks(t, tile, own_rows, place, ends)
        for h in range(heads):
            for s in range(tile // part):
                row = t * tile + s * part
                ref = pieces[row // own_rows]
                here = pl.ds(row % own_rows, part)
                there = slice(s * part, (s + 1) * part)
                query = ref[here, h * HD : (h + 1) * HD] * jnp.asarray(HD**-0.5, BF16)
                key = ref[here, width + h * HD : width + (h + 1) * HD]
                value = ref[here, 2 * width + h * HD : 2 * width + (h + 1) * HD]
                qa[h, t, there, :] = jnp.concatenate([query, query_marks[there]], axis=1)
                ka[h, t, there, :] = jnp.concatenate([key, key_marks[there]], axis=1)
                ones = jnp.ones((part, HD), BF16)
                vt[h, t, :, there] = jnp.concatenate([value, ones], axis=1).T

    def query_tile(i, carry):
        range_i = tile_range(i, tile, own_rows, place, ends)

        acc[...] = jnp.zeros(acc.shape, F32)
        top[...] = jnp.full(top.shape, -3e38, F32)

        def key_tile(j, inner):
            @pl.when(share_item(range_i, tile_range(j, tile, own_rows, place, ends), item_count))
            def _():
                scores = [mxu(ka[h, j], qa[h, i], NT) for h in range(heads)]
                for h in range(heads):
                    old = top[h]
                    new = jnp.maximum(old, jnp.max(scores[h], axis=0, keepdims=True))
                    probs = jnp.exp(scores[h] - new).astype(BF16)
                    top[h] = new
                    acc[h] = acc[h] * jnp.exp(old - new) + mxu(vt[h, j], probs, NN)

            return inner

        lax.fori_loop(0, tiles, key_tile, 0)
        for h in range(heads):
            total = jnp.maximum(acc[h, HD : HD + 1, :], 1e-30)
            lse_out[h, i] = top[h] + jnp.log(total)
        mixed = [acc[h, :HD, :] / jnp.maximum(acc[h, HD : HD + 1, :], 1e-30) for h in range(heads)]
        here = pl.ds(pl.multiple_of(i * tile, tile), tile)
        for h in range(0, heads, 2):
            group = mixed[h : h + 2]
            both = jnp.concatenate(group, axis=0) if len(group) > 1 else group[0]
            out[here, h * HD : (h + len(group)) * HD] = both.T.astype(BF16)
        return carry

    lax.fori_loop(0, tiles, query_tile, 0)


def attend(lengths, place, pieces):
    own_rows, width3 = pieces[0].shape
    width = width3 // 3
    heads = width // HD
    rows = own_rows * len(pieces)
    tile = min(256, rows)
    tiles = rows // tile
    body = functools.partial(attend_body, lengths.shape[0], heads, tile, len(pieces))
    return call(
        body,
        (1,),
        [scalars(), scalars()] + [whole((own_rows, width3))] * len(pieces),
        [whole((rows, width)), whole((heads, tiles, 1, tile))],
        [like((rows, width), BF16), like((heads, tiles, 1, tile), F32)],
        rows * rows * width * 2,
        10 * rows * width,
        [
            pltpu.VMEM((heads, tiles, tile, 2 * HD), BF16),
            pltpu.VMEM((heads, tiles, tile, 2 * HD), BF16),
            pltpu.VMEM((heads, tiles, 2 * HD, tile), BF16),
            pltpu.VMEM((heads, 2 * HD, tile), F32),
            pltpu.VMEM((heads, 1, tile), F32),
        ],
    )(lengths, place, *pieces)


def attend_back_body(item_count, heads, tile, piece_count, lengths, place_ref, *refs):
    pieces = refs[:piece_count]
    grads = refs[piece_count : 2 * piece_count]
    mixed, lse, out = refs[2 * piece_count : 2 * piece_count + 3]
    qa, ka, kt, vals, dos, delta, dk, dv, dqt = refs[2 * piece_count + 3 :]
    own_rows = pieces[0].shape[0]
    rows = own_rows * piece_count
    tiles = rows // tile
    width = heads * HD
    place = place_ref[0]
    ends = item_ends(lengths, item_count)
    part = min(tile, own_rows)
    scale = HD**-0.5
    for t in range(tiles):
        query_marks, key_marks = marks(t, tile, own_rows, place, ends)
        for s in range(tile // part):
            row = t * tile + s * part
            ref = pieces[row // own_rows]
            grad_ref = grads[row // own_rows]
            here = pl.ds(row % own_rows, part)
            there = slice(s * part, (s + 1) * part)
            for h in range(heads):
                query = ref[here, h * HD : (h + 1) * HD] * jnp.asarray(scale, BF16)
                key = ref[here, width + h * HD : width + (h + 1) * HD]
                qa[h, t, there, :] = jnp.concatenate([query, query_marks[there]], axis=1)
                ka[h, t, there, :] = jnp.concatenate([key, key_marks[there]], axis=1)
                vals[h, t, there, :] = ref[here, 2 * width + h * HD : 2 * width + (h + 1) * HD]
                dos[h, t, there, :] = grad_ref[here, h * HD : (h + 1) * HD]
            for h in range(0, heads, 2):
                count = min(2, heads - h)
                columns = slice(h * HD, (h + count) * HD)
                keys = ref[here, width + h * HD : width + (h + count) * HD].T
                weighed = (
                    grad_ref[here, columns].astype(F32)
                    * mixed[pl.ds(row, part), columns].astype(F32)
                ).T
                for k in range(count):
                    kt[h + k, t, :, there] = keys[k * HD : (k + 1) * HD]
                    delta[h + k, t, :, there] = column_sum(weighed[k * HD : (k + 1) * HD])
    dqt[...] = jnp.zeros(dqt.shape, F32)

    def key_tile(j, carry):
        range_j = tile_range(j, tile, own_rows, place, ends)
        dk[...] = jnp.zeros(dk.shape, F32)
        dv[...] = jnp.zeros(dv.shape, F32)

        def query_tile(i, inner):
            @pl.when(share_item(range_j, tile_range(i, tile, own_rows, place, ends), item_count))
            def _():
                for h in range(heads):
                    scores = mxu(ka[h, j], qa[h, i], NT)
                    grad_probs = mxu(vals[h, j], dos[h, i], NT)
                    probs = jnp.exp(scores - lse[h, i])
                    grad_scores = (probs * (grad_probs - delta[h, i])).astype(BF16)
                    dv[h] += mxu(probs.astype(BF16), dos[h, i], NN)
                    dk[h] += mxu(grad_scores, qa[h, i], NN)
                    dqt[h, i] += mxu(kt[h, j], grad_scores, NN)

            return inner

        lax.fori_loop(0, tiles, query_tile, 0)
        here = pl.ds(pl.multiple_of(j * tile, tile), tile)
        for h in range(0, heads, 2):
            count = min(2, heads - h)
            keys = [dk[h + k][:, :HD] for k in range(count)]
            values = [dv[h + k] for k in range(count)]
            if count > 1:
                keys, values = [jnp.concatenate(keys, axis=1)], [jnp.concatenate(values, axis=1)]
            out[here, width + h * HD : width + (h + count) * HD] = keys[0].astype(BF16)
            out[here, 2 * width + h * HD : 2 * width + (h + count) * HD] = values[0].astype(BF16)
        return carry

    lax.fori_loop(0, tiles, key_tile, 0)
    for t in range(tiles):
        for h in range(0, heads, 2):
            count = min(2, heads - h)
            both = [dqt[h + k, t] for k in range(count)]
            both = jnp.concatenate(both, axis=0) if count > 1 else both[0]
            out[t * tile : (t + 1) * tile, h * HD : (h + count) * HD] = (both.T * scale).astype(BF16)


def attend_back(lengths, place, pieces, grads, mixed, lse):
    own_rows, width3 = pieces[0].shape
    width = width3 // 3
    heads = width // HD
    rows = own_rows * len(pieces)
    tile = min(256, rows)
    tiles = rows // tile
    body = functools.partial(attend_back_body, lengths.shape[0], heads, tile, len(pieces))
    return call(
        body,
        (1,),
        [scalars(), scalars()]
        + [whole((own_rows, width3))] * len(pieces)
        + [whole((own_rows, width))] * len(pieces)
        + [whole((rows, width)), whole((heads, tiles, 1, tile))],
        whole((rows, width3)),
        like((rows, width3), BF16),
        rows * rows * width * 5,
        16 * rows * width,
        [
            pltpu.VMEM((heads, tiles, tile, 2 * HD), BF16),
            pltpu.VMEM((heads, tiles, tile, 2 * HD), BF16),
            pltpu.VMEM((heads, tiles, HD, tile), BF16),
            pltpu.VMEM((heads, tiles, tile, HD), BF16),
            pltpu.VMEM((heads, tiles, tile, HD), BF16),
            pltpu.VMEM((heads, tiles, 1, tile), F32),
            pltpu.VMEM((heads, tile, 2 * HD), F32),
            pltpu.VMEM((heads, tile, HD), F32),
            pltpu.VMEM((heads, tiles, HD, tile), F32),
        ],
    )(lengths, place, *pieces, *grads, mixed, lse)


def branch_body(item_count, piece_count, lengths, place, *refs):
    mixed = refs[:piece_count]
    weights = refs[piece_count : 2 * piece_count]
    stream0, shift, gain, bias, stream1, normed, squares = refs[2 * piece_count :]
    tile = stream0.shape[0]
    attn = shift[...]
    for left, right in zip(mixed, weights):
        attn = attn + mxu(left[...], right[...], NN)
    first = place[0] * (tile * pl.num_programs(0)) + pl.program_id(0) * tile
    valid = valid_column(lengths, item_count, first, tile)
    stream = stream0[...] + attn
    stream1[...] = stream
    scaled, _ = normalize(stream)
    normed[...] = (scaled * gain[...] + bias[...]).astype(BF16)

    @pl.when(pl.program_id(0) == 0)
    def _():
        squares[...] = jnp.zeros(squares.shape, F32)

    squares[...] += column_sum(valid * attn * attn)


def branch(lengths, place, mixed, weights, stream0, shift, gain, bias):
    rows, width = stream0.shape
    tile = min(256, rows)
    count = len(mixed)
    block = pl.BlockSpec((tile, width), lambda i: (i, 0))
    narrow = pl.BlockSpec((tile, mixed[0].shape[1]), lambda i: (i, 0))
    line = whole((1, width))
    return call(
        functools.partial(branch_body, lengths.shape[0], count),
        (rows // tile,),
        [scalars(), scalars()]
        + [narrow] * count
        + [whole(weights[0].shape)] * count
        + [block, line, line, line],
        [block, block, line],
        [like((rows, width), F32), like((rows, width), BF16), like((1, width), F32)],
        2 * rows * width * width,
        rows * width * 12 + 2 * width * width,
    )(lengths, place, *mixed, *weights, stream0, shift, gain, bias)


def feed_body(normed, grad_mlp, w_up, up_bias, w_down, act_out, upin_out, mlp_out, norm_out, bias_out):
    hidden = w_up.shape[1]
    chunk = min(256, hidden)
    left, grad = normed[...], grad_mlp[...]
    mlp = norm = None

    @pl.when(pl.program_id(0) == 0)
    def _():
        bias_out[...] = jnp.zeros(bias_out.shape, F32)

    for c in range(0, hidden, chunk):
        here = slice(c, c + chunk)
        up = mxu(left, w_up[:, here], NN) + up_bias[:, here]
        grad_act = mxu(grad, w_down[here, :], NT)
        size = jnp.abs(up)
        decay = jnp.exp(-0.5 * up * up)
        t = 1.0 / (1.0 + (0.3275911 * 0.7071067811865476) * size)
        series = t * (
            0.254829592
            + t * (-0.284496736 + t * (1.421413741 + t * (-1.453152027 + t * 1.061405429)))
        )
        tail = 0.5 * series * decay
        share = jnp.where(up >= 0.0, 1.0 - tail, tail)
        act = (up * share).astype(BF16)
        upin = ((share + up * decay * 0.3989422804014327) * grad_act).astype(BF16)
        act_out[:, here] = act
        upin_out[:, here] = upin
        bias_out[:, here] += column_sum(upin.astype(F32))
        mlp_part = mxu(act, w_down[here, :], NN)
        norm_part = mxu(upin, w_up[:, here], NT)
        mlp = mlp_part if mlp is None else mlp + mlp_part
        norm = norm_part if norm is None else norm + norm_part
    mlp_out[...] = mlp.astype(BF16)
    norm_out[...] = norm.astype(BF16)


def feed(normed, grad_mlp, w_up, up_bias, w_down):
    rows, width = normed.shape
    hidden = w_up.shape[1]
    tile = min(256, rows)
    block = pl.BlockSpec((tile, width), lambda i: (i, 0))
    wide = pl.BlockSpec((tile, hidden), lambda i: (i, 0))
    return call(
        feed_body,
        (rows // tile,),
        [block, block, whole(w_up.shape), whole((1, hidden)), whole(w_down.shape)],
        [wide, wide, block, block, whole((1, hidden))],
        [
            like((rows, hidden), BF16),
            like((rows, hidden), BF16),
            like((rows, width), BF16),
            like((rows, width), BF16),
            like((1, hidden), F32),
        ],
        8 * rows * width * hidden,
        12 * rows * width + 4 * width * hidden,
        transcendentals=rows * hidden,
    )(normed, grad_mlp, w_up, up_bias, w_down)


def outer_body(piece_count, *refs):
    left, right, out = refs[:piece_count], refs[piece_count : 2 * piece_count], refs[-1]
    total = None
    for a, b in zip(left, right):
        term = mxu(a[...], b[...], TN)
        total = term if total is None else total + term
    out[...] = total.astype(out.dtype)


def outer(left, right):
    rows, depth = left[0].shape
    width = right[0].shape[1]
    tile = min(256, depth)
    count = len(left)
    return call(
        functools.partial(outer_body, count),
        (depth // tile,),
        [pl.BlockSpec((rows, tile), lambda i: (0, i))] * count + [whole((rows, width))] * count,
        pl.BlockSpec((tile, width), lambda i: (i, 0)),
        like((depth, width), BF16),
        2 * count * rows * depth * width,
        2 * count * rows * (depth + width) + 2 * depth * width,
    )(*left, *right)


def second_back_body(item_count, piece_count, lengths, place, half_a, half_b, stream1, cotangent, gain, *refs):
    weights = refs[:piece_count]
    grad_out, attn_out = refs[piece_count : piece_count + 2]
    mixed_out = refs[piece_count + 2 : 2 * piece_count + 2]
    sums = refs[-1]
    tile = stream1.shape[0]
    first = place[0] * (tile * pl.num_programs(0)) + pl.program_id(0) * tile
    valid = valid_column(lengths, item_count, first, tile)
    grad_norm = half_a[...].astype(F32) + half_b[...].astype(F32)
    scaled, rstd = normalize(stream1[...])
    grad = valid * cotangent[...].astype(F32) + norm_back(grad_norm, scaled, gain[...], rstd)
    grad_out[...] = grad
    rounded = grad.astype(BF16)
    attn_out[...] = rounded

    @pl.when(pl.program_id(0) == 0)
    def _():
        sums[...] = jnp.zeros(sums.shape, F32)

    sums[0:1] += column_sum(grad_norm * scaled)
    sums[1:2] += column_sum(grad_norm)
    sums[2:3] += column_sum(rounded.astype(F32))
    for weight, mixed in zip(weights, mixed_out):
        mixed[...] = mxu(rounded, weight[...], NT).astype(BF16)


def second_back(lengths, place, half_a, half_b, stream1, cotangent, gain, weights):
    rows, width = stream1.shape
    tile = min(256, rows)
    count = len(weights)
    depth = weights[0].shape[0]
    block = pl.BlockSpec((tile, width), lambda i: (i, 0))
    narrow = pl.BlockSpec((tile, depth), lambda i: (i, 0))
    results = call(
        functools.partial(second_back_body, lengths.shape[0], count),
        (rows // tile,),
        [scalars(), scalars(), block, block, block, block, whole((1, width))]
        + [whole(weights[0].shape)] * count,
        [block, block] + [narrow] * count + [whole((8, width))],
        [like((rows, width), F32), like((rows, width), BF16)]
        + [like((rows, depth), BF16)] * count
        + [like((8, width), F32)],
        2 * rows * width * width,
        rows * width * 20 + 2 * width * width,
    )(lengths, place, half_a, half_b, stream1, cotangent, gain, *weights)
    return results[0], results[1], results[2:-1], results[-1][:3]


def output_body(item_count, lengths, place, half_a, half_b, shift, stream1, cotangent, out, sums):
    tile = stream1.shape[0]
    first = place[0] * (tile * pl.num_programs(0)) + pl.program_id(0) * tile
    valid = valid_column(lengths, item_count, first, tile)
    mlp = half_a[...].astype(F32) + half_b[...].astype(F32) + shift[...]
    stream2 = stream1[...] + mlp
    out[...] = (valid * stream2).astype(BF16)

    @pl.when(pl.program_id(0) == 0)
    def _():
        sums[...] = jnp.zeros(sums.shape, F32)

    sums[0:1] += column_sum(valid * stream2 * stream2)
    sums[1:2] += column_sum(valid * mlp * mlp)
    sums[2:3] += column_sum((valid * cotangent[...].astype(F32)).astype(BF16).astype(F32))
    sums[3:4] += jnp.broadcast_to(column_sum(valid), (1, stream1.shape[1]))


def output_end(lengths, place, half_a, half_b, shift, stream1, cotangent):
    rows, width = stream1.shape
    tile = min(256, rows)
    block = pl.BlockSpec((tile, width), lambda i: (i, 0))
    out, sums = call(
        functools.partial(output_body, lengths.shape[0]),
        (rows // tile,),
        [scalars(), scalars(), block, block, whole((1, width)), block, block],
        [block, whole((8, width))],
        [like((rows, width), BF16), like((8, width), F32)],
        12 * rows * width,
        rows * width * 12,
    )(lengths, place, half_a, half_b, shift, stream1, cotangent)
    return out, sums[:4]


def input_body(half_a, half_b, stream0, grad_stream1, gain, out, sums):
    grad_norm = half_a[...].astype(F32) + half_b[...].astype(F32)
    scaled, rstd = normalize(stream0[...])
    out[...] = grad_stream1[...] + norm_back(grad_norm, scaled, gain[...], rstd)

    @pl.when(pl.program_id(0) == 0)
    def _():
        sums[...] = jnp.zeros(sums.shape, F32)

    sums[0:1] += column_sum(grad_norm * scaled)
    sums[1:2] += column_sum(grad_norm)


def input_end(half_a, half_b, stream0, grad_stream1, gain):
    rows, width = stream0.shape
    tile = min(256, rows)
    block = pl.BlockSpec((tile, width), lambda i: (i, 0))
    out, sums = call(
        input_body,
        (rows // tile,),
        [block, block, block, block, whole((1, width))],
        [block, whole((8, width))],
        [like((rows, width), F32), like((8, width), F32)],
        12 * rows * width,
        rows * width * 16,
    )(half_a, half_b, stream0, grad_stream1, gain)
    return out, sums[:2]


def swap(array, axis, bit):
    return lax.ppermute(array, axis, [(i, i ^ bit) for i in range(lax.axis_size(axis))])


def gather(own, axis="mp"):
    pieces = {0: own}
    bit = lax.axis_size(axis) // 2
    while bit:
        for p in sorted(pieces):
            pieces[p | bit] = swap(pieces[p], axis, bit)
        bit //= 2
    return [pieces[p] for p in range(len(pieces))]


def exchange(parts, axis="mp"):
    return [parts[0]] + [swap(parts[p], axis, p) for p in range(1, len(parts))]


def add(left, right):
    return (left.astype(F32) + right.astype(F32)).astype(left.dtype)


def scatter_sum(parts, axis="mp"):
    count, bit = len(parts), 1
    kept = dict(enumerate(parts))
    while bit < count:
        arrived = {p: swap(kept[p | bit], axis, bit) for p in kept if not p & bit}
        if 2 * bit == count:
            return kept[0], arrived[0]
        kept = {p: add(kept[p], arrived[p]) for p in arrived}
        bit *= 2
    return kept[0], jnp.zeros_like(kept[0])


def total(array, axis):
    bit = 1
    while bit < lax.axis_size(axis):
        array = array + swap(array, axis, bit)
        bit *= 2
    return array


def per_device(
    tokens, cotangent, item_lengths, gsd_ratio, ln1_gain, ln1_bias, w_qkv, qv_bias, w_out, out_bias,
    ln2_gain, ln2_bias, w_up, up_bias, w_down, down_bias,
):
    own_rows, width = tokens.shape
    mp_count = lax.axis_size("mp")
    mine = lax.axis_index("mp")
    place = mine.astype(jnp.int32)[None]
    depth = w_qkv.shape[1]
    item_count = item_lengths.shape[0]
    gain1, bias1 = ln1_gain.astype(F32)[None], ln1_bias.astype(F32)[None]
    gain2, bias2 = ln2_gain[None], ln2_bias[None]

    stream0, normed1_own = encode(item_lengths, gsd_ratio, place, tokens, gain1, bias1)
    normed1 = gather(normed1_own)
    w_flat = w_qkv.reshape(3 * depth, width)
    shift = jnp.concatenate([qv_bias[0], jnp.zeros((depth,), F32), qv_bias[1]])[None]
    qkv = [(mxu(piece, w_flat, NT) + shift).astype(BF16) for piece in normed1]

    rows_here = mine * own_rows + jnp.arange(own_rows, dtype=jnp.int32)
    valid = (rows_here < jnp.sum(item_lengths)).astype(F32)[:, None]
    grad_mlp_own = (valid * cotangent.astype(F32)).astype(BF16)
    w_out_all = gather(w_out)
    grad_mlp = gather(grad_mlp_own)

    attended, logsum = attend(item_lengths, place, qkv)
    mixed = exchange([attended[p * own_rows : (p + 1) * own_rows] for p in range(mp_count)])
    stream1, normed2_own, attn_squares = branch(
        item_lengths, place, mixed, w_out_all, stream0, out_bias[None], gain2, bias2
    )
    normed2 = gather(normed2_own)

    fed = [feed(normed2[p], grad_mlp[p], w_up, up_bias[None], w_down) for p in range(mp_count)]
    norm2_a, norm2_b = scatter_sum([f[3] for f in fed])
    mlp_a, mlp_b = scatter_sum([f[2] for f in fed])
    grad_down = outer([f[0] for f in fed], grad_mlp)
    grad_up = outer(normed2, [f[1] for f in fed])
    grad_up_bias = functools.reduce(jnp.add, [f[4] for f in fed])

    grad_stream1, grad_attn, grad_mixed, second_sums = second_back(
        item_lengths, place, norm2_a, norm2_b, stream1, cotangent, gain2, w_out_all
    )
    output, output_sums = output_end(
        item_lengths, place, mlp_a, mlp_b, down_bias[None], stream1, cotangent
    )

    grads = exchange(list(grad_mixed))
    out_a, out_b = scatter_sum([outer([m], [grad_attn]) for m in mixed])
    grad_out_weight = add(out_a, out_b)
    grad_proj = attend_back(item_lengths, place, qkv, grads, attended, logsum)
    proj_parts = [grad_proj[p * own_rows : (p + 1) * own_rows] for p in range(mp_count)]
    norm1_a, norm1_b = scatter_sum([mxu(part, w_flat, NN).astype(BF16) for part in proj_parts])
    grad_qkv = outer(proj_parts, normed1)
    proj_sums = jnp.sum(grad_proj.astype(F32), axis=0)
    input_grad, first_sums = input_end(norm1_a, norm1_b, stream0, grad_stream1, gain1)

    grad_down, grad_up = lax.psum((grad_down, grad_up), "dp")
    grad_qkv, grad_out_weight = lax.psum((grad_qkv, grad_out_weight), "dp")
    rows = jnp.concatenate([first_sums, second_sums, output_sums, attn_squares], axis=0)
    rows = total(rows, "mp")
    flat = jnp.concatenate([rows.reshape(-1), grad_up_bias[0], proj_sums])
    flat = jnp.pad(flat, (0, -flat.size % 1024))
    flat = total(flat.reshape(-1, 128), "dp").reshape(-1)
    rows = flat[: rows.size].reshape(rows.shape)
    up_sums = flat[rows.size : rows.size + up_bias.shape[0]]
    proj_sums = flat[rows.size + up_bias.shape[0] :][: 3 * depth]
    squares = jnp.stack([jnp.sum(rows[5]), jnp.sum(rows[9]), jnp.sum(rows[6])])
    stats = jnp.sqrt(squares / (rows[8, 0] * width))
    return (
        output,
        input_grad,
        rows[0],
        rows[1],
        grad_qkv.astype(F32).reshape(3, depth, width),
        jnp.stack([proj_sums[:depth], proj_sums[2 * depth :]]),
        grad_out_weight.astype(F32),
        rows[4],
        rows[2],
        rows[3],
        grad_up.astype(F32),
        up_sums,
        grad_down.astype(F32),
        rows[7],
        stats,
    )


def solution(mesh):
    rows, one = P(("dp", "mp"), None), P()
    placed = (
        rows, rows, P("dp"), P("dp"), one, one, P(None, "mp", None), P(None, "mp"), P("mp", None), one,
        one, one, P(None, "mp"), P("mp"), P("mp", None), one,
    )
    results = (
        rows, rows, one, one, P(None, "mp", None), P(None, "mp"), P("mp", None), one,
        one, one, P(None, "mp"), P("mp"), P("mp", None), one, one,
    )
    return jax.shard_map(per_device, mesh=mesh, in_specs=placed, out_specs=results, check_vma=False)
```

```python
import functools
import math

import jax
import jax.numpy as jnp
import numpy as np
from jax import lax
from jax.experimental import pallas as pl
from jax.experimental.pallas import tpu as pltpu
from jax.sharding import PartitionSpec as P

HD = 64
EPS = 1e-06
MASKED = -1e30
F32 = jnp.float32
BF16 = jnp.bfloat16
NT = (((1,), (1,)), ((), ()))
TN = (((0,), (0,)), ((), ()))
NN = (((1,), (0,)), ((), ()))


def mxu(left, right, dims):
    return lax.dot_general(left, right, dims, preferred_element_type=F32)


def whole(shape):
    return pl.BlockSpec(shape, lambda *_: (0,) * len(shape))


def scalars():
    return pl.BlockSpec(memory_space=pltpu.SMEM)


def call(body, grid, in_specs, out_specs, out_shape, flops, moved, scratch=(), limit=12):
    return pl.pallas_call(
        body,
        grid=grid,
        in_specs=in_specs,
        out_specs=out_specs,
        out_shape=out_shape,
        scratch_shapes=list(scratch),
        compiler_params=pltpu.CompilerParams(
            dimension_semantics=("arbitrary",) * len(grid), vmem_limit_bytes=limit * 1024 * 1024
        ),
        cost_estimate=pl.CostEstimate(
            flops=0, bytes_accessed=0, transcendentals=0
        ),
    )


def like(shape, dtype):
    return jax.ShapeDtypeStruct(shape, dtype)


def item_ends(lengths_ref, item_count):
    ends, total = [], 0
    for item in range(item_count):
        total = total + lengths_ref[item]
        ends.append(total)
    return ends


def segment_of(rows, ends):
    segment = jnp.zeros(rows.shape, jnp.int32)
    for end in ends:
        segment = segment + jnp.where(rows >= end, 1, 0)
    return segment


def scalar_segment(row, ends):
    segment = jnp.int32(0)
    for end in ends:
        segment = segment + jnp.where(row >= end, 1, 0)
    return segment


def valid_column(lengths_ref, item_count, first_row, row_count):
    rows = first_row + lax.broadcasted_iota(jnp.int32, (row_count, 1), 0)
    return jnp.where(rows < item_ends(lengths_ref, item_count)[-1], 1.0, 0.0).astype(F32)


def normalize(stream):
    centred = stream - jnp.mean(stream, axis=1, keepdims=True)
    rstd = lax.rsqrt(jnp.mean(centred * centred, axis=1, keepdims=True) + EPS)
    return centred * rstd, rstd


def norm_back(gradient, scaled, gain, rstd):
    spread = gradient * gain
    first = jnp.mean(spread, axis=1, keepdims=True)
    second = jnp.mean(spread * scaled, axis=1, keepdims=True)
    return rstd * (spread - first - scaled * second)


def column_sum(array):
    return jnp.sum(array, axis=0, keepdims=True)


def sin_cos(angle):
    turns = jnp.floor(angle * (2.0 / math.pi) + 0.5)
    rest = angle - turns * 1.5703125
    rest = rest - turns * 4.837512969970703125e-4
    rest = rest - turns * 7.54978995489188216e-8
    square = rest * rest
    sine = rest + rest * square * (
        -1.6666654611e-1 + square * (8.3321608736e-3 + square * -1.9515295891e-4)
    )
    cosine = (
        1.0
        - 0.5 * square
        + square
        * square
        * (
            4.166664568298827e-2
            + square * (-1.388731625493765e-3 + square * 2.443315711809948e-5)
        )
    )
    quarter = turns.astype(jnp.int32)
    odd = (quarter & 1) == 1
    sine_flip = (quarter & 2) != 0
    cosine_flip = ((quarter + 1) & 2) != 0
    first = jnp.where(odd, cosine, sine)
    second = jnp.where(odd, sine, cosine)
    return jnp.where(sine_flip, -first, first), jnp.where(cosine_flip, -second, second)


def encode_body(item_count, lengths, ratios, place, tokens, freq, gain, bias, stream_out, normed_out):
    rows_here, width = tokens.shape
    row = (
        place[0] * (rows_here * pl.num_programs(0))
        + pl.program_id(0) * rows_here
        + lax.broadcasted_iota(jnp.int32, (rows_here, 1), 0)
    )
    position = jnp.zeros((rows_here, 1), jnp.int32)
    ratio = jnp.zeros((rows_here, 1), F32)
    start = 0
    for item in range(item_count):
        end = start + lengths[item]
        inside = (row >= start) & (row < end)
        position = jnp.where(inside, row - start, position)
        ratio = jnp.where(inside, ratios[item], ratio)
        start = end
    angle = (position.astype(F32) * ratio) * freq[...]
    sine, cosine = sin_cos(angle)
    stream = tokens[...].astype(F32) + jnp.concatenate([sine, cosine], axis=1)
    stream_out[...] = stream
    scaled, _ = normalize(stream)
    normed_out[...] = (scaled * gain[...].astype(F32) + bias[...].astype(F32)).astype(BF16)


def encode(lengths, ratios, place, tokens, gain, bias):
    rows, width = tokens.shape
    half = width // 2
    tile = min(128, rows)
    freq = np.exp(np.arange(half) * (-math.log(10000.0) / half)).astype(np.float32)[None]
    body = functools.partial(encode_body, lengths.shape[0])
    block = pl.BlockSpec((tile, width), lambda i: (i, 0))
    return call(
        body,
        (rows // tile,),
        [scalars(), scalars(), scalars(), block, whole((1, half)), whole((1, width)), whole((1, width))],
        [block, block],
        [like((rows, width), F32), like((rows, width), BF16)],
        60 * rows * width,
        8 * rows * width,
    )(lengths, ratios, place, tokens, freq, gain, bias)


def mask_body(item_count, lengths, place, cotangent, out):
    rows = cotangent.shape[0]
    valid = valid_column(lengths, item_count, place[0] * rows, rows)
    out[...] = (valid * cotangent[...].astype(F32)).astype(BF16)


def mask_rows(lengths, place, cotangent):
    return call(
        functools.partial(mask_body, lengths.shape[0]),
        (1,),
        [scalars(), scalars(), whole(cotangent.shape)],
        whole(cotangent.shape),
        like(cotangent.shape, BF16),
        2 * cotangent.size,
        4 * cotangent.size,
    )(lengths, place, cotangent)


def local_tile(tile, tile_rows, own_rows, place):
    return tile ^ ((place * own_rows) // tile_rows)


def first_and_last(tile, tile_rows, other_rows, ends):
    low = scalar_segment(tile * tile_rows, ends)
    high = scalar_segment(tile * tile_rows + tile_rows - 1, ends)
    start, stop = jnp.int32(0), jnp.int32(0)
    for item, end in enumerate(ends):
        start = jnp.where(low > item, end, start)
        stop = jnp.where(high >= item, end, stop)
    return start // other_rows, (stop - 1) // other_rows


def used_tiles(tile_rows, ends):
    return (ends[-1] + tile_rows - 1) // tile_rows


def head_lanes(count):
    lane = lax.broadcasted_iota(jnp.int32, (1, 2 * HD), 1)
    return [jnp.where(lane // HD == k, 1.0, 0.0) for k in range(count)]


def marks(tile, tile_rows, own_rows, place, ends):
    rows = tile * tile_rows + lax.broadcasted_iota(jnp.int32, (tile_rows, 2 * HD), 0)
    lane = lax.broadcasted_iota(jnp.int32, (tile_rows, 2 * HD), 1) % HD
    same = segment_of(rows ^ (place * own_rows), ends) == lane
    query_marks = jnp.where(same, 1.0, 0.0)
    key_marks = jnp.where(same | (lane > len(ends)), 0.0, MASKED)
    return query_marks, key_marks


class Rows:
    def __init__(self, tile_rows, own_rows):
        self.part = min(tile_rows, own_rows)
        self.tile_rows, self.own_rows = tile_rows, own_rows

    def pair(self, refs, tile, column, count):
        found = []
        for row in range(tile * self.tile_rows, (tile + 1) * self.tile_rows, self.part):
            ref = refs[row // self.own_rows]
            found.append(ref[pl.ds(row % self.own_rows, self.part), column : column + count * HD])
        found = found[0] if len(found) == 1 else jnp.concatenate(found, axis=0)
        if count == 1:
            found = jnp.concatenate([found, jnp.zeros_like(found)], axis=1)
        return found


def attend_body(item_count, heads, tile_q, tile, piece_count, lengths, place_ref, *refs):
    pieces = refs[:piece_count]
    out, lse_out = refs[piece_count : piece_count + 2]
    qa, ka, vt, acc, top = refs[piece_count + 2 :]
    own_rows = pieces[0].shape[0]
    tiles = own_rows * piece_count // tile
    ratio = tile_q // tile
    width = heads * HD
    place = place_ref[0]
    ends = item_ends(lengths, item_count)
    rows = Rows(tile, own_rows)
    lanes = head_lanes(2)
    for t in range(tiles):
        query_marks, key_marks = marks(t, tile, own_rows, place, ends)
        here = slice(t % ratio * tile, (t % ratio + 1) * tile)
        for h in range(0, heads, 2):
            count = min(2, heads - h)
            query = rows.pair(pieces, t, h * HD, count)
            key = rows.pair(pieces, t, width + h * HD, count)
            value = rows.pair(pieces, t, 2 * width + h * HD, count).T
            for k in range(count):
                mine, other = lanes[k], lanes[1 - k]
                scale = (mine * HD**-0.5).astype(BF16)
                qa[h + k, t // ratio, here] = query * scale + (query_marks * other).astype(BF16)
                ka[h + k, t] = key * mine.astype(BF16) + (key_marks * other).astype(BF16)
                vt[h + k, t, :HD] = value[k * HD : (k + 1) * HD]
                vt[h + k, t, HD:] = jnp.ones((vt.shape[2] - HD, tile), BF16)

    def query_tile(tile_index, carry):
        i = local_tile(tile_index, tile_q, own_rows, place)
        first, last = first_and_last(tile_index, tile_q, tile, ends)
        acc[...] = jnp.zeros(acc.shape, F32)
        top[...] = jnp.full(top.shape, -3e38, F32)

        def key_tile(other_index, inner):
            j = local_tile(other_index, tile, own_rows, place)
            scores = [mxu(ka[h, j], qa[h, i], NT) for h in range(heads)]
            old = [top[h] for h in range(heads)]
            new = [jnp.maximum(old[h], jnp.max(scores[h], axis=0, keepdims=True)) for h in range(heads)]
            probs = [jnp.exp(scores[h] - new[h]).astype(BF16) for h in range(heads)]
            mixed = [mxu(vt[h, j], probs[h], NN) for h in range(heads)]
            for h in range(heads):
                top[h] = new[h]
                acc[h] = acc[h] * jnp.exp(old[h] - new[h]) + mixed[h]
            return inner

        lax.fori_loop(first, last + 1, key_tile, 0)
        here = pl.ds(pl.multiple_of(i * tile_q, tile_q), tile_q)
        for h in range(0, heads, 2):
            count = min(2, heads - h)
            mixed = []
            for k in range(count):
                total = acc[h + k, HD : HD + 1, :]
                lse = top[h + k] + jnp.log(total)
                for s in range(ratio):
                    lse_out[h + k, i * ratio + s] = lse[:, s * tile : (s + 1) * tile]
                mixed.append(acc[h + k, :HD, :] / total)
            mixed = jnp.concatenate(mixed, axis=0) if count > 1 else mixed[0]
            out[here, h * HD : (h + count) * HD] = mixed.T.astype(BF16)
        return carry

    def unused_tile(tile_index, carry):
        i = local_tile(tile_index, tile_q, own_rows, place)
        for s in range(ratio):
            lse_out[:, i * ratio + s] = jnp.zeros((heads, 1, tile), F32)
        out[pl.ds(pl.multiple_of(i * tile_q, tile_q), tile_q), :] = jnp.zeros((tile_q, width), BF16)
        return carry

    used = used_tiles(tile_q, ends)
    lax.fori_loop(0, used, query_tile, 0)
    lax.fori_loop(used, tiles // ratio, unused_tile, 0)


def attend(lengths, place, pieces):
    own_rows, width3 = pieces[0].shape
    width = width3 // 3
    heads = width // HD
    rows = own_rows * len(pieces)
    tile = min(256, rows)
    tile_q = min(512, rows)
    tiles = rows // tile
    body = functools.partial(attend_body, lengths.shape[0], heads, tile_q, tile, len(pieces))
    return call(
        body,
        (1,),
        [scalars(), scalars()] + [whole((own_rows, width3))] * len(pieces),
        [whole((rows, width)), whole((heads, tiles, 1, tile))],
        [like((rows, width), BF16), like((heads, tiles, 1, tile), F32)],
        rows * rows * width * 2,
        10 * rows * width,
        [
            pltpu.VMEM((heads, rows // tile_q, tile_q, 2 * HD), BF16),
            pltpu.VMEM((heads, tiles, tile, 2 * HD), BF16),
            pltpu.VMEM((heads, tiles, HD + 16, tile), BF16),
            pltpu.VMEM((heads, HD + 16, tile_q), F32),
            pltpu.VMEM((heads, 1, tile_q), F32),
        ],
        limit=20,
    )(lengths, place, *pieces)


def attend_back_body(item_count, start, heads, tile, piece_count, lengths, place_ref, *refs):
    pieces = refs[:piece_count]
    grads = refs[piece_count : 2 * piece_count]
    mixed, lse, out, sums = refs[2 * piece_count : 2 * piece_count + 4]
    qa, qm, ka, kt, vals, dos, delta, dk, dv, dqt = refs[2 * piece_count + 4 :]
    own_rows = pieces[0].shape[0]
    tiles = own_rows * piece_count // tile
    width = heads * HD
    full = pieces[0].shape[1] // 3
    base = start * HD
    place = place_ref[0]
    ends = item_ends(lengths, item_count)
    rows = Rows(tile, own_rows)
    lanes = head_lanes(2)
    scale = HD**-0.5
    for t in range(tiles):
        query_marks, key_marks = marks(t, tile, own_rows, place, ends)
        for h in range(0, heads, 2):
            count = min(2, heads - h)
            column = base + h * HD
            query = rows.pair(pieces, t, column, count)
            key = rows.pair(pieces, t, full + column, count)
            grad = rows.pair(grads, t, column, count)
            came = mixed[t * tile : (t + 1) * tile, column : column + count * HD].astype(F32)
            if count == 1:
                came = jnp.concatenate([came, jnp.zeros_like(came)], axis=1)
            weighed = (grad.astype(F32) * came).T
            turned = key.T
            vals[h // 2, t] = rows.pair(pieces, t, 2 * full + column, count)
            for k in range(count):
                mine, other = lanes[k], lanes[1 - k]
                alone = query * (mine * scale).astype(BF16)
                qm[h + k, t] = alone
                qa[h + k, t] = alone + (query_marks * other).astype(BF16)
                ka[h + k, t] = key * mine.astype(BF16) + (key_marks * other).astype(BF16)
                dos[h + k, t] = grad * mine.astype(BF16)
                kt[h + k, t] = turned[k * HD : (k + 1) * HD]
                delta[h + k, t] = column_sum(weighed[k * HD : (k + 1) * HD])
    dqt[...] = jnp.zeros(dqt.shape, F32)

    def key_tile(tile_index, carry):
        j = local_tile(tile_index, tile, own_rows, place)
        first, last = first_and_last(tile_index, tile, tile, ends)
        dk[...] = jnp.zeros(dk.shape, F32)
        dv[...] = jnp.zeros(dv.shape, F32)

        def query_tile(other_index, inner):
            i = local_tile(other_index, tile, own_rows, place)
            scores = [mxu(ka[h, j], qa[h, i], NT) for h in range(heads)]
            grad_probs = [mxu(vals[h // 2, j], dos[h, i], NT) for h in range(heads)]
            for h in range(heads):
                probs = jnp.exp(scores[h] - lse[start + h, i])
                grad_scores = (probs * (grad_probs[h] - delta[h, i])).astype(BF16)
                dv[h] += mxu(probs.astype(BF16), dos[h, i], NN)
                dk[h] += mxu(grad_scores, qm[h, i], NN)
                dqt[h, i] += mxu(kt[h, j], grad_scores, NN)
            return inner

        lax.fori_loop(first, last + 1, query_tile, 0)
        here = pl.ds(pl.multiple_of(j * tile, tile), tile)
        for h in range(0, heads, 2):
            count = min(2, heads - h)
            first = width + h * HD
            for kept, column in ((dk, first), (dv, width + first)):
                both = kept[h] + kept[h + 1] if count > 1 else kept[h]
                out[here, column : column + count * HD] = both[:, : count * HD].astype(BF16)
        return carry

    def unused_tile(tile_index, carry):
        j = local_tile(tile_index, tile, own_rows, place)
        here = pl.ds(pl.multiple_of(j * tile, tile), tile)
        out[here, width:] = jnp.zeros((tile, 2 * width), BF16)
        return carry

    used = used_tiles(tile, ends)
    lax.fori_loop(0, used, key_tile, 0)
    lax.fori_loop(used, tiles, unused_tile, 0)
    for t in range(tiles):
        for h in range(0, heads, 2):
            count = min(2, heads - h)
            both = [dqt[h + k, t] for k in range(count)]
            both = jnp.concatenate(both, axis=0) if count > 1 else both[0]
            out[t * tile : (t + 1) * tile, h * HD : (h + count) * HD] = (both.T * scale).astype(BF16)
    sums[...] = column_sum(out[...].astype(F32))


def attend_back(lengths, place, pieces, grads, mixed, lse, start, heads):
    own_rows = pieces[0].shape[0]
    width = heads * HD
    pairs = (heads + 1) // 2
    rows = own_rows * len(pieces)
    tile = min(256, rows)
    tiles = rows // tile
    body = functools.partial(attend_back_body, lengths.shape[0], start, heads, tile, len(pieces))
    return call(
        body,
        (1,),
        [scalars(), scalars()]
        + [whole(piece.shape) for piece in pieces]
        + [whole(grad.shape) for grad in grads]
        + [whole(mixed.shape), whole(lse.shape)],
        [whole((rows, 3 * width)), whole((1, 3 * width))],
        [like((rows, 3 * width), BF16), like((1, 3 * width), F32)],
        rows * rows * width * 5,
        16 * rows * width,
        [
            pltpu.VMEM((heads, tiles, tile, 2 * HD), BF16),
            pltpu.VMEM((heads, tiles, tile, 2 * HD), BF16),
            pltpu.VMEM((heads, tiles, tile, 2 * HD), BF16),
            pltpu.VMEM((heads, tiles, HD, tile), BF16),
            pltpu.VMEM((pairs, tiles, tile, 2 * HD), BF16),
            pltpu.VMEM((heads, tiles, tile, 2 * HD), BF16),
            pltpu.VMEM((heads, tiles, 1, tile), F32),
            pltpu.VMEM((heads, tile, 2 * HD), F32),
            pltpu.VMEM((heads, tile, 2 * HD), F32),
            pltpu.VMEM((heads, tiles, HD, tile), F32),
        ],
        limit=20,
    )(lengths, place, *pieces, *grads, mixed, lse)


def branch_body(item_count, piece_count, lengths, place, *refs):
    mixed = refs[:piece_count]
    weights = refs[piece_count : 2 * piece_count]
    stream0, shift, gain, bias, stream1, normed, squares = refs[2 * piece_count :]
    tile = stream0.shape[0]
    attn = shift[...]
    for left, right in zip(mixed, weights):
        attn = attn + mxu(left[...], right[...], NN)
    first = place[0] * (tile * pl.num_programs(0)) + pl.program_id(0) * tile
    valid = valid_column(lengths, item_count, first, tile)
    stream = stream0[...] + attn
    stream1[...] = stream
    scaled, _ = normalize(stream)
    normed[...] = (scaled * gain[...] + bias[...]).astype(BF16)

    @pl.when(pl.program_id(0) == 0)
    def _():
        squares[...] = jnp.zeros(squares.shape, F32)

    squares[...] += column_sum(valid * attn * attn)


def branch(lengths, place, mixed, weights, stream0, shift, gain, bias):
    rows, width = stream0.shape
    tile = min(256, rows)
    count = len(mixed)
    block = pl.BlockSpec((tile, width), lambda i: (i, 0))
    narrow = pl.BlockSpec((tile, mixed[0].shape[1]), lambda i: (i, 0))
    line = whole((1, width))
    return call(
        functools.partial(branch_body, lengths.shape[0], count),
        (rows // tile,),
        [scalars(), scalars()]
        + [narrow] * count
        + [whole(weights[0].shape)] * count
        + [block, line, line, line],
        [block, block, line],
        [like((rows, width), F32), like((rows, width), BF16), like((1, width), F32)],
        2 * rows * width * width,
        rows * width * 12 + 2 * width * width,
    )(lengths, place, *mixed, *weights, stream0, shift, gain, bias)


def feed_body(normed, grad_mlp, w_up, up_bias, w_down, act_out, upin_out, mlp_out, norm_out, bias_out):
    hidden = w_up.shape[1]
    chunk = min(512, hidden)
    left, grad = normed[...], grad_mlp[...]
    mlp = norm = None

    @pl.when(pl.program_id(0) == 0)
    def _():
        bias_out[...] = jnp.zeros(bias_out.shape, F32)

    for c in range(0, hidden, chunk):
        here = slice(c, c + chunk)
        up = mxu(left, w_up[:, here], NN) + up_bias[:, here]
        grad_act = mxu(grad, w_down[here, :], NT)
        size = jnp.abs(up)
        decay = jnp.exp(-0.5 * up * up)
        t = 1.0 / (1.0 + (0.3275911 * 0.7071067811865476) * size)
        series = t * (
            0.254829592
            + t * (-0.284496736 + t * (1.421413741 + t * (-1.453152027 + t * 1.061405429)))
        )
        tail = 0.5 * series * decay
        share = jnp.where(up >= 0.0, 1.0 - tail, tail)
        act = (up * share).astype(BF16)
        upin = ((share + up * decay * 0.3989422804014327) * grad_act).astype(BF16)
        act_out[:, here] = act
        upin_out[:, here] = upin
        bias_out[:, here] += column_sum(upin.astype(F32))
        mlp_part = mxu(act, w_down[here, :], NN)
        norm_part = mxu(upin, w_up[:, here], NT)
        mlp = mlp_part if mlp is None else mlp + mlp_part
        norm = norm_part if norm is None else norm + norm_part
    mlp_out[...] = mlp.astype(BF16)
    norm_out[...] = norm.astype(BF16)


def feed(normed, grad_mlp, w_up, up_bias, w_down):
    rows, width = normed.shape
    hidden = w_up.shape[1]
    tile = min(512, rows)
    block = pl.BlockSpec((tile, width), lambda i: (i, 0))
    wide = pl.BlockSpec((tile, hidden), lambda i: (i, 0))
    return call(
        feed_body,
        (rows // tile,),
        [block, block, whole(w_up.shape), whole((1, hidden)), whole(w_down.shape)],
        [wide, wide, block, block, whole((1, hidden))],
        [
            like((rows, hidden), BF16),
            like((rows, hidden), BF16),
            like((rows, width), BF16),
            like((rows, width), BF16),
            like((1, hidden), F32),
        ],
        8 * rows * width * hidden,
        12 * rows * width + 4 * width * hidden,
        limit=24,
    )(normed, grad_mlp, w_up, up_bias, w_down)


def splits(rows, bits):
    return bits and rows % (16 * 2 ** len(bits)) == 0


def position(block, bits):
    found, step = 0, 2 ** len(bits) // 2
    for bit in bits:
        found = found + jnp.where(block & bit != 0, step, 0)
        step //= 2
    return found


def put(value, first_row, bits, here, kept, sent):
    if sent is None:
        kept[first_row : first_row + value.shape[0]] = value
        return
    half = kept.shape[0]
    size = 2 * half // 2 ** len(bits)
    step = math.gcd(size, value.shape[0])
    for row in range(first_row, first_row + value.shape[0], step):
        spot = position((row // size) ^ here, bits) * size + row % size
        part = value[row - first_row : row - first_row + step]

        @pl.when(spot < half)
        def _():
            kept[pl.ds(pl.multiple_of(spot, 16), step)] = part

        @pl.when(spot >= half)
        def _():
            sent[pl.ds(pl.multiple_of(spot - half, 16), step)] = part


def outer_body(bits, tile, count, place, *refs):
    left, right = refs[:-2 - count], refs[-2 - count : -2]
    kept, sent = refs[-2:]
    for first in range(0, left[0].shape[1], tile):
        total = None
        for p in range(count):
            if len(left) == count:
                a = left[p][:, first : first + tile]
            else:
                size = right[0].shape[0]
                a = left[0][p * size : (p + 1) * size, first : first + tile]
            term = mxu(a, right[p][...], TN)
            total = term if total is None else total + term
        put(total.astype(BF16), first, bits, place[1], kept, sent)


def outer(place, left, right, bits):
    depth = left[0].shape[1]
    rows, width = right[0].shape
    count = len(right)
    tile = 256 if depth % 256 == 0 else depth
    halves = 2 if splits(depth, bits) else 1
    body = functools.partial(outer_body, bits, tile, count)
    if halves == 1:
        body = lambda *refs: outer_body(bits, tile, count, *refs, None)
    return call(
        body,
        (1,),
        [scalars()] + [whole(a.shape) for a in left] + [whole((rows, width))] * count,
        [whole((depth // halves, width))] * halves,
        [like((depth // halves, width), BF16)] * halves,
        2 * count * rows * depth * width,
        2 * count * rows * (depth + width) + 2 * depth * width,
        limit=24,
    )(place, *left, *right)


def each_body(bits, count, place, *refs):
    for left, out in zip(refs[:count], refs[count + 1 :]):
        value = mxu(left[...], refs[count][...], TN).astype(BF16)
        depth = value.shape[0]
        if splits(depth, bits):
            put(value, 0, bits, place[1], out.at[: depth // 2], out.at[depth // 2 :])
        else:
            out[...] = value


def outer_each(place, left, right, bits):
    rows, depth = left[0].shape
    width = right.shape[1]
    count = len(left)
    return call(
        functools.partial(each_body, bits, count),
        (1,),
        [scalars()] + [whole((rows, depth))] * count + [whole((rows, width))],
        [whole((depth, width))] * count,
        [like((depth, width), BF16)] * count,
        2 * count * rows * depth * width,
        2 * (count * rows * depth + rows * width + count * depth * width),
    )(place, *left, right)


def unpack_body(bits, sections, place, first, second, *outs):
    half, shares = first.shape[0], 2 ** len(bits)
    size = 2 * half // shares
    for block in range(shares):
        spot = position(block ^ place[1], bits) * size
        offset = 0
        for out, rows in zip(outs, sections):
            count = rows // shares
            start = spot + offset
            low = pl.ds(pl.multiple_of(jnp.minimum(start, half - count), 16), count)
            high = pl.ds(pl.multiple_of(jnp.maximum(start - half, 0), 16), count)
            part = jnp.where(spot < half, first[low], second[high])
            out[block * count : (block + 1) * count] = part.astype(out.dtype)
            offset += count


def unpack(place, first, second, bits, sections, dtype=F32):
    half, width = first.shape
    return call(
        functools.partial(unpack_body, bits, sections),
        (1,),
        [scalars(), whole(first.shape), whole(second.shape)],
        [whole((rows, width)) for rows in sections],
        [like((rows, width), dtype) for rows in sections],
        2 * half * width,
        12 * half * width,
    )(place, first, second)


def project_body(group_count, piece_count, *refs):
    grads = refs[:group_count]
    weights = refs[group_count : 2 * group_count]
    normed = refs[2 * group_count : 2 * group_count + piece_count]
    outs = refs[2 * group_count + piece_count : -1]
    sums = refs[-1]
    size = normed[0].shape[0]
    plain = weighed = 0.0
    for p in range(piece_count):
        total = None
        for grad, weight in zip(grads, weights):
            term = mxu(grad[p * size : (p + 1) * size], weight[...], NN)
            total = term if total is None else total + term
        outs[p][...] = total.astype(BF16)
        plain = plain + column_sum(total)
        weighed = weighed + column_sum(total * normed[p][...].astype(F32))
    sums[0:1] = plain
    sums[1:2] = weighed


def project_back(grads, weights, normed):
    size, width = normed[0].shape
    depth = sum(w.shape[0] for w in weights)
    count = len(normed)
    results = call(
        functools.partial(project_body, len(grads), count),
        (1,),
        [whole(g.shape) for g in grads] + [whole(w.shape) for w in weights] + [whole((size, width))] * count,
        [whole((size, width))] * count + [whole((8, width))],
        [like((size, width), BF16)] * count + [like((8, width), F32)],
        2 * count * size * depth * width,
        2 * count * size * (depth + 2 * width) + 2 * depth * width,
        limit=20,
    )(*grads, *weights, *normed)
    return list(results[:-1]), results[-1][:2]


def second_back_body(item_count, piece_count, lengths, place, half_a, half_b, stream1, cotangent, gain, *refs):
    weights = refs[:piece_count]
    grad_out, attn_out = refs[piece_count : piece_count + 2]
    mixed_out = refs[piece_count + 2 : 2 * piece_count + 2]
    sums = refs[-1]
    tile = stream1.shape[0]
    first = place[0] * (tile * pl.num_programs(0)) + pl.program_id(0) * tile
    valid = valid_column(lengths, item_count, first, tile)
    grad_norm = half_a[...].astype(F32) + half_b[...].astype(F32)
    scaled, rstd = normalize(stream1[...])
    grad = valid * cotangent[...].astype(F32) + norm_back(grad_norm, scaled, gain[...], rstd)
    grad_out[...] = grad
    rounded = grad.astype(BF16)
    attn_out[...] = rounded

    @pl.when(pl.program_id(0) == 0)
    def _():
        sums[...] = jnp.zeros(sums.shape, F32)

    sums[0:1] += column_sum(grad_norm * scaled)
    sums[1:2] += column_sum(grad_norm)
    sums[2:3] += column_sum(rounded.astype(F32))
    for weight, mixed in zip(weights, mixed_out):
        mixed[...] = mxu(rounded, weight[...], NT).astype(BF16)


def second_back(lengths, place, half_a, half_b, stream1, cotangent, gain, weights):
    rows, width = stream1.shape
    tile = min(256, rows)
    count = len(weights)
    depth = weights[0].shape[0]
    block = pl.BlockSpec((tile, width), lambda i: (i, 0))
    narrow = pl.BlockSpec((tile, depth), lambda i: (i, 0))
    results = call(
        functools.partial(second_back_body, lengths.shape[0], count),
        (rows // tile,),
        [scalars(), scalars(), block, block, block, block, whole((1, width))]
        + [whole(weights[0].shape)] * count,
        [block, block] + [narrow] * count + [whole((8, width))],
        [like((rows, width), F32), like((rows, width), BF16)]
        + [like((rows, depth), BF16)] * count
        + [like((8, width), F32)],
        2 * rows * width * width,
        rows * width * 20 + 2 * width * width,
    )(lengths, place, half_a, half_b, stream1, cotangent, gain, *weights)
    return results[0], results[1], results[2:-1], results[-1][:3]


def output_body(item_count, lengths, place, half_a, half_b, shift, stream1, cotangent, out, sums):
    tile = stream1.shape[0]
    first = place[0] * (tile * pl.num_programs(0)) + pl.program_id(0) * tile
    valid = valid_column(lengths, item_count, first, tile)
    mlp = half_a[...].astype(F32) + half_b[...].astype(F32) + shift[...]
    stream2 = stream1[...] + mlp
    out[...] = (valid * stream2).astype(BF16)

    @pl.when(pl.program_id(0) == 0)
    def _():
        sums[...] = jnp.zeros(sums.shape, F32)

    sums[0:1] += column_sum(valid * stream2 * stream2)
    sums[1:2] += column_sum(valid * mlp * mlp)
    sums[2:3] += column_sum((valid * cotangent[...].astype(F32)).astype(BF16).astype(F32))
    sums[3:4] += jnp.broadcast_to(column_sum(valid), (1, stream1.shape[1]))


def output_end(lengths, place, half_a, half_b, shift, stream1, cotangent):
    rows, width = stream1.shape
    tile = min(256, rows)
    block = pl.BlockSpec((tile, width), lambda i: (i, 0))
    out, sums = call(
        functools.partial(output_body, lengths.shape[0]),
        (rows // tile,),
        [scalars(), scalars(), block, block, whole((1, width)), block, block],
        [block, whole((8, width))],
        [like((rows, width), BF16), like((8, width), F32)],
        12 * rows * width,
        rows * width * 12,
    )(lengths, place, half_a, half_b, shift, stream1, cotangent)
    return out, sums[:4]


def input_body(half_a, half_b, stream0, grad_stream1, gain, out):
    grad_norm = half_a[...].astype(F32) + half_b[...].astype(F32)
    scaled, rstd = normalize(stream0[...])
    out[...] = grad_stream1[...] + norm_back(grad_norm, scaled, gain[...].astype(F32), rstd)


def input_end(half_a, half_b, stream0, grad_stream1, gain):
    rows, width = stream0.shape
    tile = min(256, rows)
    block = pl.BlockSpec((tile, width), lambda i: (i, 0))
    return call(
        input_body,
        (rows // tile,),
        [block, block, block, block, whole((1, width))],
        block,
        like((rows, width), F32),
        12 * rows * width,
        rows * width * 16,
    )(half_a, half_b, stream0, grad_stream1, gain)


def swap(array, axis, bit):
    return lax.ppermute(array, axis, [(i, i ^ bit) for i in range(lax.axis_size(axis))])


def after(array, *others):
    return lax.optimization_barrier((array, *others))[0]


def spread(own, top):
    pieces, bit = {0: own}, top // 2
    while bit:
        for p in sorted(pieces):
            pieces[p | bit] = swap(pieces[p], "mp", bit)
        bit //= 2
    return [pieces[p] for p in range(len(pieces))]


def add(left, right):
    return (left.astype(F32) + right.astype(F32)).astype(left.dtype)


def fold(parts):
    bit = 1
    while len(parts) > 1:
        parts = [add(parts[p], swap(parts[p + 1], "mp", bit)) for p in range(0, len(parts), 2)]
        bit *= 2
    return parts[0]


def exchange(parts):
    return [parts[0]] + [swap(parts[p], "mp", p) for p in range(1, len(parts))]


def total(array, axis):
    bit = 1
    while bit < lax.axis_size(axis):
        array = array + swap(array, axis, bit)
        bit *= 2
    return array


def own_block(place, weight, bits):
    if not splits(weight.shape[0], bits):
        return weight
    size = weight.shape[0] // 2 ** len(bits)
    return lax.dynamic_slice_in_dim(weight, place[1] * size, size, 0)


def join_blocks(place, kept, rows, bits):
    if kept.shape[0] == rows:
        return kept
    for bit in bits[:0:-1]:
        kept = jnp.concatenate([kept, swap(kept, "dp", bit)], axis=0)
    return unpack(place, kept, swap(kept, "dp", bits[0]), bits, [rows], kept.dtype)[0]


class DpSum:
    def __init__(self, place, parts, bits, *others):
        self.place, self.bits, self.steps = place, bits, 0
        self.sections = [sum(half.shape[0] for half in halves) for halves in parts]
        blocks, width = max(2 ** len(bits) // 2, 1), parts[0][0].shape[1]
        halves = [
            jnp.concatenate([half.reshape(blocks, -1, width) for half in group], axis=1).reshape(-1, width)
            for group in zip(*parts)
        ]
        if len(halves) == 1:
            self.kept = lax.psum(halves[0], "dp")
            return
        self.kept, self.sent = halves
        self.came = swap(after(self.sent, *others), "dp", bits[0])

    def step(self, *others):
        if not self.more():
            return
        self.steps += 1
        came, count = after(self.came, *others), len(self.bits)
        if self.steps < count:
            half = came.shape[0] // 2
            self.sent = add(self.kept[half:], came[half:])
            self.kept = add(self.kept[:half], came[:half])
            self.came = swap(self.sent, "dp", self.bits[self.steps])
        elif self.steps < 2 * count:
            if self.steps == count:
                self.kept = add(self.kept, came)
            else:
                self.kept = jnp.concatenate([self.kept, came], axis=0)
            self.sent = self.kept
            self.came = swap(self.kept, "dp", self.bits[2 * count - 1 - self.steps])

    def now(self):
        return [self.kept, self.sent] if hasattr(self, "came") else []

    def more(self):
        return hasattr(self, "came") and self.steps < 2 * len(self.bits) - 1

    def done(self):
        if not hasattr(self, "came"):
            return [self.kept.astype(F32)]
        return unpack(self.place, self.kept, self.came, self.bits, self.sections)


def advance(chains, others):
    for chain in chains:
        chain.step(*others)
    return [array for chain in chains for array in chain.now()] or list(others)


def per_device(
    tokens, cotangent, lengths, gsd_ratio, ln1_gain, ln1_bias, w_qkv, qv_bias, w_out, out_bias,
    ln2_gain, ln2_bias, w_up, up_bias, w_down, down_bias,
):
    own_rows, width = tokens.shape
    mp_count, dp_count = lax.axis_size("mp"), lax.axis_size("dp")
    top = mp_count // 2
    low_first = [1 << k for k in range(dp_count.bit_length() - 1)] if dp_count & (dp_count - 1) == 0 else []
    low_second = low_first[1:2] + low_first[:1] + low_first[2:]
    place = jnp.stack([lax.axis_index("mp"), lax.axis_index("dp")]).astype(jnp.int32)
    depth = w_qkv.shape[1]
    heads = depth // HD
    gain2, bias2 = ln2_gain[None], ln2_bias[None]
    up_shift = up_bias[None]

    w_out_block = swap(own_block(place, w_out, low_first), "mp", top)
    tokens = after(tokens, w_out_block)
    stream0, normed1_own = encode(lengths, gsd_ratio, place, tokens, ln1_gain[None], ln1_bias[None])
    normed1_far = swap(normed1_own, "mp", top)
    w_out_far = join_blocks(place, w_out_block, depth, low_first)
    normed1 = spread(normed1_own, top)
    w_flat = w_qkv.reshape(3 * depth, width)
    shift = jnp.concatenate([qv_bias[0], jnp.zeros((depth,), F32), qv_bias[1]])[None]

    def project(piece):
        return (mxu(piece, w_flat, NT) + shift).astype(BF16)

    qkv = [project(piece) for piece in normed1]
    grad_mlp_own = mask_rows(lengths, place, cotangent)
    grad_mlp = spread(grad_mlp_own, top)
    w_out_all = spread(w_out, top)
    normed1_far = after(normed1_far, w_out_far, *qkv, *grad_mlp, *w_out_all)
    grad_mlp_far = swap(after(grad_mlp_own, normed1_far), "mp", top)
    normed1 += spread(normed1_far, top)
    w_out_all += spread(w_out_far, top)
    qkv += [project(piece) for piece in normed1[top:]]

    attended, logsum = attend(lengths, place, qkv)
    attended, grad_mlp_far = lax.optimization_barrier((attended, grad_mlp_far))
    mixed = exchange([attended[p * own_rows : (p + 1) * own_rows] for p in range(mp_count)])
    grad_mlp += spread(grad_mlp_far, top)
    mixed[0] = after(mixed[0], *grad_mlp)
    stream1, normed2_own, attn_squares = branch(
        lengths, place, mixed, w_out_all, stream0, out_bias[None], gain2, bias2
    )

    normed2_far = swap(normed2_own, "mp", top)
    normed2 = spread(normed2_own, top)
    fed = [feed(normed2[p], grad_mlp[p], w_up, up_shift, w_down) for p in range(top)]
    normed2_far = after(normed2_far, *[f[3] for f in fed])
    normed2 += spread(normed2_far, top)
    norm2_near = fold([f[3] for f in fed])
    mlp_near = fold([f[2] for f in fed])
    normed2[-1] = after(normed2[-1], norm2_near, mlp_near)
    fed += [feed(normed2[p], grad_mlp[p], w_up, up_shift, w_down) for p in range(top, mp_count)]
    norm2_part = fold([f[3] for f in fed[top:]])
    norm2_far = swap(norm2_part, "mp", top)
    acts, upins = [f[0] for f in fed], [f[1] for f in fed]
    acts[-1] = after(acts[-1], norm2_part)
    down_halves = outer(place, acts, grad_mlp, low_first)
    grad_down = DpSum(place, [down_halves], low_first)
    upins[-1] = after(upins[-1], *down_halves)
    up_halves = outer(place, normed2, upins, low_second)
    grad_up = DpSum(place, [up_halves], low_second)
    grad_up_bias = functools.reduce(jnp.add, [f[4] for f in fed])
    norm2_far = after(norm2_far, *up_halves)
    grad_stream1, grad_attn, grad_mixed, second_sums = second_back(
        lengths, place, norm2_near, norm2_far, stream1, cotangent, gain2, w_out_all
    )

    grads = exchange(list(grad_mixed))
    out_parts = outer_each(place, mixed, grad_attn, low_first)
    out_near, out_part = fold(out_parts[:top]), fold(out_parts[top:])
    mlp_part = fold([f[2] for f in fed[top:]])
    now = advance([grad_down, grad_up], [grad_attn])
    grads[-1] = after(grads[-1], out_near, out_part, mlp_part, *now)
    out_far = swap(after(out_part, grads[-1]), "mp", top)
    mlp_far = None
    proj, weights, proj_sums, grad_proj = [], [], [], []
    held = list(qkv)
    for start in range(0, heads, 2):
        count = min(2, heads - start)
        rows = slice(start * HD, (start + count) * HD)
        weights.append(w_qkv[:, rows].reshape(3 * count * HD, width))
        part, sums = attend_back(lengths, place, held, grads, attended, logsum, start, count)
        proj.append(part)
        proj_sums.append(sums.reshape(3, count * HD))
        halves = [outer(place, [part], normed1, low_first)]
        if mlp_far is None:
            out_far = after(out_far, part)
            out_sum = add(out_near, out_far)
            if len(halves[0]) > 1 and splits(depth, low_first):
                halves.append([out_sum[: depth // 2], out_sum[depth // 2 :]])
            mlp_far = swap(after(mlp_part, out_far), "mp", top)
        now = advance([grad_down, grad_up, *grad_proj], [part])
        grad_proj.append(DpSum(place, halves, low_first, *now))
        now = now + grad_proj[-1].now()
        held[-1] = after(qkv[-1], *now)
    proj[-1] = after(proj[-1], *now)
    parts, first_sums = project_back(proj, weights, normed1)
    now = advance(grad_proj, [first_sums])
    parts[-1] = after(parts[-1], *now)
    norm1_part = fold(parts[top:])
    norm1_far = swap(norm1_part, "mp", top)
    now = advance([grad_down, grad_up], [norm1_part])
    now = advance(grad_proj, now)
    norm1_near = fold(parts[:top])
    mlp_far = after(mlp_far, first_sums)
    output, output_sums = output_end(
        lengths, place, mlp_near, mlp_far, down_bias[None], stream1, cotangent
    )
    norm1_far = after(norm1_far, output_sums, *now)
    input_grad = input_end(norm1_near, norm1_far, stream0, grad_stream1, ln1_gain[None])
    now = advance([grad_down, grad_up], [input_grad])
    while any(chain.more() for chain in grad_proj):
        now = advance(grad_proj, now)

    grad_down, grad_up = grad_down.done()[0], grad_up.done()[0]
    grad_proj = [chain.done() for chain in grad_proj]
    if len(grad_proj[0]) > 1:
        grad_out_weight = grad_proj[0][1]
    else:
        grad_out_weight = lax.psum(out_sum, "dp").astype(F32)
    grad_qkv = jnp.concatenate([grad[0].reshape(3, -1, width) for grad in grad_proj], axis=1)
    rows = jnp.concatenate([first_sums, second_sums, output_sums, attn_squares], axis=0)
    rows = total(rows, "mp")
    proj_sums = jnp.concatenate(proj_sums, axis=1)
    flat = jnp.concatenate([rows.reshape(-1), grad_up_bias[0], proj_sums[0], proj_sums[2]])
    flat = jnp.pad(flat, (0, -flat.size % 1024))
    flat = total(flat.reshape(-1, 128), "dp").reshape(-1)
    rows = flat[: rows.size].reshape(rows.shape)
    up_sums = flat[rows.size : rows.size + up_bias.shape[0]]
    proj_sums = flat[rows.size + up_bias.shape[0] :][: 2 * depth].reshape(2, depth)
    squares = jnp.stack([jnp.sum(rows[5]), jnp.sum(rows[9]), jnp.sum(rows[6])])
    stats = jnp.sqrt(squares / (rows[8, 0] * width))
    grad_ln1_gain = (rows[1] - ln1_bias.astype(F32) * rows[0]) / ln1_gain.astype(F32)
    return (
        output, input_grad, grad_ln1_gain, rows[0], grad_qkv, proj_sums, grad_out_weight, rows[4],
        rows[2], rows[3], grad_up, up_sums, grad_down, rows[7], stats,
    )


def solution(mesh):
    rows, one = P(("dp", "mp"), None), P()
    placed = (
        rows, rows, P("dp"), P("dp"), one, one, P(None, "mp", None), P(None, "mp"), P("mp", None), one,
        one, one, P(None, "mp"), P("mp"), P("mp", None), one,
    )
    results = (
        rows, rows, one, one, P(None, "mp", None), P(None, "mp"), P("mp", None), one,
        one, one, P(None, "mp"), P("mp"), P("mp", None), one, one,
    )
    return jax.shard_map(per_device, mesh=mesh, in_specs=placed, out_specs=results, check_vma=False)
```

```python
import functools
import math

import jax
import jax.numpy as jnp
import numpy as np
from jax import lax
from jax.experimental import pallas as pl
from jax.experimental.pallas import tpu as pltpu
from jax.sharding import PartitionSpec as P

HD = 64
EPS = 1e-06
MASKED = -1e30
F32 = jnp.float32
BF16 = jnp.bfloat16
NT = (((1,), (1,)), ((), ()))
TN = (((0,), (0,)), ((), ()))
NN = (((1,), (0,)), ((), ()))


def mxu(left, right, dims):
    return lax.dot_general(left, right, dims, preferred_element_type=F32)


def whole(shape):
    return pl.BlockSpec(shape, lambda *_: (0,) * len(shape))


def scalars():
    return pl.BlockSpec(memory_space=pltpu.SMEM)


def call(body, grid, in_specs, out_specs, out_shape, flops, moved, scratch=(), limit=12):
    return pl.pallas_call(
        body,
        grid=grid,
        in_specs=in_specs,
        out_specs=out_specs,
        out_shape=out_shape,
        scratch_shapes=list(scratch),
        compiler_params=pltpu.CompilerParams(
            dimension_semantics=("arbitrary",) * len(grid), vmem_limit_bytes=limit * 1024 * 1024
        ),
        cost_estimate=pl.CostEstimate(
            flops=0, bytes_accessed=0, transcendentals=0
        ),
    )


def like(shape, dtype):
    return jax.ShapeDtypeStruct(shape, dtype)


def item_ends(lengths_ref, item_count):
    ends, total = [], 0
    for item in range(item_count):
        total = total + lengths_ref[item]
        ends.append(total)
    return ends


def segment_of(rows, ends):
    segment = jnp.zeros(rows.shape, jnp.int32)
    for end in ends:
        segment = segment + jnp.where(rows >= end, 1, 0)
    return segment


def scalar_segment(row, ends):
    segment = jnp.int32(0)
    for end in ends:
        segment = segment + jnp.where(row >= end, 1, 0)
    return segment


def valid_column(lengths_ref, item_count, first_row, row_count):
    rows = first_row + lax.broadcasted_iota(jnp.int32, (row_count, 1), 0)
    return jnp.where(rows < item_ends(lengths_ref, item_count)[-1], 1.0, 0.0).astype(F32)


def normalize(stream):
    centred = stream - jnp.mean(stream, axis=1, keepdims=True)
    rstd = lax.rsqrt(jnp.mean(centred * centred, axis=1, keepdims=True) + EPS)
    return centred * rstd, rstd


def norm_back(gradient, scaled, gain, rstd):
    spread = gradient * gain
    first = jnp.mean(spread, axis=1, keepdims=True)
    second = jnp.mean(spread * scaled, axis=1, keepdims=True)
    return rstd * (spread - first - scaled * second)


def column_sum(array):
    return jnp.sum(array, axis=0, keepdims=True)


def sin_cos(angle):
    turns = jnp.floor(angle * (2.0 / math.pi) + 0.5)
    rest = angle - turns * 1.5703125
    rest = rest - turns * 4.837512969970703125e-4
    rest = rest - turns * 7.54978995489188216e-8
    square = rest * rest
    sine = rest + rest * square * (
        -1.6666654611e-1 + square * (8.3321608736e-3 + square * -1.9515295891e-4)
    )
    cosine = (
        1.0
        - 0.5 * square
        + square
        * square
        * (
            4.166664568298827e-2
            + square * (-1.388731625493765e-3 + square * 2.443315711809948e-5)
        )
    )
    quarter = turns.astype(jnp.int32)
    odd = (quarter & 1) == 1
    sine_flip = (quarter & 2) != 0
    cosine_flip = ((quarter + 1) & 2) != 0
    first = jnp.where(odd, cosine, sine)
    second = jnp.where(odd, sine, cosine)
    return jnp.where(sine_flip, -first, first), jnp.where(cosine_flip, -second, second)


def encode_body(item_count, lengths, ratios, place, tokens, freq, gain, bias, stream_out, normed_out):
    rows_here, width = tokens.shape
    row = (
        place[0] * (rows_here * pl.num_programs(0))
        + pl.program_id(0) * rows_here
        + lax.broadcasted_iota(jnp.int32, (rows_here, 1), 0)
    )
    position = jnp.zeros((rows_here, 1), jnp.int32)
    ratio = jnp.zeros((rows_here, 1), F32)
    start = 0
    for item in range(item_count):
        end = start + lengths[item]
        inside = (row >= start) & (row < end)
        position = jnp.where(inside, row - start, position)
        ratio = jnp.where(inside, ratios[item], ratio)
        start = end
    angle = (position.astype(F32) * ratio) * freq[...]
    sine, cosine = sin_cos(angle)
    stream = tokens[...].astype(F32) + jnp.concatenate([sine, cosine], axis=1)
    stream_out[...] = stream
    scaled, _ = normalize(stream)
    normed_out[...] = (scaled * gain[...].astype(F32) + bias[...].astype(F32)).astype(BF16)


def encode(lengths, ratios, place, tokens, gain, bias):
    rows, width = tokens.shape
    half = width // 2
    tile = min(128, rows)
    freq = np.exp(np.arange(half) * (-math.log(10000.0) / half)).astype(np.float32)[None]
    body = functools.partial(encode_body, lengths.shape[0])
    block = pl.BlockSpec((tile, width), lambda i: (i, 0))
    return call(
        body,
        (rows // tile,),
        [scalars(), scalars(), scalars(), block, whole((1, half)), whole((1, width)), whole((1, width))],
        [block, block],
        [like((rows, width), F32), like((rows, width), BF16)],
        60 * rows * width,
        8 * rows * width,
    )(lengths, ratios, place, tokens, freq, gain, bias)


def mask_body(item_count, lengths, place, cotangent, out):
    rows = cotangent.shape[0]
    valid = valid_column(lengths, item_count, place[0] * rows, rows)
    out[...] = (valid * cotangent[...].astype(F32)).astype(BF16)


def mask_rows(lengths, place, cotangent):
    return call(
        functools.partial(mask_body, lengths.shape[0]),
        (1,),
        [scalars(), scalars(), whole(cotangent.shape)],
        whole(cotangent.shape),
        like(cotangent.shape, BF16),
        2 * cotangent.size,
        4 * cotangent.size,
    )(lengths, place, cotangent)


def local_tile(tile, tile_rows, own_rows, place):
    return tile ^ ((place * own_rows) // tile_rows)


def first_and_last(tile, tile_rows, other_rows, ends):
    low = scalar_segment(tile * tile_rows, ends)
    high = scalar_segment(tile * tile_rows + tile_rows - 1, ends)
    start, stop = jnp.int32(0), jnp.int32(0)
    for item, end in enumerate(ends):
        start = jnp.where(low > item, end, start)
        stop = jnp.where(high >= item, end, stop)
    return start // other_rows, (stop - 1) // other_rows


def used_tiles(tile_rows, ends):
    return (ends[-1] + tile_rows - 1) // tile_rows


def head_lanes(count):
    lane = lax.broadcasted_iota(jnp.int32, (1, 2 * HD), 1)
    return [jnp.where(lane // HD == k, 1.0, 0.0) for k in range(count)]


def marks(tile, tile_rows, own_rows, place, ends):
    rows = tile * tile_rows + lax.broadcasted_iota(jnp.int32, (tile_rows, 2 * HD), 0)
    lane = lax.broadcasted_iota(jnp.int32, (tile_rows, 2 * HD), 1) % HD
    same = segment_of(rows ^ (place * own_rows), ends) == lane
    query_marks = jnp.where(same, 1.0, 0.0)
    key_marks = jnp.where(same | (lane > len(ends)), 0.0, MASKED)
    return query_marks, key_marks


class Rows:
    def __init__(self, tile_rows, own_rows):
        self.part = min(tile_rows, own_rows)
        self.tile_rows, self.own_rows = tile_rows, own_rows

    def pair(self, refs, tile, column, count):
        found = []
        for row in range(tile * self.tile_rows, (tile + 1) * self.tile_rows, self.part):
            ref = refs[row // self.own_rows]
            found.append(ref[pl.ds(row % self.own_rows, self.part), column : column + count * HD])
        found = found[0] if len(found) == 1 else jnp.concatenate(found, axis=0)
        if count == 1:
            found = jnp.concatenate([found, jnp.zeros_like(found)], axis=1)
        return found


def attend_body(item_count, heads, tile_q, tile, piece_count, lengths, place_ref, *refs):
    pieces = refs[:piece_count]
    out, lse_out = refs[piece_count : piece_count + 2]
    qa, ka, vt, acc, top = refs[piece_count + 2 :]
    own_rows = pieces[0].shape[0]
    tiles = own_rows * piece_count // tile
    ratio = tile_q // tile
    width = heads * HD
    place = place_ref[0]
    ends = item_ends(lengths, item_count)
    rows = Rows(tile, own_rows)
    lanes = head_lanes(2)
    for t in range(tiles):
        query_marks, key_marks = marks(t, tile, own_rows, place, ends)
        here = slice(t % ratio * tile, (t % ratio + 1) * tile)
        for h in range(0, heads, 2):
            count = min(2, heads - h)
            query = rows.pair(pieces, t, h * HD, count)
            key = rows.pair(pieces, t, width + h * HD, count)
            value = rows.pair(pieces, t, 2 * width + h * HD, count).T
            for k in range(count):
                mine, other = lanes[k], lanes[1 - k]
                scale = (mine * HD**-0.5).astype(BF16)
                qa[h + k, t // ratio, here] = query * scale + (query_marks * other).astype(BF16)
                ka[h + k, t] = key * mine.astype(BF16) + (key_marks * other).astype(BF16)
                vt[h + k, t, :HD] = value[k * HD : (k + 1) * HD]
                vt[h + k, t, HD:] = jnp.ones((vt.shape[2] - HD, tile), BF16)

    def query_tile(tile_index, carry):
        i = local_tile(tile_index, tile_q, own_rows, place)
        first, last = first_and_last(tile_index, tile_q, tile, ends)
        acc[...] = jnp.zeros(acc.shape, F32)
        top[...] = jnp.full(top.shape, -3e38, F32)

        def key_tile(other_index, inner):
            j = local_tile(other_index, tile, own_rows, place)
            scores = [mxu(ka[h, j], qa[h, i], NT) for h in range(heads)]
            old = [top[h] for h in range(heads)]
            new = [jnp.maximum(old[h], jnp.max(scores[h], axis=0, keepdims=True)) for h in range(heads)]
            probs = [jnp.exp(scores[h] - new[h]).astype(BF16) for h in range(heads)]
            mixed = [mxu(vt[h, j], probs[h], NN) for h in range(heads)]
            for h in range(heads):
                top[h] = new[h]
                acc[h] = acc[h] * jnp.exp(old[h] - new[h]) + mixed[h]
            return inner

        lax.fori_loop(first, last + 1, key_tile, 0)
        here = pl.ds(pl.multiple_of(i * tile_q, tile_q), tile_q)
        for h in range(0, heads, 2):
            count = min(2, heads - h)
            mixed = []
            for k in range(count):
                total = acc[h + k, HD : HD + 1, :]
                lse = top[h + k] + jnp.log(total)
                for s in range(ratio):
                    lse_out[h + k, i * ratio + s] = lse[:, s * tile : (s + 1) * tile]
                mixed.append(acc[h + k, :HD, :] / total)
            mixed = jnp.concatenate(mixed, axis=0) if count > 1 else mixed[0]
            out[here, h * HD : (h + count) * HD] = mixed.T.astype(BF16)
        return carry

    def unused_tile(tile_index, carry):
        i = local_tile(tile_index, tile_q, own_rows, place)
        for s in range(ratio):
            lse_out[:, i * ratio + s] = jnp.zeros((heads, 1, tile), F32)
        out[pl.ds(pl.multiple_of(i * tile_q, tile_q), tile_q), :] = jnp.zeros((tile_q, width), BF16)
        return carry

    used = used_tiles(tile_q, ends)
    lax.fori_loop(0, used, query_tile, 0)
    lax.fori_loop(used, tiles // ratio, unused_tile, 0)


def attend(lengths, place, pieces):
    own_rows, width3 = pieces[0].shape
    width = width3 // 3
    heads = width // HD
    rows = own_rows * len(pieces)
    tile = min(256, rows)
    tile_q = min(512, rows)
    tiles = rows // tile
    body = functools.partial(attend_body, lengths.shape[0], heads, tile_q, tile, len(pieces))
    return call(
        body,
        (1,),
        [scalars(), scalars()] + [whole((own_rows, width3))] * len(pieces),
        [whole((rows, width)), whole((heads, tiles, 1, tile))],
        [like((rows, width), BF16), like((heads, tiles, 1, tile), F32)],
        rows * rows * width * 2,
        10 * rows * width,
        [
            pltpu.VMEM((heads, rows // tile_q, tile_q, 2 * HD), BF16),
            pltpu.VMEM((heads, tiles, tile, 2 * HD), BF16),
            pltpu.VMEM((heads, tiles, HD + 16, tile), BF16),
            pltpu.VMEM((heads, HD + 16, tile_q), F32),
            pltpu.VMEM((heads, 1, tile_q), F32),
        ],
        limit=20,
    )(lengths, place, *pieces)


def attend_back_body(item_count, start, heads, tile, piece_count, lengths, place_ref, *refs):
    pieces = refs[:piece_count]
    grads = refs[piece_count : 2 * piece_count]
    mixed, lse, out, sums = refs[2 * piece_count : 2 * piece_count + 4]
    qa, qm, ka, kt, vals, dos, delta, dk, dv, dqt = refs[2 * piece_count + 4 :]
    own_rows = pieces[0].shape[0]
    tiles = own_rows * piece_count // tile
    width = heads * HD
    full = pieces[0].shape[1] // 3
    base = start * HD
    place = place_ref[0]
    ends = item_ends(lengths, item_count)
    rows = Rows(tile, own_rows)
    lanes = head_lanes(2)
    scale = HD**-0.5
    for t in range(tiles):
        query_marks, key_marks = marks(t, tile, own_rows, place, ends)
        for h in range(0, heads, 2):
            count = min(2, heads - h)
            column = base + h * HD
            query = rows.pair(pieces, t, column, count)
            key = rows.pair(pieces, t, full + column, count)
            grad = rows.pair(grads, t, column, count)
            came = mixed[t * tile : (t + 1) * tile, column : column + count * HD].astype(F32)
            if count == 1:
                came = jnp.concatenate([came, jnp.zeros_like(came)], axis=1)
            weighed = (grad.astype(F32) * came).T
            turned = key.T
            vals[h // 2, t] = rows.pair(pieces, t, 2 * full + column, count)
            for k in range(count):
                mine, other = lanes[k], lanes[1 - k]
                alone = query * (mine * scale).astype(BF16)
                qm[h + k, t] = alone
                qa[h + k, t] = alone + (query_marks * other).astype(BF16)
                ka[h + k, t] = key * mine.astype(BF16) + (key_marks * other).astype(BF16)
                dos[h + k, t] = grad * mine.astype(BF16)
                kt[h + k, t] = turned[k * HD : (k + 1) * HD]
                delta[h + k, t] = column_sum(weighed[k * HD : (k + 1) * HD])
    dqt[...] = jnp.zeros(dqt.shape, F32)

    def key_tile(tile_index, carry):
        j = local_tile(tile_index, tile, own_rows, place)
        first, last = first_and_last(tile_index, tile, tile, ends)
        dk[...] = jnp.zeros(dk.shape, F32)
        dv[...] = jnp.zeros(dv.shape, F32)

        def query_tile(other_index, inner):
            i = local_tile(other_index, tile, own_rows, place)
            scores = [mxu(ka[h, j], qa[h, i], NT) for h in range(heads)]
            grad_probs = [mxu(vals[h // 2, j], dos[h, i], NT) for h in range(heads)]
            for h in range(heads):
                probs = jnp.exp(scores[h] - lse[start + h, i])
                grad_scores = (probs * (grad_probs[h] - delta[h, i])).astype(BF16)
                dv[h] += mxu(probs.astype(BF16), dos[h, i], NN)
                dk[h] += mxu(grad_scores, qm[h, i], NN)
                dqt[h, i] += mxu(kt[h, j], grad_scores, NN)
            return inner

        lax.fori_loop(first, last + 1, query_tile, 0)
        here = pl.ds(pl.multiple_of(j * tile, tile), tile)
        for h in range(0, heads, 2):
            count = min(2, heads - h)
            first = width + h * HD
            for kept, column in ((dk, first), (dv, width + first)):
                both = kept[h] + kept[h + 1] if count > 1 else kept[h]
                out[here, column : column + count * HD] = both[:, : count * HD].astype(BF16)
        return carry

    def unused_tile(tile_index, carry):
        j = local_tile(tile_index, tile, own_rows, place)
        here = pl.ds(pl.multiple_of(j * tile, tile), tile)
        out[here, width:] = jnp.zeros((tile, 2 * width), BF16)
        return carry

    used = used_tiles(tile, ends)
    lax.fori_loop(0, used, key_tile, 0)
    lax.fori_loop(used, tiles, unused_tile, 0)
    for t in range(tiles):
        for h in range(0, heads, 2):
            count = min(2, heads - h)
            both = [dqt[h + k, t] for k in range(count)]
            both = jnp.concatenate(both, axis=0) if count > 1 else both[0]
            out[t * tile : (t + 1) * tile, h * HD : (h + count) * HD] = (both.T * scale).astype(BF16)
    sums[...] = column_sum(out[...].astype(F32))


def attend_back(lengths, place, pieces, grads, mixed, lse, start, heads):
    own_rows = pieces[0].shape[0]
    width = heads * HD
    pairs = (heads + 1) // 2
    rows = own_rows * len(pieces)
    tile = min(256, rows)
    tiles = rows // tile
    body = functools.partial(attend_back_body, lengths.shape[0], start, heads, tile, len(pieces))
    return call(
        body,
        (1,),
        [scalars(), scalars()]
        + [whole(piece.shape) for piece in pieces]
        + [whole(grad.shape) for grad in grads]
        + [whole(mixed.shape), whole(lse.shape)],
        [whole((rows, 3 * width)), whole((1, 3 * width))],
        [like((rows, 3 * width), BF16), like((1, 3 * width), F32)],
        rows * rows * width * 5,
        16 * rows * width,
        [
            pltpu.VMEM((heads, tiles, tile, 2 * HD), BF16),
            pltpu.VMEM((heads, tiles, tile, 2 * HD), BF16),
            pltpu.VMEM((heads, tiles, tile, 2 * HD), BF16),
            pltpu.VMEM((heads, tiles, HD, tile), BF16),
            pltpu.VMEM((pairs, tiles, tile, 2 * HD), BF16),
            pltpu.VMEM((heads, tiles, tile, 2 * HD), BF16),
            pltpu.VMEM((heads, tiles, 1, tile), F32),
            pltpu.VMEM((heads, tile, 2 * HD), F32),
            pltpu.VMEM((heads, tile, 2 * HD), F32),
            pltpu.VMEM((heads, tiles, HD, tile), F32),
        ],
        limit=20,
    )(lengths, place, *pieces, *grads, mixed, lse)


def branch_body(item_count, piece_count, lengths, place, *refs):
    mixed = refs[:piece_count]
    weights = refs[piece_count : 2 * piece_count]
    stream0, shift, gain, bias, stream1, normed, squares = refs[2 * piece_count :]
    tile = stream0.shape[0]
    attn = shift[...]
    for left, right in zip(mixed, weights):
        attn = attn + mxu(left[...], right[...], NN)
    first = place[0] * (tile * pl.num_programs(0)) + pl.program_id(0) * tile
    valid = valid_column(lengths, item_count, first, tile)
    stream = stream0[...] + attn
    stream1[...] = stream
    scaled, _ = normalize(stream)
    normed[...] = (scaled * gain[...] + bias[...]).astype(BF16)

    @pl.when(pl.program_id(0) == 0)
    def _():
        squares[...] = jnp.zeros(squares.shape, F32)

    squares[...] += column_sum(valid * attn * attn)


def branch(lengths, place, mixed, weights, stream0, shift, gain, bias):
    rows, width = stream0.shape
    tile = min(256, rows)
    count = len(mixed)
    block = pl.BlockSpec((tile, width), lambda i: (i, 0))
    narrow = pl.BlockSpec((tile, mixed[0].shape[1]), lambda i: (i, 0))
    line = whole((1, width))
    return call(
        functools.partial(branch_body, lengths.shape[0], count),
        (rows // tile,),
        [scalars(), scalars()]
        + [narrow] * count
        + [whole(weights[0].shape)] * count
        + [block, line, line, line],
        [block, block, line],
        [like((rows, width), F32), like((rows, width), BF16), like((1, width), F32)],
        2 * rows * width * width,
        rows * width * 12 + 2 * width * width,
    )(lengths, place, *mixed, *weights, stream0, shift, gain, bias)


def feed_body(normed, grad_mlp, w_up, up_bias, w_down, act_out, upin_out, mlp_out, norm_out, bias_out):
    hidden = w_up.shape[1]
    chunk = min(512, hidden)
    left, grad = normed[...], grad_mlp[...]
    mlp = norm = None

    @pl.when(pl.program_id(0) == 0)
    def _():
        bias_out[...] = jnp.zeros(bias_out.shape, F32)

    for c in range(0, hidden, chunk):
        here = slice(c, c + chunk)
        up = mxu(left, w_up[:, here], NN) + up_bias[:, here]
        grad_act = mxu(grad, w_down[here, :], NT)
        size = jnp.abs(up)
        decay = jnp.exp(-0.5 * up * up)
        t = 1.0 / (1.0 + (0.3275911 * 0.7071067811865476) * size)
        series = t * (
            0.254829592
            + t * (-0.284496736 + t * (1.421413741 + t * (-1.453152027 + t * 1.061405429)))
        )
        tail = 0.5 * series * decay
        share = jnp.where(up >= 0.0, 1.0 - tail, tail)
        act = (up * share).astype(BF16)
        upin = ((share + up * decay * 0.3989422804014327) * grad_act).astype(BF16)
        act_out[:, here] = act
        upin_out[:, here] = upin
        bias_out[:, here] += column_sum(upin.astype(F32))
        mlp_part = mxu(act, w_down[here, :], NN)
        norm_part = mxu(upin, w_up[:, here], NT)
        mlp = mlp_part if mlp is None else mlp + mlp_part
        norm = norm_part if norm is None else norm + norm_part
    mlp_out[...] = mlp.astype(BF16)
    norm_out[...] = norm.astype(BF16)


def feed(normed, grad_mlp, w_up, up_bias, w_down):
    rows, width = normed.shape
    hidden = w_up.shape[1]
    tile = min(512, rows)
    block = pl.BlockSpec((tile, width), lambda i: (i, 0))
    wide = pl.BlockSpec((tile, hidden), lambda i: (i, 0))
    return call(
        feed_body,
        (rows // tile,),
        [block, block, whole(w_up.shape), whole((1, hidden)), whole(w_down.shape)],
        [wide, wide, block, block, whole((1, hidden))],
        [
            like((rows, hidden), BF16),
            like((rows, hidden), BF16),
            like((rows, width), BF16),
            like((rows, width), BF16),
            like((1, hidden), F32),
        ],
        8 * rows * width * hidden,
        12 * rows * width + 4 * width * hidden,
        limit=24,
    )(normed, grad_mlp, w_up, up_bias, w_down)


def splits(rows, bits):
    return bits and rows % (16 * 2 ** len(bits)) == 0


def position(ordinal, here, bits):
    number = sum(bit for k, bit in enumerate(bits) if ordinal >> k & 1)
    found, step = 0, 2 ** len(bits) // 2
    for bit in bits:
        found = found + jnp.where((number ^ here) & bit != 0, step, 0)
        step //= 2
    return found


def put(value, first_row, bits, here, kept, sent):
    if sent is None:
        kept[first_row : first_row + value.shape[0]] = value
        return
    half = kept.shape[0]
    size = 2 * half // 2 ** len(bits)
    step = math.gcd(size, value.shape[0])
    for row in range(first_row, first_row + value.shape[0], step):
        spot = position(row // size, here, bits) * size + row % size
        part = value[row - first_row : row - first_row + step]

        @pl.when(spot < half)
        def _():
            kept[pl.ds(pl.multiple_of(spot, 16), step)] = part

        @pl.when(spot >= half)
        def _():
            sent[pl.ds(pl.multiple_of(spot - half, 16), step)] = part


def outer_body(groups, tile, count, based, place, *refs):
    pairs = sum(len(halves) for _, _, halves in groups)
    base, refs = refs[:based], refs[based:]
    left, right, outs = refs[: -count - pairs], refs[-count - pairs : -pairs], list(refs[-pairs:])
    for start, bits, halves in groups:
        kept = outs.pop(0)
        sent = outs.pop(0) if len(halves) > 1 else None
        rows = sum(halves)
        step = tile if rows % tile == 0 else rows
        for first in range(0, rows, step):
            total = base[0][start + first : start + first + step] if base else None
            for p in range(count):
                if len(left) == count:
                    a = left[p][:, start + first : start + first + step]
                else:
                    size = right[0].shape[0]
                    a = left[0][p * size : (p + 1) * size, start + first : start + first + step]
                term = mxu(a, right[p][...], TN)
                total = term if total is None else total + term
            put(total.astype(kept.dtype), first, bits, place[1], kept, sent)


def outer(place, left, right, groups, base=(), dtype=BF16):
    rows, width = right[0].shape
    count = len(right)
    found, start = [], 0
    for size, bits in groups:
        halves = [size // 2] * 2 if splits(size, bits) else [size]
        found.append((start, bits, halves))
        start += size
    outs = [rows_out for _, _, halves in found for rows_out in halves]
    results = call(
        functools.partial(outer_body, found, 256, count, len(base)),
        (1,),
        [scalars()] + [whole(a.shape) for a in (*base, *left)] + [whole((rows, width))] * count,
        [whole((rows_out, width)) for rows_out in outs],
        [like((rows_out, width), dtype) for rows_out in outs],
        0,
        0,
        limit=24,
    )(place, *base, *left, *right)
    results = list(results)
    return [[results.pop(0) for _ in halves] for _, _, halves in found]


def each_body(bits, count, place, *refs):
    for left, out in zip(refs[:count], refs[count + 1 :]):
        value = mxu(left[...], refs[count][...], TN).astype(BF16)
        depth = value.shape[0]
        if splits(depth, bits):
            put(value, 0, bits, place[1], out.at[: depth // 2], out.at[depth // 2 :])
        else:
            out[...] = value


def outer_each(place, left, right, bits):
    rows, depth = left[0].shape
    width = right.shape[1]
    count = len(left)
    return call(
        functools.partial(each_body, bits, count),
        (1,),
        [scalars()] + [whole((rows, depth))] * count + [whole((rows, width))],
        [whole((depth, width))] * count,
        [like((depth, width), BF16)] * count,
        2 * count * rows * depth * width,
        2 * (count * rows * depth + rows * width + count * depth * width),
    )(place, *left, right)


def unpack_body(bits, sections, place, first, second, *outs):
    half, shares = first.shape[0], 2 ** len(bits)
    size = 2 * half // shares
    for block in range(shares):
        spot = position(block, place[1], bits) * size
        offset = 0
        for out, rows in zip(outs, sections):
            count = rows // shares
            start = spot + offset
            low = pl.ds(pl.multiple_of(jnp.minimum(start, half - count), 16), count)
            high = pl.ds(pl.multiple_of(jnp.maximum(start - half, 0), 16), count)
            part = jnp.where(spot < half, first[low], second[high])
            out[block * count : (block + 1) * count] = part.astype(out.dtype)
            offset += count


def unpack(place, first, second, bits, sections, dtype=F32):
    half, width = first.shape
    return call(
        functools.partial(unpack_body, bits, sections),
        (1,),
        [scalars(), whole(first.shape), whole(second.shape)],
        [whole((rows, width)) for rows in sections],
        [like((rows, width), dtype) for rows in sections],
        2 * half * width,
        12 * half * width,
    )(place, first, second)


def project_body(group_count, piece_count, *refs):
    grads = refs[:group_count]
    weights = refs[group_count : 2 * group_count]
    normed = refs[2 * group_count : 2 * group_count + piece_count]
    outs = refs[2 * group_count + piece_count : -1]
    sums = refs[-1]
    size = normed[0].shape[0]
    plain = weighed = 0.0
    for p in range(piece_count):
        total = None
        for grad, weight in zip(grads, weights):
            term = mxu(grad[p * size : (p + 1) * size], weight[...], NN)
            total = term if total is None else total + term
        outs[p][...] = total.astype(BF16)
        plain = plain + column_sum(total)
        weighed = weighed + column_sum(total * normed[p][...].astype(F32))
    sums[0:1] = plain
    sums[1:2] = weighed


def project_back(grads, weights, normed):
    size, width = normed[0].shape
    depth = sum(w.shape[0] for w in weights)
    count = len(normed)
    results = call(
        functools.partial(project_body, len(grads), count),
        (1,),
        [whole(g.shape) for g in grads] + [whole(w.shape) for w in weights] + [whole((size, width))] * count,
        [whole((size, width))] * count + [whole((8, width))],
        [like((size, width), BF16)] * count + [like((8, width), F32)],
        2 * count * size * depth * width,
        2 * count * size * (depth + 2 * width) + 2 * depth * width,
        limit=20,
    )(*grads, *weights, *normed)
    return list(results[:-1]), results[-1][:2]


def second_back_body(item_count, piece_count, lengths, place, half_a, half_b, stream1, cotangent, gain, *refs):
    weights = refs[:piece_count]
    grad_out, attn_out = refs[piece_count : piece_count + 2]
    mixed_out = refs[piece_count + 2 : 2 * piece_count + 2]
    sums = refs[-1]
    tile = stream1.shape[0]
    first = place[0] * (tile * pl.num_programs(0)) + pl.program_id(0) * tile
    valid = valid_column(lengths, item_count, first, tile)
    grad_norm = half_a[...].astype(F32) + half_b[...].astype(F32)
    scaled, rstd = normalize(stream1[...])
    grad = valid * cotangent[...].astype(F32) + norm_back(grad_norm, scaled, gain[...], rstd)
    grad_out[...] = grad
    rounded = grad.astype(BF16)
    attn_out[...] = rounded

    @pl.when(pl.program_id(0) == 0)
    def _():
        sums[...] = jnp.zeros(sums.shape, F32)

    sums[0:1] += column_sum(grad_norm * scaled)
    sums[1:2] += column_sum(grad_norm)
    sums[2:3] += column_sum(rounded.astype(F32))
    for weight, mixed in zip(weights, mixed_out):
        mixed[...] = mxu(rounded, weight[...], NT).astype(BF16)


def second_back(lengths, place, half_a, half_b, stream1, cotangent, gain, weights):
    rows, width = stream1.shape
    tile = min(256, rows)
    count = len(weights)
    depth = weights[0].shape[0]
    block = pl.BlockSpec((tile, width), lambda i: (i, 0))
    narrow = pl.BlockSpec((tile, depth), lambda i: (i, 0))
    results = call(
        functools.partial(second_back_body, lengths.shape[0], count),
        (rows // tile,),
        [scalars(), scalars(), block, block, block, block, whole((1, width))]
        + [whole(weights[0].shape)] * count,
        [block, block] + [narrow] * count + [whole((8, width))],
        [like((rows, width), F32), like((rows, width), BF16)]
        + [like((rows, depth), BF16)] * count
        + [like((8, width), F32)],
        2 * rows * width * width,
        rows * width * 20 + 2 * width * width,
    )(lengths, place, half_a, half_b, stream1, cotangent, gain, *weights)
    return results[0], results[1], results[2:-1], results[-1][:3]


def output_body(item_count, lengths, place, half_a, half_b, shift, stream1, cotangent, out, sums):
    tile = stream1.shape[0]
    first = place[0] * (tile * pl.num_programs(0)) + pl.program_id(0) * tile
    valid = valid_column(lengths, item_count, first, tile)
    mlp = half_a[...].astype(F32) + half_b[...].astype(F32) + shift[...]
    stream2 = stream1[...] + mlp
    out[...] = (valid * stream2).astype(BF16)

    @pl.when(pl.program_id(0) == 0)
    def _():
        sums[...] = jnp.zeros(sums.shape, F32)

    sums[0:1] += column_sum(valid * stream2 * stream2)
    sums[1:2] += column_sum(valid * mlp * mlp)
    sums[2:3] += column_sum((valid * cotangent[...].astype(F32)).astype(BF16).astype(F32))
    sums[3:4] += jnp.broadcast_to(column_sum(valid), (1, stream1.shape[1]))


def output_end(lengths, place, half_a, half_b, shift, stream1, cotangent):
    rows, width = stream1.shape
    tile = min(256, rows)
    block = pl.BlockSpec((tile, width), lambda i: (i, 0))
    out, sums = call(
        functools.partial(output_body, lengths.shape[0]),
        (rows // tile,),
        [scalars(), scalars(), block, block, whole((1, width)), block, block],
        [block, whole((8, width))],
        [like((rows, width), BF16), like((8, width), F32)],
        12 * rows * width,
        rows * width * 12,
    )(lengths, place, half_a, half_b, shift, stream1, cotangent)
    return out, sums[:4]


def input_body(half_a, half_b, stream0, grad_stream1, gain, out):
    grad_norm = half_a[...].astype(F32) + half_b[...].astype(F32)
    scaled, rstd = normalize(stream0[...])
    out[...] = grad_stream1[...] + norm_back(grad_norm, scaled, gain[...].astype(F32), rstd)


def input_end(half_a, half_b, stream0, grad_stream1, gain):
    rows, width = stream0.shape
    tile = min(256, rows)
    block = pl.BlockSpec((tile, width), lambda i: (i, 0))
    return call(
        input_body,
        (rows // tile,),
        [block, block, block, block, whole((1, width))],
        block,
        like((rows, width), F32),
        12 * rows * width,
        rows * width * 16,
    )(half_a, half_b, stream0, grad_stream1, gain)


def swap(array, axis, bit):
    return lax.ppermute(array, axis, [(i, i ^ bit) for i in range(lax.axis_size(axis))])


def after(array, *others):
    return lax.optimization_barrier((array, *others))[0]


def spread(own, top):
    pieces, bit = {0: own}, top // 2
    while bit:
        for p in sorted(pieces):
            pieces[p | bit] = swap(pieces[p], "mp", bit)
        bit //= 2
    return [pieces[p] for p in range(len(pieces))]


def add(left, right):
    return (left.astype(F32) + right.astype(F32)).astype(left.dtype)


def fold(parts, *others):
    bit = 1
    while len(parts) > 1:
        came = [swap(parts[p + 1], "mp", bit) for p in range(0, len(parts), 2)]
        if others:
            came = [after(array, *others) for array in came]
        parts = [add(parts[2 * k], array) for k, array in enumerate(came)]
        bit *= 2
    return parts[0]


def exchange(parts):
    return [parts[0]] + [swap(parts[p], "mp", p) for p in range(1, len(parts))]


def total(array, axis):
    bit = 1
    while bit < lax.axis_size(axis):
        array = array + swap(array, axis, bit)
        bit *= 2
    return array


def own_block(place, weight, bits):
    if not splits(weight.shape[0], bits):
        return weight
    size = weight.shape[0] // 2 ** len(bits)
    return lax.dynamic_slice_in_dim(weight, place[1] * size, size, 0)


def join_blocks(place, kept, rows, bits):
    if kept.shape[0] == rows:
        return kept
    for bit in bits[:0:-1]:
        kept = jnp.concatenate([kept, swap(kept, "dp", bit)], axis=0)
    return unpack(place, kept, swap(kept, "dp", bits[0]), bits, [rows], kept.dtype)[0]


class DpSum:
    def __init__(self, place, parts, bits, *others):
        self.place, self.bits, self.steps = place, bits, 0
        self.sections = [sum(half.shape[0] for half in halves) for halves in parts]
        blocks, width = max(2 ** (len(bits) - 1) // 2, 1), parts[0][0].shape[1]
        halves = [
            jnp.concatenate([half.reshape(blocks, -1, width) for half in group], axis=1).reshape(-1, width)
            for group in zip(*parts)
        ]
        if len(halves) == 1:
            self.kept = lax.psum(halves[0], "dp")
            return
        self.kept, self.sent = halves
        self.came = swap(after(self.sent, *others), "dp", bits[0])

    def step(self, *others):
        if not self.more():
            return
        self.steps += 1
        came, count = after(self.came, *others), len(self.bits)
        if self.steps < count:
            half = came.shape[0] // 2
            self.sent = add(self.kept[half:], came[half:])
            self.kept = add(self.kept[:half], came[:half])
            if self.steps == count - 1:
                self.kept = self.sent = jnp.concatenate([self.kept, self.sent], axis=0)
            self.came = swap(self.sent, "dp", self.bits[self.steps])
        else:
            if self.steps == count:
                self.kept = add(self.kept, came)
            else:
                self.kept = jnp.concatenate([self.kept, came], axis=0)
            self.sent = self.kept
            self.came = swap(self.kept, "dp", self.bits[2 * count - 2 - self.steps])

    def now(self):
        return [self.kept, self.sent] if hasattr(self, "came") else []

    def more(self):
        return hasattr(self, "came") and self.steps < 2 * len(self.bits) - 2

    def done(self, *others):
        if not hasattr(self, "came"):
            return [self.kept.astype(F32)]
        came = after(self.came, *others) if others else self.came
        return unpack(self.place, self.kept, came, self.bits[:-1], self.sections)


def advance(chains, others):
    for chain in chains:
        chain.step(*others)
    return [array for chain in chains for array in chain.now()] or list(others)


def per_device(
    tokens, cotangent, lengths, gsd_ratio, ln1_gain, ln1_bias, w_qkv, qv_bias, w_out, out_bias,
    ln2_gain, ln2_bias, w_up, up_bias, w_down, down_bias,
):
    own_rows, width = tokens.shape
    mp_count, dp_count = lax.axis_size("mp"), lax.axis_size("dp")
    top = mp_count // 2
    low_first = [1 << k for k in range(dp_count.bit_length() - 1)] if dp_count & (dp_count - 1) == 0 else []
    low_second = low_first[1:2] + low_first[:1] + low_first[2:]
    low_last = low_first[1:] + low_first[:1]
    place = jnp.stack([lax.axis_index("mp"), lax.axis_index("dp")]).astype(jnp.int32)
    depth = w_qkv.shape[1]
    heads = depth // HD
    gain2, bias2 = ln2_gain[None], ln2_bias[None]
    up_shift = up_bias[None]

    w_out_block = swap(own_block(place, w_out, low_first), "mp", top)
    grad_mlp_own = mask_rows(lengths, place, cotangent)
    early = own_rows // 8
    grad_mlp_far = swap(grad_mlp_own[:early], "mp", top)
    tokens = after(tokens, w_out_block)
    stream0, normed1_own = encode(lengths, gsd_ratio, place, tokens, ln1_gain[None], ln1_bias[None])
    normed1_far = swap(after(normed1_own, grad_mlp_far), "mp", top)
    w_out_far = join_blocks(place, w_out_block, depth, low_first)
    normed1 = spread(normed1_own, top)
    w_flat = w_qkv.reshape(3 * depth, width)
    shift = jnp.concatenate([qv_bias[0], jnp.zeros((depth,), F32), qv_bias[1]])[None]

    def project(piece):
        return (mxu(piece, w_flat, NT) + shift).astype(BF16)

    qkv = [project(piece) for piece in normed1]
    grad_mlp = spread(grad_mlp_own, top)
    w_out_all = spread(w_out, top)
    normed1_far = after(normed1_far, w_out_far, *qkv, *grad_mlp, *w_out_all)
    grad_mlp_late = swap(after(grad_mlp_own[early:], normed1_far), "mp", top)
    normed1 += spread(normed1_far, top)
    w_out_all += spread(w_out_far, top)
    qkv += [project(piece) for piece in normed1[top:]]

    attended, logsum = attend(lengths, place, qkv)
    attended, grad_mlp_late = lax.optimization_barrier((attended, grad_mlp_late))
    grad_mlp_far = jnp.concatenate([grad_mlp_far, grad_mlp_late], axis=0)
    mixed = exchange([attended[p * own_rows : (p + 1) * own_rows] for p in range(mp_count)])
    grad_mlp += spread(grad_mlp_far, top)
    mixed[0] = after(mixed[0], *grad_mlp)
    stream1, normed2_own, attn_squares = branch(
        lengths, place, mixed, w_out_all, stream0, out_bias[None], gain2, bias2
    )

    normed2_far = swap(normed2_own, "mp", top)
    normed2 = spread(normed2_own, top)
    fed = [feed(normed2[p], grad_mlp[p], w_up, up_shift, w_down) for p in range(top)]
    [[down_base]] = outer(place, [f[0] for f in fed], grad_mlp[:top], [(w_down.shape[0], [])], dtype=F32)
    [[up_base]] = outer(place, normed2, [f[1] for f in fed], [(width, [])], dtype=F32)
    far_normed = spread(after(normed2_far, down_base, up_base), top)
    norm2_near, mlp_near = fold([f[3] for f in fed]), fold([f[2] for f in fed])
    far_normed[-1] = after(far_normed[-1], norm2_near, mlp_near)
    right = grad_mlp[top:]
    far_fed = [feed(n, g, w_up, up_shift, w_down) for n, g in zip(far_normed, right)]
    norm2_part = fold([f[3] for f in far_fed])
    norm2_far = swap(norm2_part, "mp", top)
    acts, upins = [f[0] for f in far_fed], [f[1] for f in far_fed]
    acts[-1] = after(acts[-1], norm2_part)
    [down_halves] = outer(place, acts, right, [(w_down.shape[0], low_first[:-1])], [down_base])
    grad_down = DpSum(place, [down_halves], low_first)
    upins[-1] = after(upins[-1], *down_halves)
    [up_halves] = outer(place, far_normed, upins, [(width, low_last[:-1])], [up_base])
    grad_up = DpSum(place, [up_halves], low_last)
    grad_up_bias = functools.reduce(jnp.add, [f[4] for f in fed + far_fed])
    norm2_far = after(norm2_far, *up_halves)
    grad_stream1, grad_attn, grad_mixed, second_sums = second_back(
        lengths, place, norm2_near, norm2_far, stream1, cotangent, gain2, w_out_all
    )

    grads = exchange(list(grad_mixed))
    out_parts = outer_each(place, mixed, grad_attn, low_first[:-1])
    out_near, out_part = fold(out_parts[:top]), fold(out_parts[top:])
    mlp_part = fold([f[2] for f in far_fed])
    now = advance([grad_down, grad_up], grads)
    grads[-1] = after(grads[-1], out_near, out_part, mlp_part, *now)
    out_far = swap(after(out_part, grads[-1]), "mp", top)
    mlp_far = swap(after(mlp_part, grads[-1]), "mp", top)
    proj, proj_sums = attend_back(lengths, place, qkv, grads, attended, logsum, 0, heads)
    now = advance([grad_down, grad_up], [proj])
    qkv_rows = 3 * depth // 2
    halves_a, halves_b = outer(
        place, [after(proj, *now)], normed1, [(qkv_rows, low_first[:-1]), (qkv_rows, low_second[:-1])]
    )
    out_far = after(out_far, *halves_a)
    out_sum = add(out_near, out_far)
    groups_a = [halves_a]
    if len(halves_a) > 1 and splits(depth, low_first[:-1]):
        groups_a.append([out_sum[: depth // 2], out_sum[depth // 2 :]])
    grad_a, grad_b = DpSum(place, groups_a, low_first), DpSum(place, [halves_b], low_second)
    main, proj_chains = [grad_down, grad_up], [grad_a, grad_b]
    now = [*now, *grad_a.now(), *grad_b.now()]
    parts, first_sums = project_back([after(proj, *now)], [w_flat], normed1)
    chains = main + proj_chains
    mp_hops = [1 << k for k in range(mp_count.bit_length() - 1)]
    dp_hops = [low_first[0], *low_first[:0:-1]] if low_first else []

    def hop(array, axis, hops, *others):
        return array + after(swap(array, axis, hops.pop(0)), *others) if hops else array

    norm1_part, norm1_near = fold(parts[top:], first_sums), fold(parts[:top], first_sums)
    now = advance(chains, [first_sums])

    norm1_far = swap(norm1_part, "mp", top)
    output, output_sums = output_end(
        lengths, place, after(mlp_near, *now), mlp_far, down_bias[None], stream1, cotangent
    )
    rows = jnp.concatenate([first_sums, second_sums, output_sums, attn_squares], axis=0)
    while len(mp_hops) > 1:
        rows = hop(rows, "mp", mp_hops, output_sums)
    flat = jnp.concatenate([grad_up_bias[0], proj_sums[0, :depth], proj_sums[0, 2 * depth :]])
    flat = jnp.pad(flat, (0, -flat.size % 1024)).reshape(-1, 128)
    flat = jnp.concatenate([rows.reshape(-1, 128), flat], axis=0)
    flat = hop(flat, "dp", dp_hops, norm1_near)
    norm1_far = after(norm1_far, flat)
    now = advance(chains, [flat])

    input_grad = input_end(
        norm1_near, norm1_far, after(stream0, *now), grad_stream1, ln1_gain[None]
    )
    flat = jnp.concatenate(
        [hop(flat[: rows.size // 128], "mp", mp_hops, input_grad), flat[rows.size // 128 :]], axis=0
    )
    now = advance(proj_chains, [input_grad, flat])
    while any(chain.more() for chain in main):
        now = advance(main, now)

    [grad_down], [grad_up] = grad_down.done(*now), grad_up.done(*now)
    while dp_hops or any(chain.more() for chain in proj_chains):
        flat = hop(flat, "dp", dp_hops, grad_down, grad_up)
        now = advance(proj_chains, [grad_down, grad_up, flat])

    grad_a, grad_b = grad_a.done(), grad_b.done()
    grad_out_weight = grad_a[1] if len(grad_a) > 1 else lax.psum(out_sum, "dp").astype(F32)
    grad_qkv = jnp.concatenate([grad_a[0], grad_b[0]], axis=0).reshape(3, depth, width)
    flat = flat.reshape(-1)
    rows = flat[: rows.size].reshape(rows.shape)
    up_sums = flat[rows.size : rows.size + up_bias.shape[0]]
    proj_sums = flat[rows.size + up_bias.shape[0] :][: 2 * depth].reshape(2, depth)
    squares = jnp.stack([jnp.sum(rows[5]), jnp.sum(rows[9]), jnp.sum(rows[6])])
    stats = jnp.sqrt(squares / (rows[8, 0] * width))
    grad_ln1_gain = (rows[1] - ln1_bias.astype(F32) * rows[0]) / ln1_gain.astype(F32)
    return (
        output, input_grad, grad_ln1_gain, rows[0], grad_qkv, proj_sums, grad_out_weight, rows[4],
        rows[2], rows[3], grad_up, up_sums, grad_down, rows[7], stats,
    )


def solution(mesh):
    rows, one = P(("dp", "mp"), None), P()
    placed = (
        rows, rows, P("dp"), P("dp"), one, one, P(None, "mp", None), P(None, "mp"), P("mp", None), one,
        one, one, P(None, "mp"), P("mp"), P("mp", None), one,
    )
    results = (
        rows, rows, one, one, P(None, "mp", None), P(None, "mp"), P("mp", None), one,
        one, one, P(None, "mp"), P("mp"), P("mp", None), one, one,
    )
    return jax.shard_map(per_device, mesh=mesh, in_specs=placed, out_specs=results, check_vma=False)
```

```python
import functools
import math

import jax
import jax.numpy as jnp
import numpy as np
from jax import lax
from jax.experimental import pallas as pl
from jax.experimental.pallas import tpu as pltpu
from jax.sharding import PartitionSpec as P

HD = 64
EPS = 1e-06
MASKED = -1e30
F32 = jnp.float32
BF16 = jnp.bfloat16
NT = (((1,), (1,)), ((), ()))
TN = (((0,), (0,)), ((), ()))
NN = (((1,), (0,)), ((), ()))


def mxu(left, right, dims):
    return lax.dot_general(left, right, dims, preferred_element_type=F32)


def whole(shape):
    return pl.BlockSpec(shape, lambda *_: (0,) * len(shape))


def scalars():
    return pl.BlockSpec(memory_space=pltpu.SMEM)


def call(body, grid, in_specs, out_specs, out_shape, flops, moved, scratch=(), limit=12):
    return pl.pallas_call(
        body,
        grid=grid,
        in_specs=in_specs,
        out_specs=out_specs,
        out_shape=out_shape,
        scratch_shapes=list(scratch),
        compiler_params=pltpu.CompilerParams(
            dimension_semantics=("arbitrary",) * len(grid), vmem_limit_bytes=limit * 1024 * 1024
        ),
        cost_estimate=pl.CostEstimate(
            flops=0, bytes_accessed=0, transcendentals=0
        ),
    )


def like(shape, dtype):
    return jax.ShapeDtypeStruct(shape, dtype)


def item_ends(lengths_ref, item_count):
    ends, total = [], 0
    for item in range(item_count):
        total = total + lengths_ref[item]
        ends.append(total)
    return ends


def segment_of(rows, ends):
    segment = jnp.zeros(rows.shape, jnp.int32)
    for end in ends:
        segment = segment + jnp.where(rows >= end, 1, 0)
    return segment


def scalar_segment(row, ends):
    segment = jnp.int32(0)
    for end in ends:
        segment = segment + jnp.where(row >= end, 1, 0)
    return segment


def valid_column(lengths_ref, item_count, first_row, row_count):
    rows = first_row + lax.broadcasted_iota(jnp.int32, (row_count, 1), 0)
    return jnp.where(rows < item_ends(lengths_ref, item_count)[-1], 1.0, 0.0).astype(F32)


def normalize(stream):
    centred = stream - jnp.mean(stream, axis=1, keepdims=True)
    rstd = lax.rsqrt(jnp.mean(centred * centred, axis=1, keepdims=True) + EPS)
    return centred * rstd, rstd


def norm_back(gradient, scaled, gain, rstd):
    spread = gradient * gain
    first = jnp.mean(spread, axis=1, keepdims=True)
    second = jnp.mean(spread * scaled, axis=1, keepdims=True)
    return rstd * (spread - first - scaled * second)


def column_sum(array):
    return jnp.sum(array, axis=0, keepdims=True)


def sin_cos(angle):
    turns = jnp.floor(angle * (2.0 / math.pi) + 0.5)
    rest = angle - turns * 1.5703125
    rest = rest - turns * 4.837512969970703125e-4
    rest = rest - turns * 7.54978995489188216e-8
    square = rest * rest
    sine = rest + rest * square * (
        -1.6666654611e-1 + square * (8.3321608736e-3 + square * -1.9515295891e-4)
    )
    cosine = (
        1.0
        - 0.5 * square
        + square
        * square
        * (
            4.166664568298827e-2
            + square * (-1.388731625493765e-3 + square * 2.443315711809948e-5)
        )
    )
    quarter = turns.astype(jnp.int32)
    odd = (quarter & 1) == 1
    sine_flip = (quarter & 2) != 0
    cosine_flip = ((quarter + 1) & 2) != 0
    first = jnp.where(odd, cosine, sine)
    second = jnp.where(odd, sine, cosine)
    return jnp.where(sine_flip, -first, first), jnp.where(cosine_flip, -second, second)


def encode_body(item_count, lengths, ratios, place, tokens, freq, gain, bias, stream_out, normed_out):
    rows_here, width = tokens.shape
    row = (
        place[0] * (rows_here * pl.num_programs(0))
        + pl.program_id(0) * rows_here
        + lax.broadcasted_iota(jnp.int32, (rows_here, 1), 0)
    )
    position = jnp.zeros((rows_here, 1), jnp.int32)
    ratio = jnp.zeros((rows_here, 1), F32)
    start = 0
    for item in range(item_count):
        end = start + lengths[item]
        inside = (row >= start) & (row < end)
        position = jnp.where(inside, row - start, position)
        ratio = jnp.where(inside, ratios[item], ratio)
        start = end
    angle = (position.astype(F32) * ratio) * freq[...]
    sine, cosine = sin_cos(angle)
    stream = tokens[...].astype(F32) + jnp.concatenate([sine, cosine], axis=1)
    stream_out[...] = stream
    scaled, _ = normalize(stream)
    normed_out[...] = (scaled * gain[...].astype(F32) + bias[...].astype(F32)).astype(BF16)


def encode(lengths, ratios, place, tokens, gain, bias):
    rows, width = tokens.shape
    half = width // 2
    tile = min(128, rows)
    freq = np.exp(np.arange(half) * (-math.log(10000.0) / half)).astype(np.float32)[None]
    body = functools.partial(encode_body, lengths.shape[0])
    block = pl.BlockSpec((tile, width), lambda i: (i, 0))
    return call(
        body,
        (rows // tile,),
        [scalars(), scalars(), scalars(), block, whole((1, half)), whole((1, width)), whole((1, width))],
        [block, block],
        [like((rows, width), F32), like((rows, width), BF16)],
        60 * rows * width,
        8 * rows * width,
    )(lengths, ratios, place, tokens, freq, gain, bias)


def mask_body(item_count, lengths, place, cotangent, out):
    rows = cotangent.shape[0]
    valid = valid_column(lengths, item_count, place[0] * rows, rows)
    out[...] = (valid * cotangent[...].astype(F32)).astype(BF16)


def mask_rows(lengths, place, cotangent):
    return call(
        functools.partial(mask_body, lengths.shape[0]),
        (1,),
        [scalars(), scalars(), whole(cotangent.shape)],
        whole(cotangent.shape),
        like(cotangent.shape, BF16),
        2 * cotangent.size,
        4 * cotangent.size,
    )(lengths, place, cotangent)


def local_tile(tile, tile_rows, own_rows, place):
    return tile ^ ((place * own_rows) // tile_rows)


def first_and_last(tile, tile_rows, other_rows, ends):
    low = scalar_segment(tile * tile_rows, ends)
    high = scalar_segment(tile * tile_rows + tile_rows - 1, ends)
    start, stop = jnp.int32(0), jnp.int32(0)
    for item, end in enumerate(ends):
        start = jnp.where(low > item, end, start)
        stop = jnp.where(high >= item, end, stop)
    return start // other_rows, (stop - 1) // other_rows


def used_tiles(tile_rows, ends):
    return (ends[-1] + tile_rows - 1) // tile_rows


def head_lanes(count):
    lane = lax.broadcasted_iota(jnp.int32, (1, 2 * HD), 1)
    return [jnp.where(lane // HD == k, 1.0, 0.0) for k in range(count)]


def marks(tile, tile_rows, own_rows, place, ends):
    rows = tile * tile_rows + lax.broadcasted_iota(jnp.int32, (tile_rows, 2 * HD), 0)
    lane = lax.broadcasted_iota(jnp.int32, (tile_rows, 2 * HD), 1) % HD
    same = segment_of(rows ^ (place * own_rows), ends) == lane
    query_marks = jnp.where(same, 1.0, 0.0)
    key_marks = jnp.where(same | (lane > len(ends)), 0.0, MASKED)
    return query_marks, key_marks


class Rows:
    def __init__(self, tile_rows, own_rows):
        self.part = min(tile_rows, own_rows)
        self.tile_rows, self.own_rows = tile_rows, own_rows

    def pair(self, refs, tile, column, count):
        found = []
        for row in range(tile * self.tile_rows, (tile + 1) * self.tile_rows, self.part):
            ref = refs[row // self.own_rows]
            found.append(ref[pl.ds(row % self.own_rows, self.part), column : column + count * HD])
        found = found[0] if len(found) == 1 else jnp.concatenate(found, axis=0)
        if count == 1:
            found = jnp.concatenate([found, jnp.zeros_like(found)], axis=1)
        return found


def attend_body(item_count, heads, tile_q, tile, piece_count, lengths, place_ref, *refs):
    pieces = refs[:piece_count]
    out, lse_out = refs[piece_count : piece_count + 2]
    qa, ka, vt, acc, top = refs[piece_count + 2 :]
    own_rows = pieces[0].shape[0]
    tiles = own_rows * piece_count // tile
    ratio = tile_q // tile
    width = heads * HD
    place = place_ref[0]
    ends = item_ends(lengths, item_count)
    rows = Rows(tile, own_rows)
    lanes = head_lanes(2)
    for t in range(tiles):
        query_marks, key_marks = marks(t, tile, own_rows, place, ends)
        here = slice(t % ratio * tile, (t % ratio + 1) * tile)
        for h in range(0, heads, 2):
            count = min(2, heads - h)
            query = rows.pair(pieces, t, h * HD, count)
            key = rows.pair(pieces, t, width + h * HD, count)
            value = rows.pair(pieces, t, 2 * width + h * HD, count).T
            for k in range(count):
                mine, other = lanes[k], lanes[1 - k]
                scale = (mine * HD**-0.5).astype(BF16)
                qa[h + k, t // ratio, here] = query * scale + (query_marks * other).astype(BF16)
                ka[h + k, t] = key * mine.astype(BF16) + (key_marks * other).astype(BF16)
                vt[h + k, t, :HD] = value[k * HD : (k + 1) * HD]
                vt[h + k, t, HD:] = jnp.ones((vt.shape[2] - HD, tile), BF16)

    def query_tile(tile_index, carry):
        i = local_tile(tile_index, tile_q, own_rows, place)
        first, last = first_and_last(tile_index, tile_q, tile, ends)
        acc[...] = jnp.zeros(acc.shape, F32)
        top[...] = jnp.full(top.shape, -3e38, F32)

        def key_tile(other_index, inner):
            j = local_tile(other_index, tile, own_rows, place)
            scores = [mxu(ka[h, j], qa[h, i], NT) for h in range(heads)]
            old = [top[h] for h in range(heads)]
            new = [jnp.maximum(old[h], jnp.max(scores[h], axis=0, keepdims=True)) for h in range(heads)]
            probs = [jnp.exp(scores[h] - new[h]).astype(BF16) for h in range(heads)]
            mixed = [mxu(vt[h, j], probs[h], NN) for h in range(heads)]
            for h in range(heads):
                top[h] = new[h]
                acc[h] = acc[h] * jnp.exp(old[h] - new[h]) + mixed[h]
            return inner

        lax.fori_loop(first, last + 1, key_tile, 0)
        here = pl.ds(pl.multiple_of(i * tile_q, tile_q), tile_q)
        for h in range(0, heads, 2):
            count = min(2, heads - h)
            mixed = []
            for k in range(count):
                total = acc[h + k, HD : HD + 1, :]
                lse = top[h + k] + jnp.log(total)
                for s in range(ratio):
                    lse_out[h + k, i * ratio + s] = lse[:, s * tile : (s + 1) * tile]
                mixed.append(acc[h + k, :HD, :] / total)
            mixed = jnp.concatenate(mixed, axis=0) if count > 1 else mixed[0]
            out[here, h * HD : (h + count) * HD] = mixed.T.astype(BF16)
        return carry

    def unused_tile(tile_index, carry):
        i = local_tile(tile_index, tile_q, own_rows, place)
        for s in range(ratio):
            lse_out[:, i * ratio + s] = jnp.zeros((heads, 1, tile), F32)
        out[pl.ds(pl.multiple_of(i * tile_q, tile_q), tile_q), :] = jnp.zeros((tile_q, width), BF16)
        return carry

    used = used_tiles(tile_q, ends)
    lax.fori_loop(0, used, query_tile, 0)
    lax.fori_loop(used, tiles // ratio, unused_tile, 0)


def attend(lengths, place, pieces):
    own_rows, width3 = pieces[0].shape
    width = width3 // 3
    heads = width // HD
    rows = own_rows * len(pieces)
    tile = min(256, rows)
    tile_q = min(512, rows)
    tiles = rows // tile
    body = functools.partial(attend_body, lengths.shape[0], heads, tile_q, tile, len(pieces))
    return call(
        body,
        (1,),
        [scalars(), scalars()] + [whole((own_rows, width3))] * len(pieces),
        [whole((rows, width)), whole((heads, tiles, 1, tile))],
        [like((rows, width), BF16), like((heads, tiles, 1, tile), F32)],
        rows * rows * width * 2,
        10 * rows * width,
        [
            pltpu.VMEM((heads, rows // tile_q, tile_q, 2 * HD), BF16),
            pltpu.VMEM((heads, tiles, tile, 2 * HD), BF16),
            pltpu.VMEM((heads, tiles, HD + 16, tile), BF16),
            pltpu.VMEM((heads, HD + 16, tile_q), F32),
            pltpu.VMEM((heads, 1, tile_q), F32),
        ],
        limit=20,
    )(lengths, place, *pieces)


def attend_back_body(item_count, start, heads, tile, piece_count, lengths, place_ref, *refs):
    pieces = refs[:piece_count]
    grads = refs[piece_count : 2 * piece_count]
    mixed, lse, out, sums = refs[2 * piece_count : 2 * piece_count + 4]
    qa, qm, ka, kt, vals, dos, delta, dk, dv, dqt = refs[2 * piece_count + 4 :]
    own_rows = pieces[0].shape[0]
    tiles = own_rows * piece_count // tile
    width = heads * HD
    full = pieces[0].shape[1] // 3
    base = start * HD
    place = place_ref[0]
    ends = item_ends(lengths, item_count)
    rows = Rows(tile, own_rows)
    lanes = head_lanes(2)
    scale = HD**-0.5
    for t in range(tiles):
        query_marks, key_marks = marks(t, tile, own_rows, place, ends)
        for h in range(0, heads, 2):
            count = min(2, heads - h)
            column = base + h * HD
            query = rows.pair(pieces, t, column, count)
            key = rows.pair(pieces, t, full + column, count)
            grad = rows.pair(grads, t, column, count)
            came = mixed[t * tile : (t + 1) * tile, column : column + count * HD].astype(F32)
            if count == 1:
                came = jnp.concatenate([came, jnp.zeros_like(came)], axis=1)
            weighed = (grad.astype(F32) * came).T
            turned = key.T
            vals[h // 2, t] = rows.pair(pieces, t, 2 * full + column, count)
            for k in range(count):
                mine, other = lanes[k], lanes[1 - k]
                alone = query * (mine * scale).astype(BF16)
                qm[h + k, t] = alone
                qa[h + k, t] = alone + (query_marks * other).astype(BF16)
                ka[h + k, t] = key * mine.astype(BF16) + (key_marks * other).astype(BF16)
                dos[h + k, t] = grad * mine.astype(BF16)
                kt[h + k, t] = turned[k * HD : (k + 1) * HD]
                delta[h + k, t] = column_sum(weighed[k * HD : (k + 1) * HD])
    dqt[...] = jnp.zeros(dqt.shape, F32)

    def key_tile(tile_index, carry):
        j = local_tile(tile_index, tile, own_rows, place)
        first, last = first_and_last(tile_index, tile, tile, ends)
        dk[...] = jnp.zeros(dk.shape, F32)
        dv[...] = jnp.zeros(dv.shape, F32)

        def query_tile(other_index, inner):
            i = local_tile(other_index, tile, own_rows, place)
            scores = [mxu(ka[h, j], qa[h, i], NT) for h in range(heads)]
            grad_probs = [mxu(vals[h // 2, j], dos[h, i], NT) for h in range(heads)]
            for h in range(heads):
                probs = jnp.exp(scores[h] - lse[start + h, i])
                grad_scores = (probs * (grad_probs[h] - delta[h, i])).astype(BF16)
                dv[h] += mxu(probs.astype(BF16), dos[h, i], NN)
                dk[h] += mxu(grad_scores, qm[h, i], NN)
                dqt[h, i] += mxu(kt[h, j], grad_scores, NN)
            return inner

        lax.fori_loop(first, last + 1, query_tile, 0)
        here = pl.ds(pl.multiple_of(j * tile, tile), tile)
        for h in range(0, heads, 2):
            count = min(2, heads - h)
            first = width + h * HD
            for kept, column in ((dk, first), (dv, width + first)):
                both = kept[h] + kept[h + 1] if count > 1 else kept[h]
                out[here, column : column + count * HD] = both[:, : count * HD].astype(BF16)
        return carry

    def unused_tile(tile_index, carry):
        j = local_tile(tile_index, tile, own_rows, place)
        here = pl.ds(pl.multiple_of(j * tile, tile), tile)
        out[here, width:] = jnp.zeros((tile, 2 * width), BF16)
        return carry

    used = used_tiles(tile, ends)
    lax.fori_loop(0, used, key_tile, 0)
    lax.fori_loop(used, tiles, unused_tile, 0)
    for t in range(tiles):
        for h in range(0, heads, 2):
            count = min(2, heads - h)
            both = [dqt[h + k, t] for k in range(count)]
            both = jnp.concatenate(both, axis=0) if count > 1 else both[0]
            out[t * tile : (t + 1) * tile, h * HD : (h + count) * HD] = (both.T * scale).astype(BF16)
    sums[...] = column_sum(out[...].astype(F32))


def attend_back(lengths, place, pieces, grads, mixed, lse, start, heads):
    own_rows = pieces[0].shape[0]
    width = heads * HD
    pairs = (heads + 1) // 2
    rows = own_rows * len(pieces)
    tile = min(256, rows)
    tiles = rows // tile
    body = functools.partial(attend_back_body, lengths.shape[0], start, heads, tile, len(pieces))
    return call(
        body,
        (1,),
        [scalars(), scalars()]
        + [whole(piece.shape) for piece in pieces]
        + [whole(grad.shape) for grad in grads]
        + [whole(mixed.shape), whole(lse.shape)],
        [whole((rows, 3 * width)), whole((1, 3 * width))],
        [like((rows, 3 * width), BF16), like((1, 3 * width), F32)],
        rows * rows * width * 5,
        16 * rows * width,
        [
            pltpu.VMEM((heads, tiles, tile, 2 * HD), BF16),
            pltpu.VMEM((heads, tiles, tile, 2 * HD), BF16),
            pltpu.VMEM((heads, tiles, tile, 2 * HD), BF16),
            pltpu.VMEM((heads, tiles, HD, tile), BF16),
            pltpu.VMEM((pairs, tiles, tile, 2 * HD), BF16),
            pltpu.VMEM((heads, tiles, tile, 2 * HD), BF16),
            pltpu.VMEM((heads, tiles, 1, tile), F32),
            pltpu.VMEM((heads, tile, 2 * HD), F32),
            pltpu.VMEM((heads, tile, 2 * HD), F32),
            pltpu.VMEM((heads, tiles, HD, tile), F32),
        ],
        limit=20,
    )(lengths, place, *pieces, *grads, mixed, lse)


def branch_body(item_count, piece_count, lengths, place, *refs):
    mixed = refs[:piece_count]
    weights = refs[piece_count : 2 * piece_count]
    stream0, shift, gain, bias, stream1, normed, squares = refs[2 * piece_count :]
    tile = stream0.shape[0]
    attn = shift[...]
    for left, right in zip(mixed, weights):
        attn = attn + mxu(left[...], right[...], NN)
    first = place[0] * (tile * pl.num_programs(0)) + pl.program_id(0) * tile
    valid = valid_column(lengths, item_count, first, tile)
    stream = stream0[...] + attn
    stream1[...] = stream
    scaled, _ = normalize(stream)
    normed[...] = (scaled * gain[...] + bias[...]).astype(BF16)

    @pl.when(pl.program_id(0) == 0)
    def _():
        squares[...] = jnp.zeros(squares.shape, F32)

    squares[...] += column_sum(valid * attn * attn)


def branch(lengths, place, mixed, weights, stream0, shift, gain, bias):
    rows, width = stream0.shape
    tile = min(256, rows)
    count = len(mixed)
    block = pl.BlockSpec((tile, width), lambda i: (i, 0))
    narrow = pl.BlockSpec((tile, mixed[0].shape[1]), lambda i: (i, 0))
    line = whole((1, width))
    return call(
        functools.partial(branch_body, lengths.shape[0], count),
        (rows // tile,),
        [scalars(), scalars()]
        + [narrow] * count
        + [whole(weights[0].shape)] * count
        + [block, line, line, line],
        [block, block, line],
        [like((rows, width), F32), like((rows, width), BF16), like((1, width), F32)],
        2 * rows * width * width,
        rows * width * 12 + 2 * width * width,
    )(lengths, place, *mixed, *weights, stream0, shift, gain, bias)


def feed_body(normed, grad_mlp, w_up, up_bias, w_down, act_out, upin_out, norm_out, bias_out, *mlp_out):
    hidden = w_up.shape[1]
    chunk = min(512, hidden)
    left, grad = normed[...], grad_mlp[...]
    mlp = norm = None

    @pl.when(pl.program_id(0) == 0)
    def _():
        bias_out[...] = jnp.zeros(bias_out.shape, F32)

    for c in range(0, hidden, chunk):
        here = slice(c, c + chunk)
        up = mxu(left, w_up[:, here], NN) + up_bias[:, here]
        grad_act = mxu(grad, w_down[here, :], NT)
        size = jnp.abs(up)
        decay = jnp.exp(-0.5 * up * up)
        t = 1.0 / (1.0 + (0.3275911 * 0.7071067811865476) * size)
        series = t * (
            0.254829592
            + t * (-0.284496736 + t * (1.421413741 + t * (-1.453152027 + t * 1.061405429)))
        )
        tail = 0.5 * series * decay
        share = jnp.where(up >= 0.0, 1.0 - tail, tail)
        act = (up * share).astype(BF16)
        upin = ((share + up * decay * 0.3989422804014327) * grad_act).astype(BF16)
        act_out[:, here] = act
        upin_out[:, here] = upin
        bias_out[:, here] += column_sum(upin.astype(F32))
        norm_part = mxu(upin, w_up[:, here], NT)
        norm = norm_part if norm is None else norm + norm_part
        if mlp_out:
            mlp_part = mxu(act, w_down[here, :], NN)
            mlp = mlp_part if mlp is None else mlp + mlp_part
    norm_out[...] = norm.astype(BF16)
    if mlp_out:
        mlp_out[0][...] = mlp.astype(BF16)


def feed(normed, grad_mlp, w_up, up_bias, w_down, with_mlp):
    rows, width = normed.shape
    hidden = w_up.shape[1]
    tile = min(512, rows)
    block = pl.BlockSpec((tile, width), lambda i: (i, 0))
    wide = pl.BlockSpec((tile, hidden), lambda i: (i, 0))
    return call(
        feed_body,
        (rows // tile,),
        [block, block, whole(w_up.shape), whole((1, hidden)), whole(w_down.shape)],
        [wide, wide, block, whole((1, hidden))] + [block] * with_mlp,
        [
            like((rows, hidden), BF16),
            like((rows, hidden), BF16),
            like((rows, width), BF16),
            like((1, hidden), F32),
        ]
        + [like((rows, width), BF16)] * with_mlp,
        8 * rows * width * hidden,
        12 * rows * width + 4 * width * hidden,
        limit=24,
    )(normed, grad_mlp, w_up, up_bias, w_down)


def splits(rows, bits):
    return bits and rows % (16 * 2 ** len(bits)) == 0


def position(ordinal, here, bits):
    number = sum(bit for k, bit in enumerate(bits) if ordinal >> k & 1)
    found, step = 0, 2 ** len(bits) // 2
    for bit in bits:
        found = found + jnp.where((number ^ here) & bit != 0, step, 0)
        step //= 2
    return found


def put(value, first_row, bits, here, kept, sent):
    if sent is None:
        kept[first_row : first_row + value.shape[0]] = value
        return
    half = kept.shape[0]
    size = 2 * half // 2 ** len(bits)
    step = math.gcd(size, value.shape[0])
    for row in range(first_row, first_row + value.shape[0], step):
        spot = position(row // size, here, bits) * size + row % size
        part = value[row - first_row : row - first_row + step]

        @pl.when(spot < half)
        def _():
            kept[pl.ds(pl.multiple_of(spot, 16), step)] = part

        @pl.when(spot >= half)
        def _():
            sent[pl.ds(pl.multiple_of(spot - half, 16), step)] = part


def outer_body(groups, tile, count, based, place, *refs):
    pairs = sum(len(halves) for _, _, halves in groups)
    base, refs = refs[:based], refs[based:]
    left, right, outs = refs[: -count - pairs], refs[-count - pairs : -pairs], list(refs[-pairs:])
    for start, bits, halves in groups:
        kept = outs.pop(0)
        sent = outs.pop(0) if len(halves) > 1 else None
        rows = sum(halves)
        step = tile if rows % tile == 0 else rows
        for first in range(0, rows, step):
            total = base[0][start + first : start + first + step] if base else None
            for p in range(count):
                if len(left) == count:
                    a = left[p][:, start + first : start + first + step]
                else:
                    size = right[0].shape[0]
                    a = left[0][p * size : (p + 1) * size, start + first : start + first + step]
                term = mxu(a, right[p][...], TN)
                total = term if total is None else total + term
            put(total.astype(kept.dtype), first, bits, place[1], kept, sent)


def outer(place, left, right, groups, base=(), dtype=BF16):
    rows, width = right[0].shape
    count = len(right)
    found, start = [], 0
    for size, bits in groups:
        halves = [size // 2] * 2 if splits(size, bits) else [size]
        found.append((start, bits, halves))
        start += size
    outs = [rows_out for _, _, halves in found for rows_out in halves]
    results = call(
        functools.partial(outer_body, found, 256, count, len(base)),
        (1,),
        [scalars()] + [whole(a.shape) for a in (*base, *left)] + [whole((rows, width))] * count,
        [whole((rows_out, width)) for rows_out in outs],
        [like((rows_out, width), dtype) for rows_out in outs],
        0,
        0,
        limit=24,
    )(place, *base, *left, *right)
    results = list(results)
    return [[results.pop(0) for _ in halves] for _, _, halves in found]


def each_body(bits, count, place, *refs):
    for left, out in zip(refs[:count], refs[count + 1 :]):
        value = mxu(left[...], refs[count][...], TN).astype(BF16)
        depth = value.shape[0]
        if splits(depth, bits):
            put(value, 0, bits, place[1], out.at[: depth // 2], out.at[depth // 2 :])
        else:
            out[...] = value


def outer_each(place, left, right, bits):
    rows, depth = left[0].shape
    width = right.shape[1]
    count = len(left)
    return call(
        functools.partial(each_body, bits, count),
        (1,),
        [scalars()] + [whole((rows, depth))] * count + [whole((rows, width))],
        [whole((depth, width))] * count,
        [like((depth, width), BF16)] * count,
        2 * count * rows * depth * width,
        2 * (count * rows * depth + rows * width + count * depth * width),
    )(place, *left, right)


def unpack_body(bits, sections, place, first, second, *outs):
    half, shares = first.shape[0], 2 ** len(bits)
    size = 2 * half // shares
    for block in range(shares):
        spot = position(block, place[1], bits) * size
        offset = 0
        for out, rows in zip(outs, sections):
            count = rows // shares
            start = spot + offset
            low = pl.ds(pl.multiple_of(jnp.minimum(start, half - count), 16), count)
            high = pl.ds(pl.multiple_of(jnp.maximum(start - half, 0), 16), count)
            part = jnp.where(spot < half, first[low], second[high])
            out[block * count : (block + 1) * count] = part.astype(out.dtype)
            offset += count


def unpack(place, first, second, bits, sections, dtype=F32):
    half, width = first.shape
    return call(
        functools.partial(unpack_body, bits, sections),
        (1,),
        [scalars(), whole(first.shape), whole(second.shape)],
        [whole((rows, width)) for rows in sections],
        [like((rows, width), dtype) for rows in sections],
        2 * half * width,
        12 * half * width,
    )(place, first, second)


def join_body(bits_a, sections_a, bits_b, sections_b, place, *refs):
    joined, rows = refs[4], sections_a[0]
    unpack_body(bits_a, sections_a, place, refs[0], refs[1], joined.at[:rows], *refs[5:])
    unpack_body(bits_b, sections_b, place, refs[2], refs[3], joined.at[rows:])


def join(place, chain_a, chain_b):
    halves = [chain_a.kept, chain_a.came, chain_b.kept, chain_b.came]
    width = halves[0].shape[1]
    outs = [chain_a.sections[0] + chain_b.sections[0], *chain_a.sections[1:]]
    return call(
        functools.partial(
            join_body, chain_a.bits[:-1], chain_a.sections, chain_b.bits[:-1], chain_b.sections
        ),
        (1,),
        [scalars()] + [whole(half.shape) for half in halves],
        [whole((rows, width)) for rows in outs],
        [like((rows, width), F32) for rows in outs],
        0,
        0,
    )(place, *halves)


def project_body(group_count, piece_count, *refs):
    grads = refs[:group_count]
    weights = refs[group_count : 2 * group_count]
    normed = refs[2 * group_count : 2 * group_count + piece_count]
    outs = refs[2 * group_count + piece_count : -1]
    sums = refs[-1]
    size = normed[0].shape[0]
    plain = weighed = 0.0
    for p in range(piece_count):
        total = None
        for grad, weight in zip(grads, weights):
            term = mxu(grad[p * size : (p + 1) * size], weight[...], NN)
            total = term if total is None else total + term
        outs[p][...] = total.astype(BF16)
        plain = plain + column_sum(total)
        weighed = weighed + column_sum(total * normed[p][...].astype(F32))
    sums[0:1] = plain
    sums[1:2] = weighed


def project_back(grads, weights, normed):
    size, width = normed[0].shape
    depth = sum(w.shape[0] for w in weights)
    count = len(normed)
    results = call(
        functools.partial(project_body, len(grads), count),
        (1,),
        [whole(g.shape) for g in grads] + [whole(w.shape) for w in weights] + [whole((size, width))] * count,
        [whole((size, width))] * count + [whole((8, width))],
        [like((size, width), BF16)] * count + [like((8, width), F32)],
        2 * count * size * depth * width,
        2 * count * size * (depth + 2 * width) + 2 * depth * width,
        limit=20,
    )(*grads, *weights, *normed)
    return list(results[:-1]), results[-1][:2]


def second_back_body(item_count, piece_count, lengths, place, half_a, half_b, stream1, cotangent, gain, *refs):
    weights = refs[:piece_count]
    grad_out, attn_out = refs[piece_count : piece_count + 2]
    mixed_out = refs[piece_count + 2 : 2 * piece_count + 2]
    sums = refs[-1]
    tile = stream1.shape[0]
    first = place[0] * (tile * pl.num_programs(0)) + pl.program_id(0) * tile
    valid = valid_column(lengths, item_count, first, tile)
    grad_norm = half_a[...].astype(F32) + half_b[...].astype(F32)
    scaled, rstd = normalize(stream1[...])
    grad = valid * cotangent[...].astype(F32) + norm_back(grad_norm, scaled, gain[...], rstd)
    grad_out[...] = grad
    rounded = grad.astype(BF16)
    attn_out[...] = rounded

    @pl.when(pl.program_id(0) == 0)
    def _():
        sums[...] = jnp.zeros(sums.shape, F32)

    sums[0:1] += column_sum(grad_norm * scaled)
    sums[1:2] += column_sum(grad_norm)
    sums[2:3] += column_sum(rounded.astype(F32))
    for weight, mixed in zip(weights, mixed_out):
        mixed[...] = mxu(rounded, weight[...], NT).astype(BF16)


def second_back(lengths, place, half_a, half_b, stream1, cotangent, gain, weights):
    rows, width = stream1.shape
    tile = min(256, rows)
    count = len(weights)
    depth = weights[0].shape[0]
    block = pl.BlockSpec((tile, width), lambda i: (i, 0))
    narrow = pl.BlockSpec((tile, depth), lambda i: (i, 0))
    results = call(
        functools.partial(second_back_body, lengths.shape[0], count),
        (rows // tile,),
        [scalars(), scalars(), block, block, block, block, whole((1, width))]
        + [whole(weights[0].shape)] * count,
        [block, block] + [narrow] * count + [whole((8, width))],
        [like((rows, width), F32), like((rows, width), BF16)]
        + [like((rows, depth), BF16)] * count
        + [like((8, width), F32)],
        2 * rows * width * width,
        rows * width * 20 + 2 * width * width,
    )(lengths, place, half_a, half_b, stream1, cotangent, gain, *weights)
    return results[0], results[1], results[2:-1], results[-1][:3]


def output_body(item_count, lengths, place, half_a, half_b, shift, stream1, cotangent, out, sums):
    tile = stream1.shape[0]
    first = place[0] * (tile * pl.num_programs(0)) + pl.program_id(0) * tile
    valid = valid_column(lengths, item_count, first, tile)
    mlp = half_a[...].astype(F32) + half_b[...].astype(F32) + shift[...]
    stream2 = stream1[...] + mlp
    out[...] = (valid * stream2).astype(BF16)

    @pl.when(pl.program_id(0) == 0)
    def _():
        sums[...] = jnp.zeros(sums.shape, F32)

    sums[0:1] += column_sum(valid * stream2 * stream2)
    sums[1:2] += column_sum(valid * mlp * mlp)
    sums[2:3] += column_sum((valid * cotangent[...].astype(F32)).astype(BF16).astype(F32))
    sums[3:4] += jnp.broadcast_to(column_sum(valid), (1, stream1.shape[1]))


def output_end(lengths, place, half_a, half_b, shift, stream1, cotangent):
    rows, width = stream1.shape
    tile = min(256, rows)
    block = pl.BlockSpec((tile, width), lambda i: (i, 0))
    out, sums = call(
        functools.partial(output_body, lengths.shape[0]),
        (rows // tile,),
        [scalars(), scalars(), block, block, whole((1, width)), block, block],
        [block, whole((8, width))],
        [like((rows, width), BF16), like((8, width), F32)],
        12 * rows * width,
        rows * width * 12,
    )(lengths, place, half_a, half_b, shift, stream1, cotangent)
    return out, sums[:4]


def input_body(half_a, half_b, stream0, grad_stream1, gain, out):
    grad_norm = half_a[...].astype(F32) + half_b[...].astype(F32)
    scaled, rstd = normalize(stream0[...])
    out[...] = grad_stream1[...] + norm_back(grad_norm, scaled, gain[...].astype(F32), rstd)


def input_end(half_a, half_b, stream0, grad_stream1, gain):
    rows, width = stream0.shape
    tile = min(256, rows)
    block = pl.BlockSpec((tile, width), lambda i: (i, 0))
    return call(
        input_body,
        (rows // tile,),
        [block, block, block, block, whole((1, width))],
        block,
        like((rows, width), F32),
        12 * rows * width,
        rows * width * 16,
    )(half_a, half_b, stream0, grad_stream1, gain)


def swap(array, axis, bit):
    return lax.ppermute(array, axis, [(i, i ^ bit) for i in range(lax.axis_size(axis))])


def after(array, *others):
    return lax.optimization_barrier((array, *others))[0]


def spread(own, top):
    pieces, bit = {0: own}, top // 2
    while bit:
        for p in sorted(pieces):
            pieces[p | bit] = swap(pieces[p], "mp", bit)
        bit //= 2
    return [pieces[p] for p in range(len(pieces))]


def add(left, right):
    return (left.astype(F32) + right.astype(F32)).astype(left.dtype)


def fold(parts, *others):
    bit = 1
    while len(parts) > 1:
        came = [swap(parts[p + 1], "mp", bit) for p in range(0, len(parts), 2)]
        if others:
            came = [after(array, *others) for array in came]
        parts = [add(parts[2 * k], array) for k, array in enumerate(came)]
        bit *= 2
    return parts[0]


def exchange(parts):
    return [parts[0]] + [swap(parts[p], "mp", p) for p in range(1, len(parts))]


def total(array, axis):
    bit = 1
    while bit < lax.axis_size(axis):
        array = array + swap(array, axis, bit)
        bit *= 2
    return array


def own_block(place, weight, bits):
    if not splits(weight.shape[0], bits):
        return weight
    size = weight.shape[0] // 2 ** len(bits)
    return lax.dynamic_slice_in_dim(weight, place[1] * size, size, 0)


def join_blocks(place, kept, rows, bits):
    if kept.shape[0] == rows:
        return kept
    for bit in bits[:0:-1]:
        kept = jnp.concatenate([kept, swap(kept, "dp", bit)], axis=0)
    return unpack(place, kept, swap(kept, "dp", bits[0]), bits, [rows], kept.dtype)[0]


class DpSum:
    def __init__(self, place, parts, bits, *others):
        self.place, self.bits, self.steps = place, bits, 0
        self.sections = [sum(half.shape[0] for half in halves) for halves in parts]
        blocks, width = max(2 ** (len(bits) - 1) // 2, 1), parts[0][0].shape[1]
        halves = [
            jnp.concatenate([half.reshape(blocks, -1, width) for half in group], axis=1).reshape(-1, width)
            for group in zip(*parts)
        ]
        if len(halves) == 1:
            self.kept = lax.psum(halves[0], "dp")
            return
        self.kept, self.sent = halves
        self.came = swap(after(self.sent, *others), "dp", bits[0])

    def step(self, *others):
        if not self.more():
            return
        self.steps += 1
        came, count = after(self.came, *others), len(self.bits)
        if self.steps < count:
            half = came.shape[0] // 2
            self.sent = add(self.kept[half:], came[half:])
            self.kept = add(self.kept[:half], came[:half])
            if self.steps == count - 1:
                self.kept = self.sent = jnp.concatenate([self.kept, self.sent], axis=0)
            self.came = swap(self.sent, "dp", self.bits[self.steps])
        else:
            if self.steps == count:
                self.kept = add(self.kept, came)
            else:
                self.kept = jnp.concatenate([self.kept, came], axis=0)
            self.sent = self.kept
            self.came = swap(self.kept, "dp", self.bits[2 * count - 2 - self.steps])

    def now(self):
        return [self.kept, self.sent] if hasattr(self, "came") else []

    def more(self):
        return hasattr(self, "came") and self.steps < 2 * len(self.bits) - 2

    def done(self, *others):
        if not hasattr(self, "came"):
            return [self.kept.astype(F32)]
        came = after(self.came, *others) if others else self.came
        return unpack(self.place, self.kept, came, self.bits[:-1], self.sections)


def advance(chains, others):
    for chain in chains:
        chain.step(*others)
    return [array for chain in chains for array in chain.now()] or list(others)


def per_device(
    tokens, cotangent, lengths, gsd_ratio, ln1_gain, ln1_bias, w_qkv, qv_bias, w_out, out_bias,
    ln2_gain, ln2_bias, w_up, up_bias, w_down, down_bias,
):
    own_rows, width = tokens.shape
    mp_count, dp_count = lax.axis_size("mp"), lax.axis_size("dp")
    top = mp_count // 2
    low_first = [1 << k for k in range(dp_count.bit_length() - 1)] if dp_count & (dp_count - 1) == 0 else []
    low_second = low_first[1:2] + low_first[:1] + low_first[2:]
    low_last = low_first[1:] + low_first[:1]
    place = jnp.stack([lax.axis_index("mp"), lax.axis_index("dp")]).astype(jnp.int32)
    depth = w_qkv.shape[1]
    heads = depth // HD
    gain2, bias2 = ln2_gain[None], ln2_bias[None]
    up_shift = up_bias[None]

    w_out_block = swap(own_block(place, w_out, low_first), "mp", top)
    grad_mlp_own = mask_rows(lengths, place, cotangent)
    early = own_rows // 8
    grad_mlp_far = swap(grad_mlp_own[:early], "mp", top)
    tokens = after(tokens, w_out_block)
    stream0, normed1_own = encode(lengths, gsd_ratio, place, tokens, ln1_gain[None], ln1_bias[None])
    normed1_far = swap(after(normed1_own, grad_mlp_far), "mp", top)
    w_out_far = join_blocks(place, w_out_block, depth, low_first)
    normed1 = spread(normed1_own, top)
    w_flat = w_qkv.reshape(3 * depth, width)
    shift = jnp.concatenate([qv_bias[0], jnp.zeros((depth,), F32), qv_bias[1]])[None]

    def project(piece):
        return (mxu(piece, w_flat, NT) + shift).astype(BF16)

    qkv = [project(piece) for piece in normed1]
    grad_mlp = spread(grad_mlp_own, top)
    w_out_all = spread(w_out, top)
    normed1_far = after(normed1_far, w_out_far, *qkv, *grad_mlp, *w_out_all)
    grad_mlp_late = swap(after(grad_mlp_own[early:], normed1_far), "mp", top)
    normed1 += spread(normed1_far, top)
    w_out_all += spread(w_out_far, top)
    qkv += [project(piece) for piece in normed1[top:]]

    attended, logsum = attend(lengths, place, qkv)
    attended, grad_mlp_late = lax.optimization_barrier((attended, grad_mlp_late))
    grad_mlp_far = jnp.concatenate([grad_mlp_far, grad_mlp_late], axis=0)
    mixed = exchange([attended[p * own_rows : (p + 1) * own_rows] for p in range(mp_count)])
    grad_mlp += spread(grad_mlp_far, top)
    mixed[0] = after(mixed[0], *grad_mlp)
    stream1, normed2_own, attn_squares = branch(
        lengths, place, mixed, w_out_all, stream0, out_bias[None], gain2, bias2
    )

    normed2_far = swap(normed2_own, "mp", top)
    normed2 = spread(normed2_own, top)
    fed = [feed(normed2[p], grad_mlp[p], w_up, up_shift, w_down, True) for p in range(top)]
    [[down_base]] = outer(place, [f[0] for f in fed], grad_mlp[:top], [(w_down.shape[0], [])], dtype=F32)
    [[up_base]] = outer(place, normed2, [f[1] for f in fed], [(width, [])], dtype=F32)
    far_normed = spread(after(normed2_far, down_base, up_base), top)
    norm2_near, mlp_near = fold([f[2] for f in fed]), fold([f[4] for f in fed])
    far_normed[-1] = after(far_normed[-1], norm2_near, mlp_near)
    right = grad_mlp[top:]
    far_fed = [feed(n, g, w_up, up_shift, w_down, False) for n, g in zip(far_normed, right)]
    norm2_part = fold([f[2] for f in far_fed])
    norm2_far = swap(norm2_part, "mp", top)
    acts, upins = [f[0] for f in far_fed], [f[1] for f in far_fed]
    acts[-1] = after(acts[-1], norm2_part)
    [down_halves] = outer(place, acts, right, [(w_down.shape[0], low_first[:-1])], [down_base])
    grad_down = DpSum(place, [down_halves], low_first)
    upins[-1] = after(upins[-1], *down_halves)
    [up_halves] = outer(place, far_normed, upins, [(width, low_last[:-1])], [up_base])
    grad_up = DpSum(place, [up_halves], low_last)
    grad_up_bias = functools.reduce(jnp.add, [f[3] for f in fed + far_fed])
    mlp_parts = [mxu(after(f[0], *up_halves), w_down, NN).astype(BF16) for f in far_fed]
    norm2_far = after(norm2_far, *mlp_parts)
    grad_stream1, grad_attn, grad_mixed, second_sums = second_back(
        lengths, place, norm2_near, norm2_far, stream1, cotangent, gain2, w_out_all
    )

    grads = exchange(list(grad_mixed))
    out_parts = outer_each(place, mixed, grad_attn, low_first[:-1])
    out_near, out_part = fold(out_parts[:top]), fold(out_parts[top:])
    now = advance([grad_down, grad_up], grads)
    grads[-1] = after(grads[-1], out_near, out_part, *now)
    out_far = swap(after(out_part, grads[-1]), "mp", top)
    proj, proj_sums = attend_back(lengths, place, qkv, grads, attended, logsum, 0, heads)
    mlp_far = swap(fold(mlp_parts, proj), "mp", top)
    now = advance([grad_down, grad_up], [proj])
    qkv_rows = 3 * depth // 2
    halves_a, halves_b = outer(
        place, [after(proj, *now)], normed1, [(qkv_rows, low_first[:-1]), (qkv_rows, low_second[:-1])]
    )
    out_far = after(out_far, proj)
    out_sum = add(out_near, out_far)
    groups_a = [halves_a]
    if len(halves_a) > 1 and splits(depth, low_first[:-1]):
        groups_a.append([out_sum[: depth // 2], out_sum[depth // 2 :]])
    grad_a, grad_b = DpSum(place, groups_a, low_first), DpSum(place, [halves_b], low_second)
    main, proj_chains = [grad_down, grad_up], [grad_a, grad_b]
    now = [*now, *grad_a.now(), *grad_b.now()]
    parts, first_sums = project_back([after(proj, *now)], [w_flat], normed1)
    chains = main + proj_chains
    mp_hops = [1 << k for k in range(mp_count.bit_length() - 1)]
    dp_hops = [low_first[0], *low_first[:0:-1]] if low_first else []

    def hop(array, axis, hops, *others):
        return array + after(swap(array, axis, hops.pop(0)), *others) if hops else array

    norm1_part, norm1_near = fold(parts[top:], first_sums), fold(parts[:top], first_sums)
    now = advance(chains, [first_sums])

    norm1_far = swap(norm1_part, "mp", top)
    output, output_sums = output_end(
        lengths, place, after(mlp_near, *now), mlp_far, down_bias[None], stream1, cotangent
    )
    rows = jnp.concatenate([first_sums, second_sums, output_sums, attn_squares], axis=0)
    while len(mp_hops) > 1:
        rows = hop(rows, "mp", mp_hops, output_sums)
    flat = jnp.concatenate([grad_up_bias[0], proj_sums[0, :depth], proj_sums[0, 2 * depth :]])
    flat = jnp.pad(flat, (0, -flat.size % 1024)).reshape(-1, 128)
    flat = jnp.concatenate([rows.reshape(-1, 128), flat], axis=0)
    flat = hop(flat, "dp", dp_hops, norm1_near)
    norm1_far = after(norm1_far, flat)
    now = advance(chains, [flat])

    input_grad = input_end(
        norm1_near, norm1_far, after(stream0, *now), grad_stream1, ln1_gain[None]
    )
    flat = jnp.concatenate(
        [hop(flat[: rows.size // 128], "mp", mp_hops, input_grad), flat[rows.size // 128 :]], axis=0
    )
    now = advance(proj_chains, [input_grad, flat])
    while any(chain.more() for chain in main):
        now = advance(main, now)

    [grad_down], [grad_up] = grad_down.done(*now), grad_up.done(*now)
    while dp_hops or any(chain.more() for chain in proj_chains):
        flat = hop(flat, "dp", dp_hops, grad_down, grad_up)
        now = advance(proj_chains, [grad_down, grad_up, flat])

    if hasattr(grad_a, "came") and hasattr(grad_b, "came"):
        grad_qkv, *others = join(place, grad_a, grad_b)
    else:
        grad_qkv, others = jnp.concatenate([grad_a.done()[0], grad_b.done()[0]], axis=0), []
    grad_qkv = grad_qkv.reshape(3, depth, width)
    grad_out_weight = others[0] if others else lax.psum(out_sum, "dp").astype(F32)
    flat = flat.reshape(-1)
    rows = flat[: rows.size].reshape(rows.shape)
    up_sums = flat[rows.size : rows.size + up_bias.shape[0]]
    proj_sums = flat[rows.size + up_bias.shape[0] :][: 2 * depth].reshape(2, depth)
    squares = jnp.stack([jnp.sum(rows[5]), jnp.sum(rows[9]), jnp.sum(rows[6])])
    stats = jnp.sqrt(squares / (rows[8, 0] * width))
    grad_ln1_gain = (rows[1] - ln1_bias.astype(F32) * rows[0]) / ln1_gain.astype(F32)
    return (
        output, input_grad, grad_ln1_gain, rows[0], grad_qkv, proj_sums, grad_out_weight, rows[4],
        rows[2], rows[3], grad_up, up_sums, grad_down, rows[7], stats,
    )


def solution(mesh):
    rows, one = P(("dp", "mp"), None), P()
    placed = (
        rows, rows, P("dp"), P("dp"), one, one, P(None, "mp", None), P(None, "mp"), P("mp", None), one,
        one, one, P(None, "mp"), P("mp"), P("mp", None), one,
    )
    results = (
        rows, rows, one, one, P(None, "mp", None), P(None, "mp"), P("mp", None), one,
        one, one, P(None, "mp"), P("mp"), P("mp", None), one, one,
    )
    return jax.shard_map(per_device, mesh=mesh, in_specs=placed, out_specs=results, check_vma=False)
```

```python
import functools
import math

import jax
import jax.numpy as jnp
import numpy as np
from jax import lax
from jax.experimental import pallas as pl
from jax.experimental.pallas import tpu as pltpu
from jax.sharding import PartitionSpec as P

HD = 64
EPS = 1e-06
MASKED = -1e30
F32 = jnp.float32
BF16 = jnp.bfloat16
NT = (((1,), (1,)), ((), ()))
TN = (((0,), (0,)), ((), ()))
NN = (((1,), (0,)), ((), ()))


def mxu(left, right, dims):
    return lax.dot_general(left, right, dims, preferred_element_type=F32)


def whole(shape):
    return pl.BlockSpec(shape, lambda *_: (0,) * len(shape))


def scalars():
    return pl.BlockSpec(memory_space=pltpu.SMEM)


def call(body, grid, in_specs, out_specs, out_shape, flops, moved, scratch=(), limit=12):
    return pl.pallas_call(
        body,
        grid=grid,
        in_specs=in_specs,
        out_specs=out_specs,
        out_shape=out_shape,
        scratch_shapes=list(scratch),
        compiler_params=pltpu.CompilerParams(
            dimension_semantics=("arbitrary",) * len(grid), vmem_limit_bytes=limit * 1024 * 1024
        ),
        cost_estimate=pl.CostEstimate(
            flops=0, bytes_accessed=0, transcendentals=0
        ),
    )


def like(shape, dtype):
    return jax.ShapeDtypeStruct(shape, dtype)


def item_ends(lengths_ref, item_count):
    ends, total = [], 0
    for item in range(item_count):
        total = total + lengths_ref[item]
        ends.append(total)
    return ends


def segment_of(rows, ends):
    segment = jnp.zeros(rows.shape, jnp.int32)
    for end in ends:
        segment = segment + jnp.where(rows >= end, 1, 0)
    return segment


def scalar_segment(row, ends):
    segment = jnp.int32(0)
    for end in ends:
        segment = segment + jnp.where(row >= end, 1, 0)
    return segment


def valid_column(lengths_ref, item_count, first_row, row_count):
    rows = first_row + lax.broadcasted_iota(jnp.int32, (row_count, 1), 0)
    return jnp.where(rows < item_ends(lengths_ref, item_count)[-1], 1.0, 0.0).astype(F32)


def normalize(stream):
    centred = stream - jnp.mean(stream, axis=1, keepdims=True)
    rstd = lax.rsqrt(jnp.mean(centred * centred, axis=1, keepdims=True) + EPS)
    return centred * rstd, rstd


def norm_back(gradient, scaled, gain, rstd):
    spread = gradient * gain
    first = jnp.mean(spread, axis=1, keepdims=True)
    second = jnp.mean(spread * scaled, axis=1, keepdims=True)
    return rstd * (spread - first - scaled * second)


def column_sum(array):
    return jnp.sum(array, axis=0, keepdims=True)


def sin_cos(angle):
    turns = jnp.floor(angle * (2.0 / math.pi) + 0.5)
    rest = angle - turns * 1.5703125
    rest = rest - turns * 4.837512969970703125e-4
    rest = rest - turns * 7.54978995489188216e-8
    square = rest * rest
    sine = rest + rest * square * (
        -1.6666654611e-1 + square * (8.3321608736e-3 + square * -1.9515295891e-4)
    )
    cosine = (
        1.0
        - 0.5 * square
        + square
        * square
        * (
            4.166664568298827e-2
            + square * (-1.388731625493765e-3 + square * 2.443315711809948e-5)
        )
    )
    quarter = turns.astype(jnp.int32)
    odd = (quarter & 1) == 1
    sine_flip = (quarter & 2) != 0
    cosine_flip = ((quarter + 1) & 2) != 0
    first = jnp.where(odd, cosine, sine)
    second = jnp.where(odd, sine, cosine)
    return jnp.where(sine_flip, -first, first), jnp.where(cosine_flip, -second, second)


def encode_body(item_count, lengths, ratios, place, tokens, freq, gain, bias, stream_out, normed_out):
    rows_here, width = tokens.shape
    row = (
        place[0] * (rows_here * pl.num_programs(0))
        + pl.program_id(0) * rows_here
        + lax.broadcasted_iota(jnp.int32, (rows_here, 1), 0)
    )
    position = jnp.zeros((rows_here, 1), jnp.int32)
    ratio = jnp.zeros((rows_here, 1), F32)
    start = 0
    for item in range(item_count):
        end = start + lengths[item]
        inside = (row >= start) & (row < end)
        position = jnp.where(inside, row - start, position)
        ratio = jnp.where(inside, ratios[item], ratio)
        start = end
    angle = (position.astype(F32) * ratio) * freq[...]
    sine, cosine = sin_cos(angle)
    stream = tokens[...].astype(F32) + jnp.concatenate([sine, cosine], axis=1)
    stream_out[...] = stream
    scaled, _ = normalize(stream)
    normed_out[...] = (scaled * gain[...].astype(F32) + bias[...].astype(F32)).astype(BF16)


def encode(lengths, ratios, place, tokens, gain, bias):
    rows, width = tokens.shape
    half = width // 2
    tile = min(256, rows)
    freq = np.exp(np.arange(half) * (-math.log(10000.0) / half)).astype(np.float32)[None]
    body = functools.partial(encode_body, lengths.shape[0])
    block = pl.BlockSpec((tile, width), lambda i: (i, 0))
    return call(
        body,
        (rows // tile,),
        [scalars(), scalars(), scalars(), block, whole((1, half)), whole((1, width)), whole((1, width))],
        [block, block],
        [like((rows, width), F32), like((rows, width), BF16)],
        60 * rows * width,
        8 * rows * width,
    )(lengths, ratios, place, tokens, freq, gain, bias)


def mask_body(item_count, lengths, place, cotangent, out):
    rows = cotangent.shape[0]
    valid = valid_column(lengths, item_count, place[0] * rows, rows)
    out[...] = (valid * cotangent[...].astype(F32)).astype(BF16)


def mask_rows(lengths, place, cotangent):
    return call(
        functools.partial(mask_body, lengths.shape[0]),
        (1,),
        [scalars(), scalars(), whole(cotangent.shape)],
        whole(cotangent.shape),
        like(cotangent.shape, BF16),
        2 * cotangent.size,
        4 * cotangent.size,
    )(lengths, place, cotangent)


def local_tile(tile, tile_rows, own_rows, place):
    return tile ^ ((place * own_rows) // tile_rows)


def first_and_last(tile, tile_rows, other_rows, ends):
    low = scalar_segment(tile * tile_rows, ends)
    high = scalar_segment(tile * tile_rows + tile_rows - 1, ends)
    start, stop = jnp.int32(0), jnp.int32(0)
    for item, end in enumerate(ends):
        start = jnp.where(low > item, end, start)
        stop = jnp.where(high >= item, end, stop)
    return start // other_rows, (stop - 1) // other_rows


def used_tiles(tile_rows, ends):
    return (ends[-1] + tile_rows - 1) // tile_rows


def head_lanes(count):
    lane = lax.broadcasted_iota(jnp.int32, (1, 2 * HD), 1)
    return [jnp.where(lane // HD == k, 1.0, 0.0) for k in range(count)]


def marks(tile, tile_rows, own_rows, place, ends):
    rows = tile * tile_rows + lax.broadcasted_iota(jnp.int32, (tile_rows, 2 * HD), 0)
    lane = lax.broadcasted_iota(jnp.int32, (tile_rows, 2 * HD), 1) % HD
    same = segment_of(rows ^ (place * own_rows), ends) == lane
    query_marks = jnp.where(same, 1.0, 0.0)
    key_marks = jnp.where(same | (lane > len(ends)), 0.0, MASKED)
    return query_marks, key_marks


class Rows:
    def __init__(self, tile_rows, own_rows):
        self.part = min(tile_rows, own_rows)
        self.tile_rows, self.own_rows = tile_rows, own_rows

    def pair(self, refs, tile, column, count):
        found = []
        for row in range(tile * self.tile_rows, (tile + 1) * self.tile_rows, self.part):
            ref = refs[row // self.own_rows]
            found.append(ref[pl.ds(row % self.own_rows, self.part), column : column + count * HD])
        found = found[0] if len(found) == 1 else jnp.concatenate(found, axis=0)
        if count == 1:
            found = jnp.concatenate([found, jnp.zeros_like(found)], axis=1)
        return found


def attend_body(item_count, heads, tile_q, tile, piece_count, lengths, place_ref, *refs):
    pieces = refs[:piece_count]
    out, lse_out = refs[piece_count : piece_count + 2]
    qa, ka, vt, acc, top = refs[piece_count + 2 :]
    own_rows = pieces[0].shape[0]
    tiles = own_rows * piece_count // tile
    ratio = tile_q // tile
    width = heads * HD
    place = place_ref[0]
    ends = item_ends(lengths, item_count)
    rows = Rows(tile, own_rows)
    lanes = head_lanes(2)
    for t in range(tiles):
        query_marks, key_marks = marks(t, tile, own_rows, place, ends)
        here = slice(t % ratio * tile, (t % ratio + 1) * tile)
        for h in range(0, heads, 2):
            count = min(2, heads - h)
            query = rows.pair(pieces, t, h * HD, count)
            key = rows.pair(pieces, t, width + h * HD, count)
            value = rows.pair(pieces, t, 2 * width + h * HD, count).T
            for k in range(count):
                mine, other = lanes[k], lanes[1 - k]
                scale = (mine * HD**-0.5).astype(BF16)
                qa[h + k, t // ratio, here] = query * scale + (query_marks * other).astype(BF16)
                ka[h + k, t] = key * mine.astype(BF16) + (key_marks * other).astype(BF16)
                vt[h + k, t, :HD] = value[k * HD : (k + 1) * HD]
                vt[h + k, t, HD:] = jnp.ones((vt.shape[2] - HD, tile), BF16)

    def query_tile(tile_index, carry):
        i = local_tile(tile_index, tile_q, own_rows, place)
        first, last = first_and_last(tile_index, tile_q, tile, ends)
        acc[...] = jnp.zeros(acc.shape, F32)
        top[...] = jnp.full(top.shape, -3e38, F32)

        def key_tile(other_index, inner):
            j = local_tile(other_index, tile, own_rows, place)
            scores = [mxu(ka[h, j], qa[h, i], NT) for h in range(heads)]
            old = [top[h] for h in range(heads)]
            new = [jnp.maximum(old[h], jnp.max(scores[h], axis=0, keepdims=True)) for h in range(heads)]
            probs = [jnp.exp(scores[h] - new[h]).astype(BF16) for h in range(heads)]
            mixed = [mxu(vt[h, j], probs[h], NN) for h in range(heads)]
            for h in range(heads):
                top[h] = new[h]
                acc[h] = acc[h] * jnp.exp(old[h] - new[h]) + mixed[h]
            return inner

        lax.fori_loop(first, last + 1, key_tile, 0)
        here = pl.ds(pl.multiple_of(i * tile_q, tile_q), tile_q)
        for h in range(0, heads, 2):
            count = min(2, heads - h)
            mixed = []
            for k in range(count):
                total = acc[h + k, HD : HD + 1, :]
                lse = top[h + k] + jnp.log(total)
                for s in range(ratio):
                    lse_out[h + k, i * ratio + s] = lse[:, s * tile : (s + 1) * tile]
                mixed.append(acc[h + k, :HD, :] / total)
            mixed = jnp.concatenate(mixed, axis=0) if count > 1 else mixed[0]
            out[here, h * HD : (h + count) * HD] = mixed.T.astype(BF16)
        return carry

    def unused_tile(tile_index, carry):
        i = local_tile(tile_index, tile_q, own_rows, place)
        for s in range(ratio):
            lse_out[:, i * ratio + s] = jnp.zeros((heads, 1, tile), F32)
        out[pl.ds(pl.multiple_of(i * tile_q, tile_q), tile_q), :] = jnp.zeros((tile_q, width), BF16)
        return carry

    used = used_tiles(tile_q, ends)
    lax.fori_loop(0, used, query_tile, 0)
    lax.fori_loop(used, tiles // ratio, unused_tile, 0)


def attend(lengths, place, pieces):
    own_rows, width3 = pieces[0].shape
    width = width3 // 3
    heads = width // HD
    rows = own_rows * len(pieces)
    tile = min(256, rows)
    tile_q = min(512, rows)
    tiles = rows // tile
    body = functools.partial(attend_body, lengths.shape[0], heads, tile_q, tile, len(pieces))
    return call(
        body,
        (1,),
        [scalars(), scalars()] + [whole((own_rows, width3))] * len(pieces),
        [whole((rows, width)), whole((heads, tiles, 1, tile))],
        [like((rows, width), BF16), like((heads, tiles, 1, tile), F32)],
        rows * rows * width * 2,
        10 * rows * width,
        [
            pltpu.VMEM((heads, rows // tile_q, tile_q, 2 * HD), BF16),
            pltpu.VMEM((heads, tiles, tile, 2 * HD), BF16),
            pltpu.VMEM((heads, tiles, HD + 16, tile), BF16),
            pltpu.VMEM((heads, HD + 16, tile_q), F32),
            pltpu.VMEM((heads, 1, tile_q), F32),
        ],
        limit=10,
    )(lengths, place, *pieces)


def attend_back_body(item_count, start, heads, tile, piece_count, lengths, place_ref, *refs):
    pieces = refs[:piece_count]
    grads = refs[piece_count : 2 * piece_count]
    mixed, lse, out, sums = refs[2 * piece_count : 2 * piece_count + 4]
    qa, qm, ka, kt, vals, dos, delta, dk, dv, dqt = refs[2 * piece_count + 4 :]
    own_rows = pieces[0].shape[0]
    tiles = own_rows * piece_count // tile
    width = heads * HD
    full = pieces[0].shape[1] // 3
    base = start * HD
    place = place_ref[0]
    ends = item_ends(lengths, item_count)
    rows = Rows(tile, own_rows)
    lanes = head_lanes(2)
    scale = HD**-0.5
    for t in range(tiles):
        query_marks, key_marks = marks(t, tile, own_rows, place, ends)
        for h in range(0, heads, 2):
            count = min(2, heads - h)
            column = base + h * HD
            query = rows.pair(pieces, t, column, count)
            key = rows.pair(pieces, t, full + column, count)
            grad = rows.pair(grads, t, column, count)
            came = mixed[t * tile : (t + 1) * tile, column : column + count * HD].astype(F32)
            if count == 1:
                came = jnp.concatenate([came, jnp.zeros_like(came)], axis=1)
            weighed = (grad.astype(F32) * came).T
            turned = key.T
            vals[h // 2, t] = rows.pair(pieces, t, 2 * full + column, count)
            for k in range(count):
                mine, other = lanes[k], lanes[1 - k]
                alone = query * (mine * scale).astype(BF16)
                qm[h + k, t] = alone
                qa[h + k, t] = alone + (query_marks * other).astype(BF16)
                ka[h + k, t] = key * mine.astype(BF16) + (key_marks * other).astype(BF16)
                dos[h + k, t] = grad * mine.astype(BF16)
                kt[h + k, t] = turned[k * HD : (k + 1) * HD]
                delta[h + k, t] = column_sum(weighed[k * HD : (k + 1) * HD])
    dqt[...] = jnp.zeros(dqt.shape, F32)

    def key_tile(tile_index, carry):
        j = local_tile(tile_index, tile, own_rows, place)
        first, last = first_and_last(tile_index, tile, tile, ends)
        dk[...] = jnp.zeros(dk.shape, F32)
        dv[...] = jnp.zeros(dv.shape, F32)

        def query_tile(other_index, inner):
            i = local_tile(other_index, tile, own_rows, place)
            scores = [mxu(ka[h, j], qa[h, i], NT) for h in range(heads)]
            grad_probs = [mxu(vals[h // 2, j], dos[h, i], NT) for h in range(heads)]
            for h in range(heads):
                probs = jnp.exp(scores[h] - lse[start + h, i])
                grad_scores = (probs * (grad_probs[h] - delta[h, i])).astype(BF16)
                dv[h] += mxu(probs.astype(BF16), dos[h, i], NN)
                dk[h] += mxu(grad_scores, qm[h, i], NN)
                dqt[h, i] += mxu(kt[h, j], grad_scores, NN)
            return inner

        lax.fori_loop(first, last + 1, query_tile, 0)
        here = pl.ds(pl.multiple_of(j * tile, tile), tile)
        for h in range(0, heads, 2):
            count = min(2, heads - h)
            first = width + h * HD
            for kept, column in ((dk, first), (dv, width + first)):
                both = kept[h] + kept[h + 1] if count > 1 else kept[h]
                out[here, column : column + count * HD] = both[:, : count * HD].astype(BF16)
        return carry

    def unused_tile(tile_index, carry):
        j = local_tile(tile_index, tile, own_rows, place)
        here = pl.ds(pl.multiple_of(j * tile, tile), tile)
        out[here, width:] = jnp.zeros((tile, 2 * width), BF16)
        return carry

    used = used_tiles(tile, ends)
    lax.fori_loop(0, used, key_tile, 0)
    lax.fori_loop(used, tiles, unused_tile, 0)
    for t in range(tiles):
        for h in range(0, heads, 2):
            count = min(2, heads - h)
            both = [dqt[h + k, t] for k in range(count)]
            both = jnp.concatenate(both, axis=0) if count > 1 else both[0]
            out[t * tile : (t + 1) * tile, h * HD : (h + count) * HD] = (both.T * scale).astype(BF16)
    sums[...] = column_sum(out[...].astype(F32))


def attend_back(lengths, place, pieces, grads, mixed, lse, start, heads):
    own_rows = pieces[0].shape[0]
    width = heads * HD
    pairs = (heads + 1) // 2
    rows = own_rows * len(pieces)
    tile = min(256, rows)
    tiles = rows // tile
    body = functools.partial(attend_back_body, lengths.shape[0], start, heads, tile, len(pieces))
    return call(
        body,
        (1,),
        [scalars(), scalars()]
        + [whole(piece.shape) for piece in pieces]
        + [whole(grad.shape) for grad in grads]
        + [whole(mixed.shape), whole(lse.shape)],
        [whole((rows, 3 * width)), whole((1, 3 * width))],
        [like((rows, 3 * width), BF16), like((1, 3 * width), F32)],
        rows * rows * width * 5,
        16 * rows * width,
        [
            pltpu.VMEM((heads, tiles, tile, 2 * HD), BF16),
            pltpu.VMEM((heads, tiles, tile, 2 * HD), BF16),
            pltpu.VMEM((heads, tiles, tile, 2 * HD), BF16),
            pltpu.VMEM((heads, tiles, HD, tile), BF16),
            pltpu.VMEM((pairs, tiles, tile, 2 * HD), BF16),
            pltpu.VMEM((heads, tiles, tile, 2 * HD), BF16),
            pltpu.VMEM((heads, tiles, 1, tile), F32),
            pltpu.VMEM((heads, tile, 2 * HD), F32),
            pltpu.VMEM((heads, tile, 2 * HD), F32),
            pltpu.VMEM((heads, tiles, HD, tile), F32),
        ],
        limit=16,
    )(lengths, place, *pieces, *grads, mixed, lse)


def branch_body(item_count, piece_count, lengths, place, *refs):
    mixed = refs[:piece_count]
    weights = refs[piece_count : 2 * piece_count]
    stream0, shift, gain, bias, stream1, normed, squares = refs[2 * piece_count :]
    tile = stream0.shape[0]
    attn = shift[...]
    for left, right in zip(mixed, weights):
        attn = attn + mxu(left[...], right[...], NN)
    first = place[0] * (tile * pl.num_programs(0)) + pl.program_id(0) * tile
    valid = valid_column(lengths, item_count, first, tile)
    stream = stream0[...] + attn
    stream1[...] = stream
    scaled, _ = normalize(stream)
    normed[...] = (scaled * gain[...] + bias[...]).astype(BF16)

    @pl.when(pl.program_id(0) == 0)
    def _():
        squares[...] = jnp.zeros(squares.shape, F32)

    squares[...] += column_sum(valid * attn * attn)


def branch(lengths, place, mixed, weights, stream0, shift, gain, bias):
    rows, width = stream0.shape
    tile = min(256, rows)
    count = len(mixed)
    block = pl.BlockSpec((tile, width), lambda i: (i, 0))
    narrow = pl.BlockSpec((tile, mixed[0].shape[1]), lambda i: (i, 0))
    line = whole((1, width))
    return call(
        functools.partial(branch_body, lengths.shape[0], count),
        (rows // tile,),
        [scalars(), scalars()]
        + [narrow] * count
        + [whole(weights[0].shape)] * count
        + [block, line, line, line],
        [block, block, line],
        [like((rows, width), F32), like((rows, width), BF16), like((1, width), F32)],
        2 * rows * width * width,
        rows * width * 12 + 2 * width * width,
    )(lengths, place, *mixed, *weights, stream0, shift, gain, bias)


def feed_body(normed, grad_mlp, w_up, up_bias, w_down, act_out, upin_out, norm_out, bias_out, *mlp_out):
    hidden = w_up.shape[1]
    chunk = min(512, hidden)
    left, grad = normed[...], grad_mlp[...]
    mlp = norm = None

    @pl.when(pl.program_id(0) == 0)
    def _():
        bias_out[...] = jnp.zeros(bias_out.shape, F32)

    for c in range(0, hidden, chunk):
        here = slice(c, c + chunk)
        up = mxu(left, w_up[:, here], NN) + up_bias[:, here]
        grad_act = mxu(grad, w_down[here, :], NT)
        size = jnp.abs(up)
        decay = jnp.exp(-0.5 * up * up)
        t = 1.0 / (1.0 + (0.3275911 * 0.7071067811865476) * size)
        series = t * (
            0.254829592
            + t * (-0.284496736 + t * (1.421413741 + t * (-1.453152027 + t * 1.061405429)))
        )
        tail = 0.5 * series * decay
        share = jnp.where(up >= 0.0, 1.0 - tail, tail)
        act = (up * share).astype(BF16)
        upin = ((share + up * decay * 0.3989422804014327) * grad_act).astype(BF16)
        act_out[:, here] = act
        upin_out[:, here] = upin
        bias_out[:, here] += column_sum(upin.astype(F32))
        norm_part = mxu(upin, w_up[:, here], NT)
        norm = norm_part if norm is None else norm + norm_part
        if mlp_out:
            mlp_part = mxu(act, w_down[here, :], NN)
            mlp = mlp_part if mlp is None else mlp + mlp_part
    norm_out[...] = norm.astype(BF16)
    if mlp_out:
        mlp_out[0][...] = mlp.astype(BF16)


def feed(normed, grad_mlp, w_up, up_bias, w_down, with_mlp):
    rows, width = normed.shape
    hidden = w_up.shape[1]
    tile = min(512, rows)
    block = pl.BlockSpec((tile, width), lambda i: (i, 0))
    wide = pl.BlockSpec((tile, hidden), lambda i: (i, 0))
    return call(
        feed_body,
        (rows // tile,),
        [block, block, whole(w_up.shape), whole((1, hidden)), whole(w_down.shape)],
        [wide, wide, block, whole((1, hidden))] + [block] * with_mlp,
        [
            like((rows, hidden), BF16),
            like((rows, hidden), BF16),
            like((rows, width), BF16),
            like((1, hidden), F32),
        ]
        + [like((rows, width), BF16)] * with_mlp,
        8 * rows * width * hidden,
        12 * rows * width + 4 * width * hidden,
        limit=16,
    )(normed, grad_mlp, w_up, up_bias, w_down)


def splits(rows, bits):
    return bits and rows % (16 * 2 ** len(bits)) == 0


def position(ordinal, here, bits):
    number = sum(bit for k, bit in enumerate(bits) if ordinal >> k & 1)
    found, step = 0, 2 ** len(bits) // 2
    for bit in bits:
        found = found + jnp.where((number ^ here) & bit != 0, step, 0)
        step //= 2
    return found


def put(value, first_row, bits, here, kept, sent):
    if sent is None:
        kept[first_row : first_row + value.shape[0]] = value
        return
    half = kept.shape[0]
    size = 2 * half // 2 ** len(bits)
    step = math.gcd(size, value.shape[0])
    for row in range(first_row, first_row + value.shape[0], step):
        spot = position(row // size, here, bits) * size + row % size
        part = value[row - first_row : row - first_row + step]

        @pl.when(spot < half)
        def _():
            kept[pl.ds(pl.multiple_of(spot, 16), step)] = part

        @pl.when(spot >= half)
        def _():
            sent[pl.ds(pl.multiple_of(spot - half, 16), step)] = part


def outer_body(groups, tile, count, based, place, *refs):
    pairs = sum(len(halves) for _, _, halves in groups)
    base, refs = refs[:based], refs[based:]
    left, right, outs = refs[: -count - pairs], refs[-count - pairs : -pairs], list(refs[-pairs:])
    for start, bits, halves in groups:
        kept = outs.pop(0)
        sent = outs.pop(0) if len(halves) > 1 else None
        rows = sum(halves)
        step = tile if rows % tile == 0 else rows
        for first in range(0, rows, step):
            total = base[0][start + first : start + first + step] if base else None
            for p in range(count):
                if len(left) == count:
                    a = left[p][:, start + first : start + first + step]
                else:
                    size = right[0].shape[0]
                    a = left[0][p * size : (p + 1) * size, start + first : start + first + step]
                term = mxu(a, right[p][...], TN)
                total = term if total is None else total + term
            put(total.astype(kept.dtype), first, bits, place[1], kept, sent)


def outer(place, left, right, groups, base=(), dtype=BF16):
    rows, width = right[0].shape
    count = len(right)
    found, start = [], 0
    for size, bits in groups:
        halves = [size // 2] * 2 if splits(size, bits) else [size]
        found.append((start, bits, halves))
        start += size
    outs = [rows_out for _, _, halves in found for rows_out in halves]
    results = call(
        functools.partial(outer_body, found, 256, count, len(base)),
        (1,),
        [scalars()] + [whole(a.shape) for a in (*base, *left)] + [whole((rows, width))] * count,
        [whole((rows_out, width)) for rows_out in outs],
        [like((rows_out, width), dtype) for rows_out in outs],
        0,
        0,
        limit=16,
    )(place, *base, *left, *right)
    results = list(results)
    return [[results.pop(0) for _ in halves] for _, _, halves in found]


def each_body(bits, count, place, *refs):
    for left, out in zip(refs[:count], refs[count + 1 :]):
        value = mxu(left[...], refs[count][...], TN).astype(BF16)
        depth = value.shape[0]
        if splits(depth, bits):
            put(value, 0, bits, place[1], out.at[: depth // 2], out.at[depth // 2 :])
        else:
            out[...] = value


def outer_each(place, left, right, bits):
    rows, depth = left[0].shape
    width = right.shape[1]
    count = len(left)
    return call(
        functools.partial(each_body, bits, count),
        (1,),
        [scalars()] + [whole((rows, depth))] * count + [whole((rows, width))],
        [whole((depth, width))] * count,
        [like((depth, width), BF16)] * count,
        2 * count * rows * depth * width,
        2 * (count * rows * depth + rows * width + count * depth * width),
    )(place, *left, right)


def unpack_body(bits, sections, place, first, second, *outs):
    half, shares = first.shape[0], 2 ** len(bits)
    size = 2 * half // shares
    for block in range(shares):
        spot = position(block, place[1], bits) * size
        offset = 0
        for out, rows in zip(outs, sections):
            count = rows // shares
            start = spot + offset
            low = pl.ds(pl.multiple_of(jnp.minimum(start, half - count), 16), count)
            high = pl.ds(pl.multiple_of(jnp.maximum(start - half, 0), 16), count)
            part = jnp.where(spot < half, first[low], second[high])
            out[block * count : (block + 1) * count] = part.astype(out.dtype)
            offset += count


def unpack(place, first, second, bits, sections, dtype=F32):
    half, width = first.shape
    return call(
        functools.partial(unpack_body, bits, sections),
        (1,),
        [scalars(), whole(first.shape), whole(second.shape)],
        [whole((rows, width)) for rows in sections],
        [like((rows, width), dtype) for rows in sections],
        2 * half * width,
        12 * half * width,
    )(place, first, second)


def join_body(bits_a, sections_a, bits_b, sections_b, place, *refs):
    joined, rows = refs[4], sections_a[0]
    unpack_body(bits_a, sections_a, place, refs[0], refs[1], joined.at[:rows], *refs[5:])
    unpack_body(bits_b, sections_b, place, refs[2], refs[3], joined.at[rows:])


def join(place, chain_a, chain_b):
    halves = [chain_a.kept, chain_a.came, chain_b.kept, chain_b.came]
    width = halves[0].shape[1]
    outs = [chain_a.sections[0] + chain_b.sections[0], *chain_a.sections[1:]]
    return call(
        functools.partial(
            join_body, chain_a.bits[:-1], chain_a.sections, chain_b.bits[:-1], chain_b.sections
        ),
        (1,),
        [scalars()] + [whole(half.shape) for half in halves],
        [whole((rows, width)) for rows in outs],
        [like((rows, width), F32) for rows in outs],
        0,
        0,
    )(place, *halves)


def project_body(group_count, piece_count, *refs):
    grads = refs[:group_count]
    weights = refs[group_count : 2 * group_count]
    normed = refs[2 * group_count : 2 * group_count + piece_count]
    outs = refs[2 * group_count + piece_count : -1]
    sums = refs[-1]
    size = normed[0].shape[0]
    plain = weighed = 0.0
    for p in range(piece_count):
        total = None
        for grad, weight in zip(grads, weights):
            term = mxu(grad[p * size : (p + 1) * size], weight[...], NN)
            total = term if total is None else total + term
        outs[p][...] = total.astype(BF16)
        plain = plain + column_sum(total)
        weighed = weighed + column_sum(total * normed[p][...].astype(F32))
    sums[0:1] = plain
    sums[1:2] = weighed


def project_back(grads, weights, normed):
    size, width = normed[0].shape
    depth = sum(w.shape[0] for w in weights)
    count = len(normed)
    results = call(
        functools.partial(project_body, len(grads), count),
        (1,),
        [whole(g.shape) for g in grads] + [whole(w.shape) for w in weights] + [whole((size, width))] * count,
        [whole((size, width))] * count + [whole((8, width))],
        [like((size, width), BF16)] * count + [like((8, width), F32)],
        2 * count * size * depth * width,
        2 * count * size * (depth + 2 * width) + 2 * depth * width,
        limit=20,
    )(*grads, *weights, *normed)
    return list(results[:-1]), results[-1][:2]


def second_back_body(item_count, piece_count, lengths, place, half_a, half_b, stream1, cotangent, gain, *refs):
    weights = refs[:piece_count]
    grad_out, attn_out = refs[piece_count : piece_count + 2]
    mixed_out = refs[piece_count + 2 : 2 * piece_count + 2]
    sums = refs[-1]
    tile = stream1.shape[0]
    first = place[0] * (tile * pl.num_programs(0)) + pl.program_id(0) * tile
    valid = valid_column(lengths, item_count, first, tile)
    grad_norm = half_a[...].astype(F32) + half_b[...].astype(F32)
    scaled, rstd = normalize(stream1[...])
    grad = valid * cotangent[...].astype(F32) + norm_back(grad_norm, scaled, gain[...], rstd)
    grad_out[...] = grad
    rounded = grad.astype(BF16)
    attn_out[...] = rounded

    @pl.when(pl.program_id(0) == 0)
    def _():
        sums[...] = jnp.zeros(sums.shape, F32)

    sums[0:1] += column_sum(grad_norm * scaled)
    sums[1:2] += column_sum(grad_norm)
    sums[2:3] += column_sum(rounded.astype(F32))
    for weight, mixed in zip(weights, mixed_out):
        mixed[...] = mxu(rounded, weight[...], NT).astype(BF16)


def second_back(lengths, place, half_a, half_b, stream1, cotangent, gain, weights):
    rows, width = stream1.shape
    tile = min(256, rows)
    count = len(weights)
    depth = weights[0].shape[0]
    block = pl.BlockSpec((tile, width), lambda i: (i, 0))
    narrow = pl.BlockSpec((tile, depth), lambda i: (i, 0))
    results = call(
        functools.partial(second_back_body, lengths.shape[0], count),
        (rows // tile,),
        [scalars(), scalars(), block, block, block, block, whole((1, width))]
        + [whole(weights[0].shape)] * count,
        [block, block] + [narrow] * count + [whole((8, width))],
        [like((rows, width), F32), like((rows, width), BF16)]
        + [like((rows, depth), BF16)] * count
        + [like((8, width), F32)],
        2 * rows * width * width,
        rows * width * 20 + 2 * width * width,
    )(lengths, place, half_a, half_b, stream1, cotangent, gain, *weights)
    return results[0], results[1], results[2:-1], results[-1][:3]


def output_body(item_count, lengths, place, half_a, half_b, shift, stream1, cotangent, out, sums):
    tile = stream1.shape[0]
    first = place[0] * (tile * pl.num_programs(0)) + pl.program_id(0) * tile
    valid = valid_column(lengths, item_count, first, tile)
    mlp = half_a[...].astype(F32) + half_b[...].astype(F32) + shift[...]
    stream2 = stream1[...] + mlp
    out[...] = (valid * stream2).astype(BF16)

    @pl.when(pl.program_id(0) == 0)
    def _():
        sums[...] = jnp.zeros(sums.shape, F32)

    sums[0:1] += column_sum(valid * stream2 * stream2)
    sums[1:2] += column_sum(valid * mlp * mlp)
    sums[2:3] += column_sum((valid * cotangent[...].astype(F32)).astype(BF16).astype(F32))
    sums[3:4] += jnp.broadcast_to(column_sum(valid), (1, stream1.shape[1]))


def output_end(lengths, place, half_a, half_b, shift, stream1, cotangent):
    rows, width = stream1.shape
    tile = min(256, rows)
    block = pl.BlockSpec((tile, width), lambda i: (i, 0))
    out, sums = call(
        functools.partial(output_body, lengths.shape[0]),
        (rows // tile,),
        [scalars(), scalars(), block, block, whole((1, width)), block, block],
        [block, whole((8, width))],
        [like((rows, width), BF16), like((8, width), F32)],
        12 * rows * width,
        rows * width * 12,
    )(lengths, place, half_a, half_b, shift, stream1, cotangent)
    return out, sums[:4]


def input_body(half_a, half_b, stream0, grad_stream1, gain, out):
    grad_norm = half_a[...].astype(F32) + half_b[...].astype(F32)
    scaled, rstd = normalize(stream0[...])
    out[...] = grad_stream1[...] + norm_back(grad_norm, scaled, gain[...].astype(F32), rstd)


def input_end(half_a, half_b, stream0, grad_stream1, gain):
    rows, width = stream0.shape
    tile = min(256, rows)
    block = pl.BlockSpec((tile, width), lambda i: (i, 0))
    return call(
        input_body,
        (rows // tile,),
        [block, block, block, block, whole((1, width))],
        block,
        like((rows, width), F32),
        12 * rows * width,
        rows * width * 16,
    )(half_a, half_b, stream0, grad_stream1, gain)


def swap(array, axis, bit):
    return lax.ppermute(array, axis, [(i, i ^ bit) for i in range(lax.axis_size(axis))])


def after(array, *others):
    return lax.optimization_barrier((array, *others))[0]


def spread(own, top):
    pieces, bit = {0: own}, top // 2
    while bit:
        for p in sorted(pieces):
            pieces[p | bit] = swap(pieces[p], "mp", bit)
        bit //= 2
    return [pieces[p] for p in range(len(pieces))]


def add(left, right):
    return (left.astype(F32) + right.astype(F32)).astype(left.dtype)


def fold(parts, *others):
    bit = 1
    while len(parts) > 1:
        came = [swap(parts[p + 1], "mp", bit) for p in range(0, len(parts), 2)]
        if others:
            came = [after(array, *others) for array in came]
        parts = [add(parts[2 * k], array) for k, array in enumerate(came)]
        bit *= 2
    return parts[0]


def exchange(parts):
    return [parts[0]] + [swap(parts[p], "mp", p) for p in range(1, len(parts))]


def total(array, axis):
    bit = 1
    while bit < lax.axis_size(axis):
        array = array + swap(array, axis, bit)
        bit *= 2
    return array


def own_block(place, weight, bits):
    if not splits(weight.shape[0], bits):
        return weight
    size = weight.shape[0] // 2 ** len(bits)
    return lax.dynamic_slice_in_dim(weight, place[1] * size, size, 0)


def join_blocks(place, kept, rows, bits):
    if kept.shape[0] == rows:
        return kept
    for bit in bits[:0:-1]:
        kept = jnp.concatenate([kept, swap(kept, "dp", bit)], axis=0)
    return unpack(place, kept, swap(kept, "dp", bits[0]), bits, [rows], kept.dtype)[0]


class DpSum:
    def __init__(self, place, parts, bits, *others):
        self.place, self.bits, self.steps = place, bits, 0
        self.sections = [sum(half.shape[0] for half in halves) for halves in parts]
        blocks, width = max(2 ** (len(bits) - 1) // 2, 1), parts[0][0].shape[1]
        halves = [
            jnp.concatenate([half.reshape(blocks, -1, width) for half in group], axis=1).reshape(-1, width)
            for group in zip(*parts)
        ]
        if len(halves) == 1:
            self.kept = lax.psum(halves[0], "dp")
            return
        self.kept, self.sent = halves
        self.came = swap(after(self.sent, *others), "dp", bits[0])

    def step(self, *others):
        if not self.more():
            return
        self.steps += 1
        came, count = after(self.came, *others), len(self.bits)
        if self.steps < count:
            half = came.shape[0] // 2
            self.sent = add(self.kept[half:], came[half:])
            self.kept = add(self.kept[:half], came[:half])
            if self.steps == count - 1:
                self.kept = self.sent = jnp.concatenate([self.kept, self.sent], axis=0)
            self.came = swap(self.sent, "dp", self.bits[self.steps])
        else:
            if self.steps == count:
                self.kept = add(self.kept, came)
            else:
                self.kept = jnp.concatenate([self.kept, came], axis=0)
            self.sent = self.kept
            self.came = swap(self.kept, "dp", self.bits[2 * count - 2 - self.steps])

    def now(self):
        return [self.kept, self.sent] if hasattr(self, "came") else []

    def more(self):
        return hasattr(self, "came") and self.steps < 2 * len(self.bits) - 2

    def done(self, *others):
        if not hasattr(self, "came"):
            return [self.kept.astype(F32)]
        came = after(self.came, *others) if others else self.came
        return unpack(self.place, self.kept, came, self.bits[:-1], self.sections)


def advance(chains, others):
    for chain in chains:
        chain.step(*others)
    return [array for chain in chains for array in chain.now()] or list(others)


def per_device(
    tokens, cotangent, lengths, gsd_ratio, ln1_gain, ln1_bias, w_qkv, qv_bias, w_out, out_bias,
    ln2_gain, ln2_bias, w_up, up_bias, w_down, down_bias,
):
    own_rows, width = tokens.shape
    mp_count, dp_count = lax.axis_size("mp"), lax.axis_size("dp")
    top = mp_count // 2
    low_first = [1 << k for k in range(dp_count.bit_length() - 1)] if dp_count & (dp_count - 1) == 0 else []
    low_second = low_first[1:2] + low_first[:1] + low_first[2:]
    low_last = low_first[1:] + low_first[:1]
    place = jnp.stack([lax.axis_index("mp"), lax.axis_index("dp")]).astype(jnp.int32)
    depth = w_qkv.shape[1]
    heads = depth // HD
    gain2, bias2 = ln2_gain[None], ln2_bias[None]
    up_shift = up_bias[None]

    w_out_block = swap(own_block(place, w_out, low_first), "mp", top)
    grad_mlp_own = mask_rows(lengths, place, cotangent)
    early = own_rows // 8
    grad_mlp_far = swap(grad_mlp_own[:early], "mp", top)
    gain1 = after(ln1_gain, w_out_block)[None]
    stream0, normed1_own = encode(lengths, gsd_ratio, place, tokens, gain1, ln1_bias[None])
    normed1_far = swap(after(normed1_own, grad_mlp_far), "mp", top)
    w_out_far = join_blocks(place, w_out_block, depth, low_first)
    normed1 = spread(normed1_own, top)
    w_flat = w_qkv.reshape(3 * depth, width)
    shift = jnp.concatenate([qv_bias[0], jnp.zeros((depth,), F32), qv_bias[1]])[None]

    def project(piece):
        return (mxu(piece, w_flat, NT) + shift).astype(BF16)

    qkv = [project(piece) for piece in normed1]
    grad_mlp = spread(grad_mlp_own, top)
    w_out_all = spread(w_out, top)
    normed1_far = after(normed1_far, w_out_far, *qkv, *grad_mlp, *w_out_all)
    grad_mlp_late = swap(after(grad_mlp_own[early:], normed1_far), "mp", top)
    normed1 += spread(normed1_far, top)
    w_out_all += spread(w_out_far, top)
    qkv += [project(piece) for piece in normed1[top:]]

    attended, logsum = attend(lengths, place, qkv)
    attended, grad_mlp_late = lax.optimization_barrier((attended, grad_mlp_late))
    grad_mlp_far = jnp.concatenate([grad_mlp_far, grad_mlp_late], axis=0)
    mixed = exchange([attended[p * own_rows : (p + 1) * own_rows] for p in range(mp_count)])
    grad_mlp += spread(grad_mlp_far, top)
    mixed[0] = after(mixed[0], *grad_mlp)
    stream1, normed2_own, attn_squares = branch(
        lengths, place, mixed, w_out_all, stream0, out_bias[None], gain2, bias2
    )

    normed2_far = swap(normed2_own, "mp", top)
    normed2 = spread(normed2_own, top)
    fed = [feed(normed2[p], grad_mlp[p], w_up, up_shift, w_down, True) for p in range(top)]
    [[down_base]] = outer(place, [f[0] for f in fed], grad_mlp[:top], [(w_down.shape[0], [])], dtype=F32)
    [[up_base]] = outer(place, normed2, [f[1] for f in fed], [(width, [])], dtype=F32)
    far_normed = spread(after(normed2_far, down_base, up_base), top)
    norm2_near, mlp_near = fold([f[2] for f in fed]), fold([f[4] for f in fed])
    far_normed[-1] = after(far_normed[-1], norm2_near, mlp_near)
    right = grad_mlp[top:]
    far_fed = [feed(n, g, w_up, up_shift, w_down, False) for n, g in zip(far_normed, right)]
    norm2_part = fold([f[2] for f in far_fed])
    norm2_far = swap(norm2_part, "mp", top)
    acts, upins = [f[0] for f in far_fed], [f[1] for f in far_fed]
    acts[-1] = after(acts[-1], norm2_part)
    [down_halves] = outer(place, acts, right, [(w_down.shape[0], low_first[:-1])], [down_base])
    grad_down = DpSum(place, [down_halves], low_first)
    upins[-1] = after(upins[-1], *down_halves)
    [up_halves] = outer(place, far_normed, upins, [(width, low_last[:-1])], [up_base])
    grad_up = DpSum(place, [up_halves], low_last)
    grad_up_bias = functools.reduce(jnp.add, [f[3] for f in fed + far_fed])
    mlp_parts = [mxu(after(f[0], *up_halves), w_down, NN).astype(BF16) for f in far_fed]
    norm2_far = after(norm2_far, *mlp_parts)
    grad_stream1, grad_attn, grad_mixed, second_sums = second_back(
        lengths, place, norm2_near, norm2_far, stream1, cotangent, gain2, w_out_all
    )

    grads = exchange(list(grad_mixed))
    out_parts = outer_each(place, mixed, grad_attn, low_first[:-1])
    out_near, out_part = fold(out_parts[:top]), fold(out_parts[top:])
    now = advance([grad_down, grad_up], grads)
    grads[-1] = after(grads[-1], out_near, out_part, *now)
    out_far = swap(after(out_part, grads[-1]), "mp", top)
    proj, proj_sums = attend_back(lengths, place, qkv, grads, attended, logsum, 0, heads)
    mlp_far = swap(fold(mlp_parts, proj), "mp", top)
    now = advance([grad_down, grad_up], [proj])
    qkv_rows = 3 * depth // 2
    halves_a, halves_b = outer(
        place, [after(proj, *now)], normed1, [(qkv_rows, low_first[:-1]), (qkv_rows, low_second[:-1])]
    )
    out_far = after(out_far, proj)
    out_sum = add(out_near, out_far)
    groups_a = [halves_a]
    if len(halves_a) > 1 and splits(depth, low_first[:-1]):
        groups_a.append([out_sum[: depth // 2], out_sum[depth // 2 :]])
    grad_a, grad_b = DpSum(place, groups_a, low_first), DpSum(place, [halves_b], low_second)
    main, proj_chains = [grad_down, grad_up], [grad_a, grad_b]
    now = [*now, *grad_a.now(), *grad_b.now()]
    parts, first_sums = project_back([after(proj, *now)], [w_flat], normed1)
    chains = main + proj_chains
    mp_hops = [1 << k for k in range(mp_count.bit_length() - 1)]
    dp_hops = [low_first[0], *low_first[:0:-1]] if low_first else []

    def hop(array, axis, hops, *others):
        return array + after(swap(array, axis, hops.pop(0)), *others) if hops else array

    norm1_part, norm1_near = fold(parts[top:], first_sums), fold(parts[:top], first_sums)
    now = advance(chains, [first_sums])

    norm1_far = swap(norm1_part, "mp", top)
    output, output_sums = output_end(
        lengths, place, after(mlp_near, *now), mlp_far, down_bias[None], stream1, cotangent
    )
    rows = jnp.concatenate([first_sums, second_sums, output_sums, attn_squares], axis=0)
    while len(mp_hops) > 1:
        rows = hop(rows, "mp", mp_hops, output_sums)
    flat = jnp.concatenate([grad_up_bias[0], proj_sums[0, :depth], proj_sums[0, 2 * depth :]])
    flat = jnp.pad(flat, (0, -flat.size % 1024)).reshape(-1, 128)
    flat = jnp.concatenate([rows.reshape(-1, 128), flat], axis=0)
    flat = hop(flat, "dp", dp_hops, norm1_near)
    norm1_far = after(norm1_far, flat)
    now = advance(chains, [flat])

    input_grad = input_end(
        norm1_near, norm1_far, after(stream0, *now), grad_stream1, ln1_gain[None]
    )
    flat = jnp.concatenate(
        [hop(flat[: rows.size // 128], "mp", mp_hops, input_grad), flat[rows.size // 128 :]], axis=0
    )
    now = advance(proj_chains, [input_grad, flat])
    while any(chain.more() for chain in main):
        now = advance(main, now)

    [grad_down], [grad_up] = grad_down.done(*now), grad_up.done(*now)
    while dp_hops or any(chain.more() for chain in proj_chains):
        flat = hop(flat, "dp", dp_hops, grad_down, grad_up)
        now = advance(proj_chains, [grad_down, grad_up, flat])

    if hasattr(grad_a, "came") and hasattr(grad_b, "came"):
        grad_qkv, *others = join(place, grad_a, grad_b)
    else:
        grad_qkv, others = jnp.concatenate([grad_a.done()[0], grad_b.done()[0]], axis=0), []
    grad_qkv = grad_qkv.reshape(3, depth, width)
    grad_out_weight = others[0] if others else lax.psum(out_sum, "dp").astype(F32)
    flat = flat.reshape(-1)
    rows = flat[: rows.size].reshape(rows.shape)
    up_sums = flat[rows.size : rows.size + up_bias.shape[0]]
    proj_sums = flat[rows.size + up_bias.shape[0] :][: 2 * depth].reshape(2, depth)
    squares = jnp.stack([jnp.sum(rows[5]), jnp.sum(rows[9]), jnp.sum(rows[6])])
    stats = jnp.sqrt(squares / (rows[8, 0] * width))
    grad_ln1_gain = (rows[1] - ln1_bias.astype(F32) * rows[0]) / ln1_gain.astype(F32)
    return (
        output, input_grad, grad_ln1_gain, rows[0], grad_qkv, proj_sums, grad_out_weight, rows[4],
        rows[2], rows[3], grad_up, up_sums, grad_down, rows[7], stats,
    )


def solution(mesh):
    rows, one = P(("dp", "mp"), None), P()
    placed = (
        rows, rows, P("dp"), P("dp"), one, one, P(None, "mp", None), P(None, "mp"), P("mp", None), one,
        one, one, P(None, "mp"), P("mp"), P("mp", None), one,
    )
    results = (
        rows, rows, one, one, P(None, "mp", None), P(None, "mp"), P("mp", None), one,
        one, one, P(None, "mp"), P("mp"), P("mp", None), one, one,
    )
    return jax.shard_map(per_device, mesh=mesh, in_specs=placed, out_specs=results, check_vma=False)
```
